32 devices in a mesh: seq: 8 (over y, x, core), trk: 4 (over z).
Axes of the slice: x: 2, y: 2, z: 4, core: 2. Of those that a mesh axis runs over, the one named last changes fastest.
Arguments:
- trunk_input: bfloat16 [3072, 1536], P('seq', 'trk'), may hold values from -6 to 6
- conv_in: bfloat16 [6, 3, 768, 1536], P(None, None, 'trk'), may hold values from -0.09375 to 0.09375
- conv_bias: bfloat16 [6, 768], P(None, 'trk'), may hold values from -3 to 3
- conv_out: bfloat16 [6, 768, 1536], P(None, 'trk'), may hold values from -0.21875 to 0.21875
- projection_bias: bfloat16 [6, 1536], P(None, 'trk'), may hold values from -3 to 3
- head_weight: bfloat16 [1536, 4096], P(None, 'trk'), may hold values from -0.15625 to 0.15625
- head_bias: bfloat16 [4096], P('trk'), may hold values from -4 to 4
- exon_bins: int32 [64, 64], P('seq'), may hold values from -1 to 3071, as said below
Outputs:
- coverage: bfloat16 [3072, 4096], P('seq', 'trk')
- gene_cov: float32 [64, 4096], P('seq', 'trk')
The draws below stay inside these ranges and needn't reach their ends.
Inputs may be any that keep to these rules, and one draw needn't show every extreme that they name: `exon_bins`: row g lists gene g's exon bins in increasing order, then -1 in the unused entries; every gene has at least one exon bin and some gene has exactly 64. The genes of rows 8 * o to 8 * (o + 1) - 1 are owned by index o of seq.
All inputs are finite; a program needn't handle non-finite values.
Results may differ from the reference program's by a relative error of at most 0.024.
Values may be sent and summed in bfloat16 or wider, within the bound.
No kernel may reach another device: no remote copies, remote signals or barrier semaphores. Data moves between devices by JAX's collectives and lax.ppermute only.
A program may use at most 128 MiB of HBM per device.

```python
import jax
import jax.numpy as jnp
from jax import lax

C = 1536
HID = 768
TRACKS = 4096
RESIDUAL_BLOCKS = 6
BASE_DILATION = 2
EXON_MAX = 64
BINS = 3072
GENES = 64
N_TRK = 4


def draw_exon_bins(key, part):
    key_count, key_stride, key_pick, key_other, key_start = jax.random.split(jax.random.fold_in(key, 11), 5)
    counts = jax.random.randint(key_count, (GENES,), 1, EXON_MAX + 1)
    stride = jax.random.randint(key_stride, (GENES,), 1, 9)
    chosen = jax.random.randint(key_pick, (), 0, GENES)
    second = (chosen + 1 + jax.random.randint(key_other, (), 0, GENES - 1)) % GENES
    gene_ids = jnp.arange(GENES)
    counts = jnp.where(gene_ids == chosen, EXON_MAX, jnp.where(gene_ids == second, 1, counts))
    extent = (counts - 1) * stride
    starts = jax.random.randint(key_start, (GENES,), 0, BINS - 8 * EXON_MAX + 1)
    starts = jnp.where(gene_ids == chosen, BINS - 1 - extent, starts)
    entry = jnp.arange(EXON_MAX)
    positions = starts[:, None] + entry[None, :] * stride[:, None]
    return jnp.where(entry[None, :] < counts[:, None], positions, -1).astype(jnp.int32)


def shard_levels(key, shape, shards, least, high):
    def one(dim, blocks):
        heights = jax.random.uniform(jax.random.fold_in(jax.random.fold_in(key, 6), dim), (blocks,), jnp.float32, least / len(shards), high / len(shards))
        return jnp.repeat(jnp.exp(heights), shape[dim] // blocks).reshape((-1,) + (1,) * (len(shape) - dim - 1))

    loudness = one(*shards[0])
    for cut in shards[1:]:
        loudness = loudness * one(*cut)
    return loudness


def bell_draw(key, shape, width, limit, pieces=(), kind=jnp.bfloat16):
    array = jax.random.normal(key, shape, jnp.float32) * width
    if len(pieces) > 0:
        array = shard_levels(key, shape, pieces, -0.22, 0.18) * array
    return jnp.clip(array, min=-limit, max=limit).astype(kind)


def setup_inputs(seed: int = 0) -> dict:
    key_list = jax.random.split(jax.random.key(seed), 9)
    return {
        "trunk_input": bell_draw(key_list[0], (BINS, C), 1.0, 6.0, ((0, 8), (1, 4))),
        "conv_in": bell_draw(key_list[1], (RESIDUAL_BLOCKS, 3, HID, C), (3 * C) ** -0.5, 0.09375, ((2, 4),)),
        "conv_bias": bell_draw(key_list[2], (RESIDUAL_BLOCKS, HID), 0.5, 3.0, ((1, 4),)),
        "conv_out": bell_draw(key_list[3], (RESIDUAL_BLOCKS, HID, C), HID ** -0.5, 0.21875, ((1, 4),)),
        "projection_bias": bell_draw(key_list[4], (RESIDUAL_BLOCKS, C), 0.5, 3.0, ((1, 4),)),
        "head_weight": bell_draw(key_list[5], (C, TRACKS), C ** -0.5, 0.15625, ((1, 4),)),
        "head_bias": bell_draw(key_list[6], (TRACKS,), 1.0, 4.0, ((0, 4),)),
        "exon_bins": draw_exon_bins(jax.random.fold_in(key_list[8], 71), 0),
    }


def contract_last(rows, kernel):
    return lax.dot_general(rows, kernel, (((1,), (1,)), ((), ())), preferred_element_type=jnp.float32)


def reference(trunk_input, conv_in, conv_bias, conv_out, projection_bias, head_weight, head_bias, exon_bins):
    trunk = trunk_input
    group_width = HID // N_TRK
    for block_layer_index in range(RESIDUAL_BLOCKS):
        dilation_step = BASE_DILATION * 2 ** block_layer_index
        padded = jnp.pad(trunk, ((dilation_step, dilation_step), (0, 0)))
        inner = jnp.zeros((BINS, HID), jnp.float32)
        for tap_index in range(3):
            window = padded[tap_index * dilation_step: tap_index * dilation_step + BINS]
            inner = inner + contract_last(window, conv_in[block_layer_index, tap_index])
        activation = jax.nn.gelu(inner + conv_bias[block_layer_index].astype(jnp.float32), approximate=True).astype(jnp.bfloat16)
        branch = jnp.zeros((BINS, C), jnp.float32)
        for group_index in range(N_TRK):
            lower = group_index * group_width
            partial_value = jnp.dot(activation[:, lower:lower + group_width], conv_out[block_layer_index, lower:lower + group_width], preferred_element_type=jnp.float32)
            rounded = lax.optimization_barrier(partial_value.astype(jnp.bfloat16))
            branch = branch + rounded.astype(jnp.float32)
        trunk = (trunk.astype(jnp.float32) + branch + projection_bias[block_layer_index].astype(jnp.float32)).astype(jnp.bfloat16)
    logits = jnp.dot(trunk, head_weight, preferred_element_type=jnp.float32)
    coverage = jax.nn.softplus(logits + head_bias.astype(jnp.float32)).astype(jnp.bfloat16)
    present = exon_bins >= 0
    safe_index = jnp.where(present, exon_bins, 0).astype(jnp.int32)
    picked = coverage[safe_index].astype(jnp.float32)
    gene_sum = jnp.sum(jnp.where(present[:, :, None], picked, jnp.float32(0.0)), axis=1)
    counts = jnp.sum(present.astype(jnp.float32), axis=1)
    gene_cov = gene_sum / counts[:, None]
    return coverage, gene_cov
```

```python
import jax
import jax.numpy as jnp
from jax import lax
from jax.sharding import PartitionSpec as P

RESIDUAL_BLOCKS = 6
BASE_DILATION = 2
BLOCKS_PER_LOAD = 2


def shifted(cells, axis, step):
    count = lax.axis_size(axis)
    return lax.ppermute(cells, axis, [(i, (i + step) % count) for i in range(count)])


def halo(cells, width):
    count = lax.axis_size("seq")
    head = cells[:width]
    tail = cells[cells.shape[0] - width :]
    above = lax.ppermute(tail, "seq", [(i, i + 1) for i in range(count - 1)])
    below = lax.ppermute(head, "seq", [(i + 1, i) for i in range(count - 1)])
    return above, below


def contract_last(rows, kernel):
    return lax.dot_general(
        rows, kernel, (((1,), (1,)), ((), ())), preferred_element_type=jnp.float32
    )


def group_size(rows, count):
    size = 1
    for g in range(1, count + 1):
        if count % g == 0 and rows % (16 * g) == 0:
            size = g
    return size


def spread_projection(conv_out):
    blocks, hidden, channels = conv_out.shape
    count = lax.axis_size("seq")
    rows = BLOCKS_PER_LOAD * hidden
    size = group_size(rows, count)
    share = rows // size
    groups = [[g * size + i for i in range(size)] for g in range(count // size)]
    mine = lax.rem(lax.axis_index("seq"), size)
    loads = []
    for first in range(0, blocks, BLOCKS_PER_LOAD):
        flat = conv_out[first : first + BLOCKS_PER_LOAD].reshape(rows, channels)
        part = lax.dynamic_slice_in_dim(flat, mine * share, share, 0)
        column = lax.all_gather(part, "trk", axis=0, tiled=False)
        whole = lax.all_gather(column, "seq", axis=0, tiled=False, axis_index_groups=groups)
        loads.append(whole)
    return loads


def block_projection(loads, block, hidden):
    whole = loads[block // BLOCKS_PER_LOAD]
    size, quarters, share, channels = whole.shape
    per = hidden // share
    first = (block % BLOCKS_PER_LOAD) * per
    part = whole[first : first + per]
    return jnp.transpose(part, (1, 0, 2, 3)).reshape(quarters, hidden, channels)


def exon_onehot(gene_block, first_bin, width_now):
    exon_matches = (
        gene_block[:, :, None] - first_bin == jnp.arange(width_now, dtype=jnp.int32)[None, None, :]
    )
    return jnp.sum(exon_matches.astype(jnp.float32), axis=1).astype(jnp.bfloat16)


def shards(
    trunk_input, conv_in, conv_bias, conv_out, projection_bias, head_weight, head_bias, exon_bins
):
    quarters = lax.axis_size("trk")
    place = lax.axis_index("trk")
    bin_rows = trunk_input.shape[0]
    hidden = conv_out.shape[1]
    gene_lists = lax.all_gather(exon_bins, "seq", axis=0, tiled=True)
    trunk = lax.all_gather(trunk_input, "trk", axis=1, tiled=True)
    biases = lax.all_gather(projection_bias, "trk", axis=1, tiled=True)
    loads = spread_projection(conv_out)
    for block in range(RESIDUAL_BLOCKS):
        step = BASE_DILATION * 2**block
        above, below = halo(trunk, step)
        padded = jnp.concatenate([above, trunk, below], axis=0)
        inner = conv_bias[block].astype(jnp.float32)
        for tap in range(3):
            inner = inner + contract_last(
                padded[tap * step : tap * step + bin_rows], conv_in[block, tap]
            )
        activation = jax.nn.gelu(inner, approximate=True).astype(jnp.bfloat16)
        weight = block_projection(loads, block, hidden)
        total = trunk.astype(jnp.float32) + biases[block].astype(jnp.float32)
        others = [activation] + [shifted(activation, "trk", k) for k in range(1, quarters)]
        for k in range(quarters):
            owner = lax.rem(place - k + quarters, quarters)
            total = total + jnp.dot(
                others[k],
                lax.dynamic_index_in_dim(weight, owner, 0, keepdims=False),
                preferred_element_type=jnp.float32,
            )
        trunk = total.astype(jnp.bfloat16)
    logits = jnp.dot(trunk, head_weight, preferred_element_type=jnp.float32)
    coverage = jax.nn.softplus(logits + head_bias.astype(jnp.float32)).astype(jnp.bfloat16)
    first_bin = lax.axis_index("seq") * bin_rows
    onehot = exon_onehot(gene_lists, first_bin, bin_rows)
    partial = jnp.dot(onehot, coverage, preferred_element_type=jnp.float32).astype(jnp.bfloat16)
    count = lax.axis_size("seq")
    parts = lax.all_to_all(
        partial.reshape(count, exon_bins.shape[0], partial.shape[1]), "seq", 0, 0, tiled=False
    )
    gene_sum = jnp.sum(parts.astype(jnp.float32), axis=0)
    counts = jnp.sum((exon_bins >= 0).astype(jnp.float32), axis=1)
    gene_cov = gene_sum / counts[:, None]
    return (coverage, gene_cov)


def solution(mesh):
    in_specs = (
        P("seq", "trk"),
        P(None, None, "trk", None),
        P(None, "trk"),
        P(None, "trk", None),
        P(None, "trk"),
        P(None, "trk"),
        P("trk"),
        P("seq", None),
    )
    out_specs = (P("seq", "trk"), P("seq", "trk"))
    return jax.shard_map(shards, mesh=mesh, in_specs=in_specs, out_specs=out_specs, check_vma=False)
```

```python
import jax
import jax.numpy as jnp
from jax import lax
from jax.sharding import PartitionSpec as P

RESIDUAL_BLOCKS = 6
BASE_DILATION = 2
BLOCKS_PER_LOAD = 2
HALO_GROUPS = ((0, 1, 2, 3), (4,), (5,))
DIGIT = 128


def dilation(block):
    return BASE_DILATION * 2**block


def after(cells, *earlier):
    return lax.optimization_barrier((cells,) + earlier)[0]


def from_others(cells):
    count = lax.axis_size("trk")
    return [cells] + [
        lax.ppermute(cells, "trk", [(i, (i + k) % count) for i in range(count)])
        for k in range(1, count)
    ]


def halo(cells, width):
    count = lax.axis_size("seq")
    head = cells[:width]
    tail = cells[cells.shape[0] - width :]
    above = lax.ppermute(tail, "seq", [(i, i + 1) for i in range(count - 1)])
    below = lax.ppermute(head, "seq", [(i + 1, i) for i in range(count - 1)])
    return above, below


def contract_last(rows, kernel):
    return lax.dot_general(
        rows, kernel, (((1,), (1,)), ((), ())), preferred_element_type=jnp.float32
    )


def group_size(rows, count):
    size = 1
    for g in range(1, count + 1):
        if count % g == 0 and rows % (16 * g) == 0:
            size = g
    return size


def exon_digits(exon_bins, channels):
    digits = jnp.concatenate([exon_bins >> 7, exon_bins & (DIGIT - 1)], axis=1)
    genes, width = digits.shape
    return jnp.pad(
        digits.astype(jnp.bfloat16), ((0, -genes % 16), (0, channels - width))
    )


def exon_lists(rows, genes, entries):
    digits = rows[:, :genes, : 2 * entries].astype(jnp.int32)
    lists = digits[:, :, :entries] * DIGIT + digits[:, :, entries:]
    return lists.reshape(-1, entries)


def exon_onehot(gene_block, first_bin, width_now):
    exon_matches = (
        gene_block[:, :, None] - first_bin == jnp.arange(width_now, dtype=jnp.int32)[None, None, :]
    )
    return jnp.sum(exon_matches.astype(jnp.float32), axis=1).astype(jnp.bfloat16)


def shards(
    trunk_input, conv_in, conv_bias, conv_out, projection_bias, head_weight, head_bias, exon_bins
):
    quarters = lax.axis_size("trk")
    place = lax.axis_index("trk")
    count = lax.axis_size("seq")
    lane = lax.axis_index("seq")
    bin_rows, channels_here = trunk_input.shape
    blocks, hidden, channels = conv_out.shape
    genes_here, entries = exon_bins.shape

    load_rows = BLOCKS_PER_LOAD * hidden
    size = group_size(load_rows, count)
    share = load_rows // size
    per_block = hidden // share
    groups = [[g * size + i for i in range(size)] for g in range(count // size)]
    mine = lax.rem(lane, size)
    packed = size == count and 2 * entries <= channels

    def column(load):
        first = load * BLOCKS_PER_LOAD
        flat = conv_out[first : first + BLOCKS_PER_LOAD].reshape(load_rows, channels)
        return lax.dynamic_slice_in_dim(flat, mine * share, share, 0)

    def gather(parts):
        return lax.all_gather(
            jnp.concatenate(parts, axis=0), "seq", axis=0, tiled=False, axis_index_groups=groups
        )

    start_width = sum(dilation(b) for b in HALO_GROUPS[0])
    above, below = halo(trunk_input, start_width)
    loads = []
    first_column = from_others(column(0))
    loads.append(gather(first_column))

    own = jnp.concatenate(
        [above, trunk_input, below, jnp.pad(projection_bias, ((0, -blocks % 4), (0, 0)))], axis=0
    )
    own = after(own, *first_column)
    quarter_cells = from_others(own)
    whole = jnp.zeros((own.shape[0], channels), own.dtype)
    for k in range(quarters):
        owner = lax.rem(place - k + quarters, quarters)
        whole = lax.dynamic_update_slice_in_dim(
            whole, quarter_cells[k], owner * channels_here, 1
        )
    wide = bin_rows + 2 * start_width
    trunk = whole[:wide]
    biases = whole[wide : wide + blocks]
    second_column = from_others(after(column(1), *quarter_cells))
    loads.append(gather(second_column))

    for group in HALO_GROUPS:
        reach = sum(dilation(b) for b in group)
        if group is not HALO_GROUPS[0]:
            above, below = halo(trunk, reach)
            trunk = jnp.concatenate([above, trunk, below], axis=0)
        for block in group:
            step = dilation(block)
            reach -= step
            rows = bin_rows + 2 * reach
            inner = conv_bias[block].astype(jnp.float32)
            for tap in range(3):
                inner = inner + contract_last(
                    trunk[tap * step : tap * step + rows], conv_in[block, tap]
                )
            activation = jax.nn.gelu(inner, approximate=True).astype(jnp.bfloat16)
            others = from_others(activation)
            if block == 0:
                last = column(2)
                third_column = from_others(after(last, *others))
                tail = [exon_digits(exon_bins, channels)] if packed else []
                loads.append(gather(third_column + tail))
            load = loads[block // BLOCKS_PER_LOAD]
            first = (block % BLOCKS_PER_LOAD) * per_block
            total = trunk[step : step + rows].astype(jnp.float32) + biases[block].astype(
                jnp.float32
            )
            for k in range(quarters):
                weight = load[first : first + per_block, k * share : (k + 1) * share]
                total = total + jnp.dot(
                    others[k],
                    weight.reshape(hidden, channels),
                    preferred_element_type=jnp.float32,
                )
            if reach > 0:
                bins = lane * bin_rows - reach + jnp.arange(rows, dtype=jnp.int32)
                inside = (bins >= 0) & (bins < count * bin_rows)
                total = jnp.where(inside[:, None], total, 0.0)
            trunk = total.astype(jnp.bfloat16)

    logits = jnp.dot(trunk, head_weight, preferred_element_type=jnp.float32)
    coverage = jax.nn.softplus(logits + head_bias.astype(jnp.float32)).astype(jnp.bfloat16)
    if packed:
        gene_lists = exon_lists(loads[-1][:, quarters * share :], genes_here, entries)
    else:
        gene_lists = lax.all_gather(exon_bins, "seq", axis=0, tiled=True)
    onehot = exon_onehot(gene_lists, lane * bin_rows, bin_rows)
    partial = jnp.dot(onehot, coverage, preferred_element_type=jnp.float32).astype(jnp.bfloat16)
    parts = lax.all_to_all(
        partial.reshape(count, genes_here, partial.shape[1]), "seq", 0, 0, tiled=False
    )
    gene_sum = jnp.sum(parts.astype(jnp.float32), axis=0)
    counts = jnp.sum((exon_bins >= 0).astype(jnp.float32), axis=1)
    gene_cov = gene_sum / counts[:, None]
    return (coverage, gene_cov)


def solution(mesh):
    in_specs = (
        P("seq", "trk"),
        P(None, None, "trk", None),
        P(None, "trk"),
        P(None, "trk", None),
        P(None, "trk"),
        P(None, "trk"),
        P("trk"),
        P("seq", None),
    )
    out_specs = (P("seq", "trk"), P("seq", "trk"))
    return jax.shard_map(shards, mesh=mesh, in_specs=in_specs, out_specs=out_specs, check_vma=False)
```

```python
import functools
import math

import jax
import jax.numpy as jnp
from jax import lax
from jax.experimental import pallas as pl
from jax.experimental.pallas import tpu as pltpu
from jax.sharding import PartitionSpec as P

RESIDUAL_BLOCKS = 6
BASE_DILATION = 2
BLOCKS_PER_LOAD = 2
FRAMED_BLOCKS = 4
DIGIT = 128
VMEM_BYTES = 24 * 2**20


def dilation(block):
    return BASE_DILATION * 2**block


def after(cells, *earlier):
    return lax.optimization_barrier((cells,) + earlier)[0]


def after_all(cells, *earlier):
    return list(lax.optimization_barrier(tuple(cells) + earlier)[: len(cells)])


def from_others(cells):
    count = lax.axis_size("trk")
    return [cells] + [
        lax.ppermute(cells, "trk", [(i, (i + k) % count) for i in range(count)])
        for k in range(1, count)
    ]


def halo(cells, width):
    count = lax.axis_size("seq")
    head = cells[:width]
    tail = cells[cells.shape[0] - width :]
    above = lax.ppermute(tail, "seq", [(i, i + 1) for i in range(count - 1)])
    below = lax.ppermute(head, "seq", [(i + 1, i) for i in range(count - 1)])
    return above, below


def group_size(rows, count):
    size = 1
    for g in range(1, count + 1):
        if count % g == 0 and rows % (16 * g) == 0:
            size = g
    return size


def tile_of(channels):
    for width in (512, 256, 384, 128):
        if channels % width == 0:
            return width
    return channels


def dot(a, b):
    return jnp.dot(a, b, preferred_element_type=jnp.float32)


def dot_last(a, b):
    return lax.dot_general(a, b, (((1,), (1,)), ((), ())), preferred_element_type=jnp.float32)


def gelu(x):
    cubic = x + 0.044715 * (x * x * x)
    return 0.5 * x * (1.0 + jnp.tanh(math.sqrt(2.0 / math.pi) * cubic))


def gelu_of_taps(sums, bias, step, rows):
    total = sums.shape[1]
    inner = sums[1] + pltpu.roll(sums[0], step, 0) + pltpu.roll(sums[2], total - step, 0)
    margin = (total - rows) // 2
    inner = inner[margin : margin + rows] + bias.astype(jnp.float32)
    return gelu(inner).astype(jnp.bfloat16)


def first_kernel(step, own_rows, order_ref, c0, c1, c2, c3, w_ref, bias_ref, act_ref, trunk_ref, sums):
    k = pl.program_id(0)
    rows = trunk_ref.shape[0]
    for j, cell in enumerate((c0, c1, c2, c3)):

        @pl.when(k == j)
        def _():
            trunk_ref[...] = cell[:rows]

    tile = trunk_ref[...]
    for t in range(3):
        part = dot_last(tile, w_ref[0, t])
        sums[t] = jnp.where(k == 0, part, sums[t] + part)

    @pl.when(k == pl.num_programs(0) - 1)
    def _():
        act_ref[...] = gelu_of_taps(sums, bias_ref[...], step, act_ref.shape[0])


def first_conv(cells, rows, order, conv_in, bias, step):
    quarters = len(cells)
    _, _, hidden, channels = conv_in.shape
    width = cells[0].shape[1]
    full = pl.BlockSpec(cells[0].shape, lambda k, order: (0, 0))
    return pl.pallas_call(
        functools.partial(first_kernel, step, rows),
        grid_spec=pltpu.PrefetchScalarGridSpec(
            num_scalar_prefetch=1,
            grid=(quarters,),
            in_specs=[full] * quarters
            + [
                pl.BlockSpec((1, 3, hidden, width), lambda k, order: (0, 0, 0, order[k])),
                pl.BlockSpec((1, hidden), lambda k, order: (0, 0)),
            ],
            out_specs=[
                pl.BlockSpec((rows, hidden), lambda k, order: (0, 0)),
                pl.BlockSpec((rows, width), lambda k, order: (0, order[k])),
            ],
            scratch_shapes=[pltpu.VMEM((3, rows, hidden), jnp.float32)],
        ),
        out_shape=[
            jax.ShapeDtypeStruct((rows, hidden), jnp.bfloat16),
            jax.ShapeDtypeStruct((rows, channels), jnp.bfloat16),
        ],
        compiler_params=pltpu.CompilerParams(vmem_limit_bytes=VMEM_BYTES),
        cost_estimate=pl.CostEstimate(
            flops=6 * rows * hidden * channels,
            bytes_accessed=2 * (3 * hidden * channels + 2 * rows * channels),
            transcendentals=rows * hidden,
        ),
    )(order, *cells, conv_in, bias)


def project(acts, weights, trunk, bias):
    whole = jnp.concatenate([w[...].reshape(-1, w.shape[-1]) for w in weights], axis=0)
    return trunk.astype(jnp.float32) + bias.astype(jnp.float32) + dot(acts[...], whole)


def keep_acts(acts_ref, acts):
    acts_ref[...] = jnp.concatenate([a[...] for a in acts], axis=1)


def fused_kernel(
    step, edge_ref, a0, a1, a2, a3, w0, w1, w2, w3, trunk_ref, pbias_ref, w_ref, bias_ref,
    act_ref, out_ref, acts_ref, sums
):
    c = pl.program_id(0)

    @pl.when(c == 0)
    def _():
        keep_acts(acts_ref, (a0, a1, a2, a3))

    total = project(acts_ref, (w0, w1, w2, w3), trunk_ref[...], pbias_ref[...])
    row = lax.broadcasted_iota(jnp.int32, total.shape, 0)
    inside = (row >= edge_ref[0]) & (row < edge_ref[1])
    tile = jnp.where(inside, total, 0.0).astype(jnp.bfloat16)
    out_ref[...] = tile
    for t in range(3):
        part = dot_last(tile, w_ref[0, t])
        sums[t] = jnp.where(c == 0, part, sums[t] + part)

    @pl.when(c == pl.num_programs(0) - 1)
    def _():
        act_ref[...] = gelu_of_taps(sums, bias_ref[...], step, act_ref.shape[0])


def projection_specs(load, part, acts, per_block, share, width):
    specs = [pl.BlockSpec(acts[0].shape, lambda c, *_: (0, 0))] * len(acts)
    for j in range(len(acts)):
        specs.append(
            pl.BlockSpec((per_block, share, width), lambda c, *_, j=j: (part, j, c))
        )
    return specs


def fused(acts, load, part, per_block, share, trunk, pbias, conv_in, block, bias, edge, rows_out):
    rows, channels = trunk.shape
    hidden = conv_in.shape[2]
    width = tile_of(channels)
    return pl.pallas_call(
        functools.partial(fused_kernel, dilation(block)),
        grid_spec=pltpu.PrefetchScalarGridSpec(
            num_scalar_prefetch=1,
            grid=(channels // width,),
            in_specs=projection_specs(load, part, acts, per_block, share, width)
            + [
                pl.BlockSpec((rows, width), lambda c, *_: (0, c)),
                pl.BlockSpec((1, width), lambda c, *_: (0, c)),
                pl.BlockSpec((1, 3, hidden, width), lambda c, *_: (block, 0, 0, c)),
                pl.BlockSpec((1, hidden), lambda c, *_: (0, 0)),
            ],
            out_specs=[
                pl.BlockSpec((rows_out, hidden), lambda c, *_: (0, 0)),
                pl.BlockSpec((rows, width), lambda c, *_: (0, c)),
            ],
            scratch_shapes=[
                pltpu.VMEM((rows, len(acts) * hidden), jnp.bfloat16),
                pltpu.VMEM((3, rows, hidden), jnp.float32),
            ],
        ),
        out_shape=[
            jax.ShapeDtypeStruct((rows_out, hidden), jnp.bfloat16),
            jax.ShapeDtypeStruct((rows, channels), jnp.bfloat16),
        ],
        compiler_params=pltpu.CompilerParams(vmem_limit_bytes=VMEM_BYTES),
        cost_estimate=pl.CostEstimate(
            flops=14 * rows * hidden * channels,
            bytes_accessed=2 * (7 * hidden * channels + 2 * rows * channels),
            transcendentals=rows * hidden,
        ),
    )(edge, *acts, *[load] * len(acts), trunk, pbias, conv_in, bias)


def projection_kernel(margin, a0, a1, a2, a3, w0, w1, w2, w3, trunk_ref, pbias_ref, out_ref, acts_ref):
    @pl.when(pl.program_id(0) == 0)
    def _():
        keep_acts(acts_ref, (a0, a1, a2, a3))

    rows = out_ref.shape[0]
    total = project(
        acts_ref, (w0, w1, w2, w3), trunk_ref[margin : margin + rows], pbias_ref[...]
    )
    out_ref[...] = total.astype(jnp.bfloat16)


def projection(acts, load, part, per_block, share, trunk, pbias):
    frame, channels = trunk.shape
    rows, hidden = acts[0].shape
    width = tile_of(channels)
    return pl.pallas_call(
        functools.partial(projection_kernel, (frame - rows) // 2),
        grid=(channels // width,),
        in_specs=projection_specs(load, part, acts, per_block, share, width)
        + [
            pl.BlockSpec((frame, width), lambda c: (0, c)),
            pl.BlockSpec((1, width), lambda c: (0, c)),
        ],
        out_specs=pl.BlockSpec((rows, width), lambda c: (0, c)),
        scratch_shapes=[pltpu.VMEM((rows, len(acts) * hidden), jnp.bfloat16)],
        out_shape=jax.ShapeDtypeStruct((rows, channels), jnp.bfloat16),
        compiler_params=pltpu.CompilerParams(vmem_limit_bytes=VMEM_BYTES),
        cost_estimate=pl.CostEstimate(
            flops=8 * rows * hidden * channels,
            bytes_accessed=2 * (4 * hidden * channels + 2 * rows * channels),
            transcendentals=0,
        ),
    )(*acts, *[load] * len(acts), trunk, pbias)


def conv_kernel(step, above_ref, trunk_ref, below_ref, w_ref, bias_ref, act_ref, sums):
    c = pl.program_id(0)
    tile = jnp.concatenate([above_ref[...], trunk_ref[...], below_ref[...]], axis=0)
    for t in range(3):
        part = dot_last(tile, w_ref[0, t])
        sums[t] = jnp.where(c == 0, part, sums[t] + part)

    @pl.when(c == pl.num_programs(0) - 1)
    def _():
        act_ref[...] = gelu_of_taps(sums, bias_ref[...], step, act_ref.shape[0])


def conv(above, trunk, below, conv_in, block, bias):
    rows, channels = trunk.shape
    hidden = conv_in.shape[2]
    step = dilation(block)
    width = tile_of(channels)
    return pl.pallas_call(
        functools.partial(conv_kernel, step),
        grid=(channels // width,),
        in_specs=[
            pl.BlockSpec((step, width), lambda c: (0, c)),
            pl.BlockSpec((rows, width), lambda c: (0, c)),
            pl.BlockSpec((step, width), lambda c: (0, c)),
            pl.BlockSpec((1, 3, hidden, width), lambda c: (block, 0, 0, c)),
            pl.BlockSpec((1, hidden), lambda c: (0, 0)),
        ],
        out_specs=pl.BlockSpec((rows, hidden), lambda c: (0, 0)),
        scratch_shapes=[pltpu.VMEM((3, rows + 2 * step, hidden), jnp.float32)],
        out_shape=jax.ShapeDtypeStruct((rows, hidden), jnp.bfloat16),
        compiler_params=pltpu.CompilerParams(vmem_limit_bytes=VMEM_BYTES),
        cost_estimate=pl.CostEstimate(
            flops=6 * rows * hidden * channels,
            bytes_accessed=2 * (3 * hidden * channels + rows * channels),
            transcendentals=rows * hidden,
        ),
    )(above, trunk, below, conv_in, bias)


def head_kernel(
    a0, a1, a2, a3, w0, w1, w2, w3, trunk_ref, pbias_ref, head_ref, hbias_ref, onehot_ref,
    cover_ref, gene_ref, acts_ref, logits
):
    c = pl.program_id(0)

    @pl.when(c == 0)
    def _():
        keep_acts(acts_ref, (a0, a1, a2, a3))

    total = project(acts_ref, (w0, w1, w2, w3), trunk_ref[...], pbias_ref[...])
    part = dot(total.astype(jnp.bfloat16), head_ref[...])
    logits[...] = jnp.where(c == 0, part, logits[...] + part)

    @pl.when(c == pl.num_programs(0) - 1)
    def _():
        x = logits[...] + hbias_ref[...].astype(jnp.float32)
        cover = (jnp.maximum(x, 0.0) + jnp.log1p(jnp.exp(-jnp.abs(x)))).astype(jnp.bfloat16)
        cover_ref[...] = cover
        gene_ref[...] = dot(onehot_ref[...], cover).astype(jnp.bfloat16)


def head(acts, load, part, per_block, share, trunk, pbias, head_weight, head_bias, onehot):
    rows, channels = trunk.shape
    hidden = acts[0].shape[1]
    tracks = head_weight.shape[1]
    genes = onehot.shape[0]
    width = tile_of(channels)
    return pl.pallas_call(
        head_kernel,
        grid=(channels // width,),
        in_specs=projection_specs(load, part, acts, per_block, share, width)
        + [
            pl.BlockSpec((rows, width), lambda c: (0, c)),
            pl.BlockSpec((1, width), lambda c: (0, c)),
            pl.BlockSpec((width, tracks), lambda c: (c, 0)),
            pl.BlockSpec((1, tracks), lambda c: (0, 0)),
            pl.BlockSpec((genes, rows), lambda c: (0, 0)),
        ],
        out_specs=[
            pl.BlockSpec((rows, tracks), lambda c: (0, 0)),
            pl.BlockSpec((genes, tracks), lambda c: (0, 0)),
        ],
        scratch_shapes=[
            pltpu.VMEM((rows, len(acts) * hidden), jnp.bfloat16),
            pltpu.VMEM((rows, tracks), jnp.float32),
        ],
        out_shape=[
            jax.ShapeDtypeStruct((rows, tracks), jnp.bfloat16),
            jax.ShapeDtypeStruct((genes, tracks), jnp.bfloat16),
        ],
        compiler_params=pltpu.CompilerParams(vmem_limit_bytes=VMEM_BYTES),
        cost_estimate=pl.CostEstimate(
            flops=8 * rows * hidden * channels + 2 * rows * channels * tracks,
            bytes_accessed=2 * (4 * hidden * channels + rows * channels + channels * tracks),
            transcendentals=2 * rows * tracks,
        ),
    )(*acts, *[load] * len(acts), trunk, pbias, head_weight, head_bias, onehot)


def exon_digits(exon_bins, channels):
    digits = jnp.concatenate([exon_bins >> 7, exon_bins & (DIGIT - 1)], axis=1)
    genes, width = digits.shape
    return jnp.pad(digits.astype(jnp.bfloat16), ((0, -genes % 16), (0, channels - width)))


def exon_lists(rows, genes, entries):
    digits = rows[:, :genes, : 2 * entries].astype(jnp.int32)
    lists = digits[:, :, :entries] * DIGIT + digits[:, :, entries:]
    return lists.reshape(-1, entries)


def exon_onehot(gene_block, first_bin, width_now):
    exon_matches = (
        gene_block[:, :, None] - first_bin == jnp.arange(width_now, dtype=jnp.int32)[None, None, :]
    )
    return jnp.sum(exon_matches.astype(jnp.float32), axis=1).astype(jnp.bfloat16)


def shards(
    trunk_input, conv_in, conv_bias, conv_out, projection_bias, head_weight, head_bias, exon_bins
):
    quarters = lax.axis_size("trk")
    place = lax.axis_index("trk")
    count = lax.axis_size("seq")
    lane = lax.axis_index("seq")
    bin_rows, channels_here = trunk_input.shape
    blocks, hidden, channels = conv_out.shape
    genes_here, entries = exon_bins.shape

    load_rows = BLOCKS_PER_LOAD * hidden
    size = group_size(load_rows, count)
    share = load_rows // size
    per_block = hidden // share
    groups = [[g * size + i for i in range(size)] for g in range(count // size)]
    mine = lax.rem(lane, size)
    packed = size == count and 2 * entries <= channels

    def column(load):
        first = load * BLOCKS_PER_LOAD
        flat = conv_out[first : first + BLOCKS_PER_LOAD].reshape(load_rows, channels)
        return lax.dynamic_slice_in_dim(flat, mine * share, share, 0)

    def gather(parts):
        return lax.all_gather(
            jnp.concatenate(parts, axis=0), "seq", axis=0, tiled=False, axis_index_groups=groups
        )

    margin = dilation(FRAMED_BLOCKS)
    frame = bin_rows + 2 * margin
    order = lax.rem(place - jnp.arange(quarters, dtype=jnp.int32) + quarters, quarters)
    edge = jnp.stack(
        [
            jnp.where(lane == 0, margin, 0),
            jnp.where(lane == count - 1, margin + bin_rows, frame),
        ]
    ).astype(jnp.int32)

    above, below = halo(trunk_input, margin)
    first_column = from_others(column(0))
    loads = [gather(first_column)]
    own = jnp.concatenate(
        [above, trunk_input, below, jnp.pad(projection_bias, ((0, -blocks % 16), (0, 0)))], axis=0
    )
    own = after(own, *first_column)
    cells = from_others(own)
    second = from_others(after(column(1), *cells))

    act, trunk = first_conv(cells, frame, order, conv_in, conv_bias[:1], dilation(0))
    biases = jnp.zeros((blocks, channels), jnp.bfloat16)
    for k in range(quarters):
        biases = lax.dynamic_update_slice_in_dim(
            biases, cells[k][frame : frame + blocks], order[k] * channels_here, 1
        )

    onehot = None
    for block in range(RESIDUAL_BLOCKS):
        others = from_others(act)
        if block == 0:
            loads.append(gather(after_all(second, *others)))
            third = from_others(after(column(2), *others))
        if block == 1:
            tail = [exon_digits(exon_bins, channels)] if packed else []
            loads.append(gather(after_all(third, *others) + tail))
        if block == 4:
            if packed:
                gene_lists = exon_lists(loads[2][:, quarters * share :], genes_here, entries)
            else:
                gene_lists = lax.all_gather(exon_bins, "seq", axis=0, tiled=True)
            onehot = exon_onehot(gene_lists, lane * bin_rows, bin_rows)
        load = loads[block // BLOCKS_PER_LOAD]
        part = block % BLOCKS_PER_LOAD
        where = (load, part, per_block, share, trunk, biases[block : block + 1])
        later = block + 1
        if later < FRAMED_BLOCKS:
            rows_out = frame if later < FRAMED_BLOCKS - 1 else bin_rows
            act, trunk = fused(
                others, *where, conv_in, later, conv_bias[later : later + 1], edge, rows_out
            )
        elif later < RESIDUAL_BLOCKS:
            trunk = projection(others, *where)
            above, below = halo(trunk, dilation(later))
            act = conv(above, trunk, below, conv_in, later, conv_bias[later : later + 1])
        else:
            coverage, partial = head(others, *where, head_weight, head_bias[None, :], onehot)

    parts = lax.all_to_all(
        partial.reshape(count, genes_here, partial.shape[1]), "seq", 0, 0, tiled=False
    )
    gene_sum = jnp.sum(parts.astype(jnp.float32), axis=0)
    counts = jnp.sum((exon_bins >= 0).astype(jnp.float32), axis=1)
    gene_cov = gene_sum / counts[:, None]
    return (coverage, gene_cov)


def solution(mesh):
    in_specs = (
        P("seq", "trk"),
        P(None, None, "trk", None),
        P(None, "trk"),
        P(None, "trk", None),
        P(None, "trk"),
        P(None, "trk"),
        P("trk"),
        P("seq", None),
    )
    out_specs = (P("seq", "trk"), P("seq", "trk"))
    return jax.shard_map(shards, mesh=mesh, in_specs=in_specs, out_specs=out_specs, check_vma=False)
```

```python
import functools
import math

import jax
import jax.numpy as jnp
from jax import lax
from jax.experimental import pallas as pl
from jax.experimental.pallas import tpu as pltpu
from jax.sharding import PartitionSpec as P

RESIDUAL_BLOCKS = 6
BASE_DILATION = 2
BLOCKS_PER_LOAD = 2
FRAMED_BLOCKS = 4
DIGIT = 128
VMEM_BYTES = 56 * 2**20


def dilation(block):
    return BASE_DILATION * 2**block


def after(cells, *earlier):
    return lax.optimization_barrier((cells,) + earlier)[0]


def after_all(cells, *earlier):
    return list(lax.optimization_barrier(tuple(cells) + earlier)[: len(cells)])


def from_others(cells):
    count = lax.axis_size("trk")
    return [cells] + [
        lax.ppermute(cells, "trk", [(i, (i + k) % count) for i in range(count)])
        for k in range(1, count)
    ]


def halo(cells, width):
    count = lax.axis_size("seq")
    head = cells[:width]
    tail = cells[cells.shape[0] - width :]
    above = lax.ppermute(tail, "seq", [(i, i + 1) for i in range(count - 1)])
    below = lax.ppermute(head, "seq", [(i + 1, i) for i in range(count - 1)])
    return above, below


def group_size(rows, count):
    size = 1
    for g in range(1, count + 1):
        if count % g == 0 and rows % (16 * g) == 0:
            size = g
    return size


def tile_of(channels):
    for width in (512, 256, 384, 128):
        if channels % width == 0:
            return width
    return channels


def dot(a, b):
    return jnp.dot(a, b, preferred_element_type=jnp.float32)


def dot_last(a, b):
    return lax.dot_general(a, b, (((1,), (1,)), ((), ())), preferred_element_type=jnp.float32)


def gelu(x):
    cubic = x + 0.044715 * (x * x * x)
    return 0.5 * x * (1.0 + jnp.tanh(math.sqrt(2.0 / math.pi) * cubic))


def gelu_of_taps(sums, bias, step, rows):
    total = sums.shape[1]
    inner = sums[1] + pltpu.roll(sums[0], step, 0) + pltpu.roll(sums[2], total - step, 0)
    margin = (total - rows) // 2
    inner = inner[margin : margin + rows] + bias.astype(jnp.float32)
    return gelu(inner).astype(jnp.bfloat16)


def pack(act):
    half = act.shape[0] // 2
    return jnp.concatenate([act[:half], act[half:]], axis=1)


def unpack(cells):
    half = cells.shape[1] // 2
    return jnp.concatenate([cells[:, :half], cells[:, half:]], axis=0)


def first_kernel(step, own_rows, order_ref, c0, c1, c2, c3, w_ref, bias_ref, act_ref, trunk_ref, sums):
    k = pl.program_id(0)
    rows = trunk_ref.shape[0]
    for j, cell in enumerate((c0, c1, c2, c3)):

        @pl.when(k == j)
        def _():
            trunk_ref[...] = cell[:rows]

    tile = trunk_ref[...]
    for t in range(3):
        part = dot_last(tile, w_ref[0, t])
        sums[t] = jnp.where(k == 0, part, sums[t] + part)

    @pl.when(k == pl.num_programs(0) - 1)
    def _():
        act_ref[...] = pack(gelu_of_taps(sums, bias_ref[...], step, 2 * act_ref.shape[0]))


def first_conv(cells, rows, order, conv_in, bias, step):
    quarters = len(cells)
    _, _, hidden, channels = conv_in.shape
    width = cells[0].shape[1]
    full = pl.BlockSpec(cells[0].shape, lambda k, order: (0, 0))
    return pl.pallas_call(
        functools.partial(first_kernel, step, rows),
        grid_spec=pltpu.PrefetchScalarGridSpec(
            num_scalar_prefetch=1,
            grid=(quarters,),
            in_specs=[full] * quarters
            + [
                pl.BlockSpec((1, 3, hidden, width), lambda k, order: (0, 0, 0, order[k])),
                pl.BlockSpec((1, hidden), lambda k, order: (0, 0)),
            ],
            out_specs=[
                pl.BlockSpec((rows // 2, 2 * hidden), lambda k, order: (0, 0)),
                pl.BlockSpec((rows, width), lambda k, order: (0, order[k])),
            ],
            scratch_shapes=[pltpu.VMEM((3, rows, hidden), jnp.float32)],
        ),
        out_shape=[
            jax.ShapeDtypeStruct((rows // 2, 2 * hidden), jnp.bfloat16),
            jax.ShapeDtypeStruct((rows, channels), jnp.bfloat16),
        ],
        compiler_params=pltpu.CompilerParams(vmem_limit_bytes=VMEM_BYTES),
        cost_estimate=pl.CostEstimate(
            flops=6 * rows * hidden * channels,
            bytes_accessed=2 * (3 * hidden * channels + 2 * rows * channels),
            transcendentals=rows * hidden,
        ),
    )(order, *cells, conv_in, bias)


def project(acts, weights, trunk, bias):
    whole = jnp.concatenate([w[...].reshape(-1, w.shape[-1]) for w in weights], axis=0)
    return trunk.astype(jnp.float32) + bias.astype(jnp.float32) + dot(acts[...], whole)


def keep_acts(acts_ref, acts):
    acts_ref[...] = jnp.concatenate([unpack(a[...]) for a in acts], axis=1)


def fused_kernel(
    step, edge_ref, a0, a1, a2, a3, w0, w1, w2, w3, trunk_ref, pbias_ref, w_ref, bias_ref,
    act_ref, out_ref, acts_ref, sums
):
    c = pl.program_id(0)

    @pl.when(c == 0)
    def _():
        keep_acts(acts_ref, (a0, a1, a2, a3))

    total = project(acts_ref, (w0, w1, w2, w3), trunk_ref[...], pbias_ref[...])
    row = lax.broadcasted_iota(jnp.int32, total.shape, 0)
    inside = (row >= edge_ref[0]) & (row < edge_ref[1])
    tile = jnp.where(inside, total, 0.0).astype(jnp.bfloat16)
    out_ref[...] = tile
    for t in range(3):
        part = dot_last(tile, w_ref[0, t])
        sums[t] = jnp.where(c == 0, part, sums[t] + part)

    @pl.when(c == pl.num_programs(0) - 1)
    def _():
        act_ref[...] = pack(gelu_of_taps(sums, bias_ref[...], step, 2 * act_ref.shape[0]))


def projection_specs(load, part, acts, per_block, share, width):
    specs = [pl.BlockSpec(acts[0].shape, lambda c, *_: (0, 0))] * len(acts)
    for j in range(len(acts)):
        specs.append(
            pl.BlockSpec((per_block, share, width), lambda c, *_, j=j: (part, j, c))
        )
    return specs


def fused(acts, load, part, per_block, share, trunk, pbias, conv_in, block, bias, edge, rows_out):
    rows, channels = trunk.shape
    hidden = conv_in.shape[2]
    width = tile_of(channels)
    return pl.pallas_call(
        functools.partial(fused_kernel, dilation(block)),
        grid_spec=pltpu.PrefetchScalarGridSpec(
            num_scalar_prefetch=1,
            grid=(channels // width,),
            in_specs=projection_specs(load, part, acts, per_block, share, width)
            + [
                pl.BlockSpec((rows, width), lambda c, *_: (0, c)),
                pl.BlockSpec((1, width), lambda c, *_: (0, c)),
                pl.BlockSpec((1, 3, hidden, width), lambda c, *_: (block, 0, 0, c)),
                pl.BlockSpec((1, hidden), lambda c, *_: (0, 0)),
            ],
            out_specs=[
                pl.BlockSpec((rows_out // 2, 2 * hidden), lambda c, *_: (0, 0)),
                pl.BlockSpec((rows, width), lambda c, *_: (0, c)),
            ],
            scratch_shapes=[
                pltpu.VMEM((rows, len(acts) * hidden), jnp.bfloat16),
                pltpu.VMEM((3, rows, hidden), jnp.float32),
            ],
        ),
        out_shape=[
            jax.ShapeDtypeStruct((rows_out // 2, 2 * hidden), jnp.bfloat16),
            jax.ShapeDtypeStruct((rows, channels), jnp.bfloat16),
        ],
        compiler_params=pltpu.CompilerParams(vmem_limit_bytes=VMEM_BYTES),
        cost_estimate=pl.CostEstimate(
            flops=14 * rows * hidden * channels,
            bytes_accessed=2 * (7 * hidden * channels + 2 * rows * channels),
            transcendentals=rows * hidden,
        ),
    )(edge, *acts, *[load] * len(acts), trunk, pbias, conv_in, bias)


def projection_kernel(margin, a0, a1, a2, a3, w0, w1, w2, w3, trunk_ref, pbias_ref, out_ref, acts_ref):
    @pl.when(pl.program_id(0) == 0)
    def _():
        keep_acts(acts_ref, (a0, a1, a2, a3))

    rows = out_ref.shape[0]
    total = project(
        acts_ref, (w0, w1, w2, w3), trunk_ref[margin : margin + rows], pbias_ref[...]
    )
    out_ref[...] = total.astype(jnp.bfloat16)


def projection(acts, load, part, per_block, share, trunk, pbias):
    frame, channels = trunk.shape
    rows, hidden = 2 * acts[0].shape[0], acts[0].shape[1] // 2
    width = tile_of(channels)
    return pl.pallas_call(
        functools.partial(projection_kernel, (frame - rows) // 2),
        grid=(channels // width,),
        in_specs=projection_specs(load, part, acts, per_block, share, width)
        + [
            pl.BlockSpec((frame, width), lambda c: (0, c)),
            pl.BlockSpec((1, width), lambda c: (0, c)),
        ],
        out_specs=pl.BlockSpec((rows, width), lambda c: (0, c)),
        scratch_shapes=[pltpu.VMEM((rows, len(acts) * hidden), jnp.bfloat16)],
        out_shape=jax.ShapeDtypeStruct((rows, channels), jnp.bfloat16),
        compiler_params=pltpu.CompilerParams(vmem_limit_bytes=VMEM_BYTES),
        cost_estimate=pl.CostEstimate(
            flops=8 * rows * hidden * channels,
            bytes_accessed=2 * (4 * hidden * channels + 2 * rows * channels),
            transcendentals=0,
        ),
    )(*acts, *[load] * len(acts), trunk, pbias)


def conv_kernel(step, above_ref, trunk_ref, below_ref, w_ref, bias_ref, act_ref, sums):
    c = pl.program_id(0)
    tile = jnp.concatenate([above_ref[...], trunk_ref[...], below_ref[...]], axis=0)
    for t in range(3):
        part = dot_last(tile, w_ref[0, t])
        sums[t] = jnp.where(c == 0, part, sums[t] + part)

    @pl.when(c == pl.num_programs(0) - 1)
    def _():
        act_ref[...] = pack(gelu_of_taps(sums, bias_ref[...], step, 2 * act_ref.shape[0]))


def conv(above, trunk, below, conv_in, block, bias):
    rows, channels = trunk.shape
    hidden = conv_in.shape[2]
    step = dilation(block)
    width = tile_of(channels)
    return pl.pallas_call(
        functools.partial(conv_kernel, step),
        grid=(channels // width,),
        in_specs=[
            pl.BlockSpec((step, width), lambda c: (0, c)),
            pl.BlockSpec((rows, width), lambda c: (0, c)),
            pl.BlockSpec((step, width), lambda c: (0, c)),
            pl.BlockSpec((1, 3, hidden, width), lambda c: (block, 0, 0, c)),
            pl.BlockSpec((1, hidden), lambda c: (0, 0)),
        ],
        out_specs=pl.BlockSpec((rows // 2, 2 * hidden), lambda c: (0, 0)),
        scratch_shapes=[pltpu.VMEM((3, rows + 2 * step, hidden), jnp.float32)],
        out_shape=jax.ShapeDtypeStruct((rows // 2, 2 * hidden), jnp.bfloat16),
        compiler_params=pltpu.CompilerParams(vmem_limit_bytes=VMEM_BYTES),
        cost_estimate=pl.CostEstimate(
            flops=6 * rows * hidden * channels,
            bytes_accessed=2 * (3 * hidden * channels + rows * channels),
            transcendentals=rows * hidden,
        ),
    )(above, trunk, below, conv_in, bias)


def head_kernel(
    a0, a1, a2, a3, w0, w1, w2, w3, trunk_ref, pbias_ref, head_ref, hbias_ref, onehot_ref,
    cover_ref, gene_ref, acts_ref, logits
):
    c = pl.program_id(0)

    @pl.when(c == 0)
    def _():
        keep_acts(acts_ref, (a0, a1, a2, a3))

    total = project(acts_ref, (w0, w1, w2, w3), trunk_ref[...], pbias_ref[...])
    part = dot(total.astype(jnp.bfloat16), head_ref[...])
    logits[...] = jnp.where(c == 0, part, logits[...] + part)

    @pl.when(c == pl.num_programs(0) - 1)
    def _():
        x = logits[...] + hbias_ref[...].astype(jnp.float32)
        cover = (jnp.maximum(x, 0.0) + jnp.log1p(jnp.exp(-jnp.abs(x)))).astype(jnp.bfloat16)
        cover_ref[...] = cover
        gene_ref[...] = dot(onehot_ref[...], cover).astype(jnp.bfloat16)


def head(acts, load, part, per_block, share, trunk, pbias, head_weight, head_bias, onehot):
    rows, channels = trunk.shape
    hidden = acts[0].shape[1] // 2
    tracks = head_weight.shape[1]
    genes = onehot.shape[0]
    width = tile_of(channels)
    return pl.pallas_call(
        head_kernel,
        grid=(channels // width,),
        in_specs=projection_specs(load, part, acts, per_block, share, width)
        + [
            pl.BlockSpec((rows, width), lambda c: (0, c)),
            pl.BlockSpec((1, width), lambda c: (0, c)),
            pl.BlockSpec((width, tracks), lambda c: (c, 0)),
            pl.BlockSpec((1, tracks), lambda c: (0, 0)),
            pl.BlockSpec((genes, rows), lambda c: (0, 0)),
        ],
        out_specs=[
            pl.BlockSpec((rows, tracks), lambda c: (0, 0)),
            pl.BlockSpec((genes, tracks), lambda c: (0, 0)),
        ],
        scratch_shapes=[
            pltpu.VMEM((rows, len(acts) * hidden), jnp.bfloat16),
            pltpu.VMEM((rows, tracks), jnp.float32),
        ],
        out_shape=[
            jax.ShapeDtypeStruct((rows, tracks), jnp.bfloat16),
            jax.ShapeDtypeStruct((genes, tracks), jnp.bfloat16),
        ],
        compiler_params=pltpu.CompilerParams(vmem_limit_bytes=VMEM_BYTES),
        cost_estimate=pl.CostEstimate(
            flops=8 * rows * hidden * channels + 2 * rows * channels * tracks,
            bytes_accessed=2 * (4 * hidden * channels + rows * channels + channels * tracks),
            transcendentals=2 * rows * tracks,
        ),
    )(*acts, *[load] * len(acts), trunk, pbias, head_weight, head_bias, onehot)


def exon_digits(exon_bins, channels):
    digits = jnp.concatenate([exon_bins >> 7, exon_bins & (DIGIT - 1)], axis=1)
    genes, width = digits.shape
    return jnp.pad(digits.astype(jnp.bfloat16), ((0, -genes % 16), (0, channels - width)))


def exon_lists(rows, genes, entries):
    digits = rows[:, :genes, : 2 * entries].astype(jnp.int32)
    lists = digits[:, :, :entries] * DIGIT + digits[:, :, entries:]
    return lists.reshape(-1, entries)


def exon_onehot(gene_block, first_bin, width_now):
    exon_matches = (
        gene_block[:, :, None] - first_bin == jnp.arange(width_now, dtype=jnp.int32)[None, None, :]
    )
    return jnp.sum(exon_matches.astype(jnp.float32), axis=1).astype(jnp.bfloat16)


def shards(
    trunk_input, conv_in, conv_bias, conv_out, projection_bias, head_weight, head_bias, exon_bins
):
    quarters = lax.axis_size("trk")
    place = lax.axis_index("trk")
    count = lax.axis_size("seq")
    lane = lax.axis_index("seq")
    bin_rows, channels_here = trunk_input.shape
    blocks, hidden, channels = conv_out.shape
    genes_here, entries = exon_bins.shape

    load_rows = BLOCKS_PER_LOAD * hidden
    size = group_size(load_rows, count)
    share = load_rows // size
    per_block = hidden // share
    groups = [[g * size + i for i in range(size)] for g in range(count // size)]
    mine = lax.rem(lane, size)
    packed = size == count and 2 * entries <= channels

    def column(load):
        first = load * BLOCKS_PER_LOAD
        flat = conv_out[first : first + BLOCKS_PER_LOAD].reshape(load_rows, channels)
        return lax.dynamic_slice_in_dim(flat, mine * share, share, 0)

    def gather(parts):
        return lax.all_gather(
            jnp.concatenate(parts, axis=0), "seq", axis=0, tiled=False, axis_index_groups=groups
        )

    margin = dilation(FRAMED_BLOCKS)
    frame = bin_rows + 2 * margin
    order = lax.rem(place - jnp.arange(quarters, dtype=jnp.int32) + quarters, quarters)
    edge = jnp.stack(
        [
            jnp.where(lane == 0, margin, 0),
            jnp.where(lane == count - 1, margin + bin_rows, frame),
        ]
    ).astype(jnp.int32)

    above, below = halo(trunk_input, margin)
    first_column = from_others(column(0))
    loads = [gather(after_all(first_column, above, below))]
    own = jnp.concatenate(
        [above, trunk_input, below, jnp.pad(projection_bias, ((0, -blocks % 16), (0, 0)))], axis=0
    )
    own = after(own, *first_column)
    cells = from_others(own)
    second = from_others(after(column(1), *cells))

    act, trunk = first_conv(cells, frame, order, conv_in, conv_bias[:1], dilation(0))
    biases = jnp.zeros((blocks, channels), jnp.bfloat16)
    for k in range(quarters):
        biases = lax.dynamic_update_slice_in_dim(
            biases, cells[k][frame : frame + blocks], order[k] * channels_here, 1
        )

    onehot = None
    for block in range(RESIDUAL_BLOCKS):
        others = from_others(act)
        if block == 0:
            loads.append(gather(after_all(second, *others)))
            third = from_others(after(column(2), *others))
        if block == 1:
            tail = [exon_digits(exon_bins, channels)] if packed else []
            loads.append(gather(after_all(third, *others) + tail))
        if block == 4:
            if packed:
                gene_lists = exon_lists(loads[2][:, quarters * share :], genes_here, entries)
            else:
                gene_lists = lax.all_gather(exon_bins, "seq", axis=0, tiled=True)
            onehot = exon_onehot(gene_lists, lane * bin_rows, bin_rows)
        load = loads[block // BLOCKS_PER_LOAD]
        part = block % BLOCKS_PER_LOAD
        where = (load, part, per_block, share, trunk, biases[block : block + 1])
        later = block + 1
        if later < FRAMED_BLOCKS:
            rows_out = frame if later < FRAMED_BLOCKS - 1 else bin_rows
            act, trunk = fused(
                others, *where, conv_in, later, conv_bias[later : later + 1], edge, rows_out
            )
        elif later < RESIDUAL_BLOCKS:
            trunk = projection(others, *where)
            above, below = halo(trunk, dilation(later))
            act = conv(above, trunk, below, conv_in, later, conv_bias[later : later + 1])
        else:
            coverage, partial = head(others, *where, head_weight, head_bias[None, :], onehot)

    parts = lax.all_to_all(
        partial.reshape(count, genes_here, partial.shape[1]), "seq", 0, 0, tiled=False
    )
    gene_sum = jnp.sum(parts.astype(jnp.float32), axis=0)
    counts = jnp.sum((exon_bins >= 0).astype(jnp.float32), axis=1)
    gene_cov = gene_sum / counts[:, None]
    return (coverage, gene_cov)


def solution(mesh):
    in_specs = (
        P("seq", "trk"),
        P(None, None, "trk", None),
        P(None, "trk"),
        P(None, "trk", None),
        P(None, "trk"),
        P(None, "trk"),
        P("trk"),
        P("seq", None),
    )
    out_specs = (P("seq", "trk"), P("seq", "trk"))
    return jax.shard_map(shards, mesh=mesh, in_specs=in_specs, out_specs=out_specs, check_vma=False)
```

```python
import functools
import math

import jax
import jax.numpy as jnp
from jax import lax
from jax.experimental import pallas as pl
from jax.experimental.pallas import tpu as pltpu
from jax.sharding import PartitionSpec as P

RESIDUAL_BLOCKS = 6
BASE_DILATION = 2
BLOCKS_PER_LOAD = 2
FRAMED_BLOCKS = 4
DIGIT = 128
VMEM_BYTES = 24 * 2**20


def dilation(block):
    return BASE_DILATION * 2**block


def after(cells, *earlier):
    return lax.optimization_barrier((cells,) + earlier)[0]


def after_all(cells, *earlier):
    return list(lax.optimization_barrier(tuple(cells) + earlier)[: len(cells)])


def from_others(cells):
    count = lax.axis_size("trk")
    return [cells] + [
        lax.ppermute(cells, "trk", [(i, (i + k) % count) for i in range(count)])
        for k in range(1, count)
    ]


def halo(cells, width):
    count = lax.axis_size("seq")
    head = cells[:width]
    tail = cells[cells.shape[0] - width :]
    above = lax.ppermute(tail, "seq", [(i, i + 1) for i in range(count - 1)])
    below = lax.ppermute(head, "seq", [(i + 1, i) for i in range(count - 1)])
    return above, below


def group_size(rows, count):
    size = 1
    for g in range(1, count + 1):
        if count % g == 0 and rows % (16 * g) == 0:
            size = g
    return size


def tile_of(channels):
    for width in (512, 256, 384, 128):
        if channels % width == 0:
            return width
    return channels


def dot(a, b):
    return jnp.dot(a, b, preferred_element_type=jnp.float32)


def dot_last(a, b):
    return lax.dot_general(a, b, (((1,), (1,)), ((), ())), preferred_element_type=jnp.float32)


def gelu(x):
    cubic = x + 0.044715 * (x * x * x)
    return 0.5 * x * (1.0 + jnp.tanh(math.sqrt(2.0 / math.pi) * cubic))


def pack(act):
    half = act.shape[0] // 2
    return jnp.concatenate([act[:half], act[half:]], axis=1)


def unpack(cells):
    half = cells.shape[1] // 2
    return jnp.concatenate([cells[:, :half], cells[:, half:]], axis=0)


class Copies:
    def __init__(self, sems):
        self.sems = sems
        self.used = 0

    def start(self, source, target):
        copy = pltpu.make_async_copy(source, target, self.sems.at[self.used])
        self.used += 1
        copy.start()
        return copy


def wait(copies):
    for copy in copies:
        copy.wait()


def columns(tile, width):
    return pl.ds(tile * width, width)


def start_acts(copies, acts, raw):
    return [copies.start(act, raw.at[j]) for j, act in enumerate(acts)]


def start_projection(copies, load, part, raw):
    quarters, per_block, share, channels = raw.shape
    width = tile_of(channels)
    tiles = []
    for c in range(channels // width):
        tiles.append(
            [
                copies.start(
                    load.at[
                        pl.ds(part * per_block, per_block), pl.ds(j * share, share), columns(c, width)
                    ],
                    raw.at[j, :, :, columns(c, width)],
                )
                for j in range(quarters)
            ]
        )
    return tiles


def start_trunk(copies, trunk, margin, target):
    rows, channels = target.shape
    width = tile_of(channels)
    return [
        copies.start(trunk.at[pl.ds(margin, rows), columns(c, width)], target.at[:, columns(c, width)])
        for c in range(channels // width)
    ]


def start_taps(copies, conv_in, block, target):
    half = target.shape[1] // 2
    return [
        [
            copies.start(conv_in.at[block, t, pl.ds(h * half, half)], target.at[t, pl.ds(h * half, half)])
            for h in range(2)
        ]
        for t in range(3)
    ]


def project(acts, weights, trunk, bias, c):
    channels = trunk.shape[1]
    cols = columns(c, tile_of(channels))
    part = dot(acts, weights[:, :, :, cols].reshape(-1, tile_of(channels)))
    total = trunk[:, cols].astype(jnp.float32) + bias[:, cols].astype(jnp.float32) + part
    trunk[:, cols] = total.astype(jnp.bfloat16)


def project_all(raw, act_copies, weights, weight_copies, trunk, trunk_copies, bias):
    wait(act_copies)
    acts = jnp.concatenate([unpack(raw[j]) for j in range(raw.shape[0])], axis=1)
    for c in range(len(weight_copies)):
        wait(weight_copies[c])
        trunk_copies[c].wait()
        project(acts, weights, trunk, bias, c)


def convolve(trunk, rows, taps, tap_copies, bias, step, act_ref):
    cells = trunk[:rows]
    sums = []
    for t in range(3):
        wait(tap_copies[t])
        sums.append(dot_last(cells, taps[t]))
    inner = sums[1] + pltpu.roll(sums[0], step, 0) + pltpu.roll(sums[2], rows - step, 0)
    keep = 2 * act_ref.shape[0]
    margin = (rows - keep) // 2
    inner = inner[margin : margin + keep] + bias.astype(jnp.float32)
    act_ref[...] = pack(gelu(inner).astype(jnp.bfloat16))


def first_kernel(
    step, order_ref, c0, c1, c2, c3, conv_in, bias_ref, act_ref, trunk_out, pbias_out, trunk, taps, sems
):
    copies = Copies(sems)
    width = c0.shape[1]
    cells = [
        copies.start(cell, trunk.at[:, pl.ds(pl.multiple_of(order_ref[k] * width, 128), width)])
        for k, cell in enumerate((c0, c1, c2, c3))
    ]
    tap_copies = start_taps(copies, conv_in, 0, taps)
    wait(cells)
    rows = trunk_out.shape[0]
    out = [
        copies.start(trunk.at[pl.ds(0, rows)], trunk_out),
        copies.start(trunk.at[pl.ds(rows, pbias_out.shape[0])], pbias_out),
    ]
    convolve(trunk, rows, taps, tap_copies, bias_ref[0:1], step, act_ref)
    wait(out)


ANY = pl.BlockSpec(memory_space=pl.ANY)
HBM = pl.BlockSpec(memory_space=pltpu.HBM)
SMEM = pl.BlockSpec(memory_space=pltpu.SMEM)
VMEM = pl.BlockSpec(memory_space=pltpu.VMEM)
BF16 = jnp.bfloat16


def shape(*dims):
    return jax.ShapeDtypeStruct(dims, BF16)


def kernel_call(body, ins, outs, out_specs, specs, scratch, flops, moved, special=0):
    return pl.pallas_call(
        body,
        in_specs=specs,
        out_specs=out_specs,
        out_shape=outs,
        scratch_shapes=scratch + [pltpu.SemaphoreType.DMA((48,))],
        compiler_params=pltpu.CompilerParams(vmem_limit_bytes=VMEM_BYTES),
        cost_estimate=pl.CostEstimate(
            flops=flops, bytes_accessed=2 * moved, transcendentals=special
        ),
    )(*ins)


def first_conv(cells, rows, order, conv_in, conv_bias, step):
    _, _, hidden, channels = conv_in.shape
    total = cells[0].shape[0]
    return kernel_call(
        functools.partial(first_kernel, step),
        (order, *cells, conv_in, conv_bias),
        [shape(rows // 2, 2 * hidden), shape(rows, channels), shape(total - rows, channels)],
        [VMEM, ANY, ANY],
        [SMEM] + [ANY] * len(cells) + [HBM, VMEM],
        [pltpu.VMEM((total, channels), BF16), pltpu.VMEM((3, hidden, channels), BF16)],
        6 * rows * hidden * channels,
        3 * hidden * channels + 2 * rows * channels,
        rows * hidden,
    )


def fused_kernel(
    block, part, edge_ref, a0, a1, a2, a3, load, trunk_in, pbias_ref, conv_in, bias_ref,
    act_ref, trunk_out, raw, weights, trunk, taps, sems
):
    copies = Copies(sems)
    act_copies = start_acts(copies, (a0, a1, a2, a3), raw)
    weight_copies = start_projection(copies, load, part, weights)
    trunk_copies = start_trunk(copies, trunk_in, 0, trunk)
    tap_copies = start_taps(copies, conv_in, block + 1, taps)
    pbias = pbias_ref[block : block + 1]
    project_all(raw, act_copies, weights, weight_copies, trunk, trunk_copies, pbias)
    rows = trunk.shape[0]
    margin = dilation(FRAMED_BLOCKS)

    @pl.when(edge_ref[0] == 1)
    def _():
        trunk[:margin] = jnp.zeros((margin, trunk.shape[1]), BF16)

    @pl.when(edge_ref[1] == 1)
    def _():
        trunk[rows - margin :] = jnp.zeros((margin, trunk.shape[1]), BF16)

    out = copies.start(trunk, trunk_out)
    bias = bias_ref[block + 1 : block + 2]
    convolve(trunk, rows, taps, tap_copies, bias, dilation(block + 1), act_ref)
    out.wait()


def projection_scratch(acts, per_block, share, channels):
    return [
        pltpu.VMEM((len(acts),) + acts[0].shape, BF16),
        pltpu.VMEM((len(acts), per_block, share, channels), BF16),
    ]


def fused(acts, load, part, per_block, share, trunk, pbias, conv_in, conv_bias, block, edge, rows_out):
    rows, channels = trunk.shape
    hidden = conv_in.shape[2]
    return kernel_call(
        functools.partial(fused_kernel, block, part),
        (edge, *acts, load, trunk, pbias, conv_in, conv_bias),
        [shape(rows_out // 2, 2 * hidden), shape(rows, channels)],
        [VMEM, ANY],
        [SMEM] + [ANY] * len(acts) + [HBM, ANY, VMEM, HBM, VMEM],
        projection_scratch(acts, per_block, share, channels)
        + [pltpu.VMEM((rows, channels), BF16), pltpu.VMEM((3, hidden, channels), BF16)],
        14 * rows * hidden * channels,
        7 * hidden * channels + 2 * rows * channels,
        rows * hidden,
    )


def projection_kernel(block, part, a0, a1, a2, a3, load, trunk_in, pbias_ref, trunk, raw, weights, sems):
    copies = Copies(sems)
    act_copies = start_acts(copies, (a0, a1, a2, a3), raw)
    weight_copies = start_projection(copies, load, part, weights)
    margin = (trunk_in.shape[0] - trunk.shape[0]) // 2
    trunk_copies = start_trunk(copies, trunk_in, margin, trunk)
    pbias = pbias_ref[block : block + 1]
    project_all(raw, act_copies, weights, weight_copies, trunk, trunk_copies, pbias)


def projection(acts, load, part, per_block, share, trunk, pbias, block):
    channels = trunk.shape[1]
    rows, hidden = 2 * acts[0].shape[0], acts[0].shape[1] // 2
    return kernel_call(
        functools.partial(projection_kernel, block, part),
        (*acts, load, trunk, pbias),
        shape(rows, channels),
        VMEM,
        [ANY] * len(acts) + [HBM, ANY, VMEM],
        projection_scratch(acts, per_block, share, channels),
        8 * rows * hidden * channels,
        4 * hidden * channels + 2 * rows * channels,
    )


def conv_kernel(block, above, trunk_in, below, conv_in, bias_ref, act_ref, trunk, taps, sems):
    copies = Copies(sems)
    step = dilation(block)
    rows = trunk_in.shape[0]
    cells = [
        copies.start(trunk_in, trunk.at[pl.ds(step, rows)]),
        copies.start(above, trunk.at[pl.ds(0, step)]),
        copies.start(below, trunk.at[pl.ds(step + rows, step)]),
    ]
    tap_copies = start_taps(copies, conv_in, block, taps)
    wait(cells)
    bias = bias_ref[block : block + 1]
    convolve(trunk, trunk.shape[0], taps, tap_copies, bias, step, act_ref)


def conv(above, trunk, below, conv_in, block, conv_bias):
    rows, channels = trunk.shape
    hidden = conv_in.shape[2]
    frame = rows + 2 * dilation(block)
    return kernel_call(
        functools.partial(conv_kernel, block),
        (above, trunk, below, conv_in, conv_bias),
        shape(rows // 2, 2 * hidden),
        VMEM,
        [ANY] * 3 + [HBM, VMEM],
        [pltpu.VMEM((frame, channels), BF16), pltpu.VMEM((3, hidden, channels), BF16)],
        6 * frame * hidden * channels,
        3 * hidden * channels + frame * channels,
        rows * hidden,
    )


def head_kernel(
    block, part, a0, a1, a2, a3, load, trunk_in, pbias_ref, head_ref, hbias_ref, onehot_ref,
    cover_out, gene_ref, raw, weights, trunk, head_w, cover, sems
):
    copies = Copies(sems)
    act_copies = start_acts(copies, (a0, a1, a2, a3), raw)
    weight_copies = start_projection(copies, load, part, weights)
    trunk_copies = start_trunk(copies, trunk_in, 0, trunk)
    channels, tracks = head_w.shape
    width = tile_of(tracks)
    band = channels // 4
    head_copies = [
        [
            copies.start(
                head_ref.at[pl.ds(r * band, band), columns(c, width)],
                head_w.at[pl.ds(r * band, band), columns(c, width)],
            )
            for r in range(4)
        ]
        for c in range(tracks // width)
    ]
    pbias = pbias_ref[block : block + 1]
    project_all(raw, act_copies, weights, weight_copies, trunk, trunk_copies, pbias)
    out = []
    for c in range(tracks // width):
        cols = columns(c, width)
        wait(head_copies[c])
        x = dot(trunk[...], head_w[:, cols]) + hbias_ref[:, cols].astype(jnp.float32)
        tile = (jnp.maximum(x, 0.0) + jnp.log1p(jnp.exp(-jnp.abs(x)))).astype(BF16)
        cover[:, cols] = tile
        out.append(copies.start(cover.at[:, cols], cover_out.at[:, cols]))
        gene_ref[:, cols] = dot(onehot_ref[...], tile).astype(BF16)
    wait(out)


def head(acts, load, part, per_block, share, trunk, pbias, block, head_weight, head_bias, onehot):
    rows, channels = trunk.shape
    hidden = acts[0].shape[1] // 2
    tracks = head_weight.shape[1]
    genes = onehot.shape[0]
    return kernel_call(
        functools.partial(head_kernel, block, part),
        (*acts, load, trunk, pbias, head_weight, head_bias, onehot),
        [shape(rows, tracks), shape(genes, tracks)],
        [ANY, VMEM],
        [ANY] * len(acts) + [HBM, ANY, VMEM, HBM, VMEM, VMEM],
        projection_scratch(acts, per_block, share, channels)
        + [
            pltpu.VMEM((rows, channels), BF16),
            pltpu.VMEM((channels, tracks), BF16),
            pltpu.VMEM((rows, tracks), BF16),
        ],
        8 * rows * hidden * channels + 2 * rows * channels * tracks,
        4 * hidden * channels + rows * channels + channels * tracks,
        2 * rows * tracks,
    )


def exon_digits(exon_bins, channels):
    digits = jnp.concatenate([exon_bins >> 7, exon_bins & (DIGIT - 1)], axis=1)
    genes, width = digits.shape
    return jnp.pad(digits.astype(jnp.bfloat16), ((0, -genes % 16), (0, channels - width)))


def exon_lists(rows, genes, entries):
    digits = rows[:, :genes, : 2 * entries].astype(jnp.int32)
    lists = digits[:, :, :entries] * DIGIT + digits[:, :, entries:]
    return lists.reshape(-1, entries)


def exon_onehot(gene_block, first_bin, width_now):
    exon_matches = (
        gene_block[:, :, None] - first_bin == jnp.arange(width_now, dtype=jnp.int32)[None, None, :]
    )
    return jnp.sum(exon_matches.astype(jnp.float32), axis=1).astype(jnp.bfloat16)


def shards(
    trunk_input, conv_in, conv_bias, conv_out, projection_bias, head_weight, head_bias, exon_bins
):
    quarters = lax.axis_size("trk")
    place = lax.axis_index("trk")
    count = lax.axis_size("seq")
    lane = lax.axis_index("seq")
    bin_rows, channels_here = trunk_input.shape
    blocks, hidden, channels = conv_out.shape
    genes_here, entries = exon_bins.shape

    load_rows = BLOCKS_PER_LOAD * hidden
    size = group_size(load_rows, count)
    share = load_rows // size
    per_block = hidden // share
    groups = [[g * size + i for i in range(size)] for g in range(count // size)]
    mine = lax.rem(lane, size)
    packed = size == count and 2 * entries <= channels

    def column(load):
        first = load * BLOCKS_PER_LOAD
        flat = conv_out[first : first + BLOCKS_PER_LOAD].reshape(load_rows, channels)
        return lax.dynamic_slice_in_dim(flat, mine * share, share, 0)

    def gather(parts):
        return lax.all_gather(
            jnp.concatenate(parts, axis=0), "seq", axis=0, tiled=False, axis_index_groups=groups
        )

    margin = dilation(FRAMED_BLOCKS)
    frame = bin_rows + 2 * margin
    order = lax.rem(place - jnp.arange(quarters, dtype=jnp.int32) + quarters, quarters)
    edge = jnp.stack([lane == 0, lane == count - 1]).astype(jnp.int32)

    above, below = halo(trunk_input, margin)
    first_column = from_others(column(0))
    loads = [gather(after_all(first_column, above, below))]
    own = jnp.concatenate(
        [above, trunk_input, below, jnp.pad(projection_bias, ((0, -blocks % 16), (0, 0)))], axis=0
    )
    own = after(own, *first_column)
    cells = from_others(own)
    second = from_others(after(column(1), *cells))

    act, trunk, biases = first_conv(cells, frame, order, conv_in, conv_bias, dilation(0))

    onehot = None
    for block in range(RESIDUAL_BLOCKS):
        others = from_others(act)
        if block == 0:
            third = from_others(after(column(2), *others))
        if block == 1:
            loads.append(gather(after_all(second, act)))
        if block == 2:
            tail = [exon_digits(exon_bins, channels)] if packed else []
            loads.append(gather(after_all(third, act) + tail))
        if block == 4:
            if packed:
                gene_lists = exon_lists(loads[2][:, quarters * share :], genes_here, entries)
            else:
                gene_lists = lax.all_gather(exon_bins, "seq", axis=0, tiled=True)
            onehot = exon_onehot(gene_lists, lane * bin_rows, bin_rows)
        load = loads[block // BLOCKS_PER_LOAD]
        part = block % BLOCKS_PER_LOAD
        where = (load, part, per_block, share, trunk, biases)
        later = block + 1
        if later < FRAMED_BLOCKS:
            rows_out = frame if later < FRAMED_BLOCKS - 1 else bin_rows
            act, trunk = fused(others, *where, conv_in, conv_bias, block, edge, rows_out)
        elif later < RESIDUAL_BLOCKS:
            trunk = projection(others, *where, block)
            above, below = halo(trunk, dilation(later))
            act = conv(above, trunk, below, conv_in, later, conv_bias)
        else:
            coverage, partial = head(
                others, *where, block, head_weight, head_bias[None, :], onehot
            )

    parts = lax.all_to_all(
        partial.reshape(count, genes_here, partial.shape[1]), "seq", 0, 0, tiled=False
    )
    gene_sum = jnp.sum(parts.astype(jnp.float32), axis=0)
    counts = jnp.sum((exon_bins >= 0).astype(jnp.float32), axis=1)
    gene_cov = gene_sum / counts[:, None]
    return (coverage, gene_cov)


def solution(mesh):
    in_specs = (
        P("seq", "trk"),
        P(None, None, "trk", None),
        P(None, "trk"),
        P(None, "trk", None),
        P(None, "trk"),
        P(None, "trk"),
        P("trk"),
        P("seq", None),
    )
    out_specs = (P("seq", "trk"), P("seq", "trk"))
    return jax.shard_map(shards, mesh=mesh, in_specs=in_specs, out_specs=out_specs, check_vma=False)
```

```python
import functools
import math

import jax
import jax.numpy as jnp
from jax import lax
from jax.experimental import pallas as pl
from jax.experimental.pallas import tpu as pltpu
from jax.sharding import PartitionSpec as P

RESIDUAL_BLOCKS = 6
BASE_DILATION = 2
BLOCKS_PER_LOAD = 2
FRAMED_BLOCKS = 4
DIGIT = 128
VMEM_BYTES = 20 * 2**20
STAGE_BYTES = 40 * 2**20


def dilation(block):
    return BASE_DILATION * 2**block


def after(cells, *earlier):
    return lax.optimization_barrier((cells,) + earlier)[0]


def after_all(cells, *earlier):
    return list(lax.optimization_barrier(tuple(cells) + earlier)[: len(cells)])


def from_others(cells):
    count = lax.axis_size("trk")
    return [cells] + [
        lax.ppermute(cells, "trk", [(i, (i + k) % count) for i in range(count)])
        for k in range(1, count)
    ]


def halo(cells, width):
    count = lax.axis_size("seq")
    head = cells[:width]
    tail = cells[cells.shape[0] - width :]
    above = lax.ppermute(tail, "seq", [(i, i + 1) for i in range(count - 1)])
    below = lax.ppermute(head, "seq", [(i + 1, i) for i in range(count - 1)])
    return above, below


def group_size(rows, count):
    size = 1
    for g in range(1, count + 1):
        if count % g == 0 and rows % (16 * g) == 0:
            size = g
    return size


def tile_of(channels):
    for width in (512, 256, 384, 128):
        if channels % width == 0:
            return width
    return channels


def dot(a, b):
    return jnp.dot(a, b, preferred_element_type=jnp.float32)


def dot_last(a, b):
    return lax.dot_general(a, b, (((1,), (1,)), ((), ())), preferred_element_type=jnp.float32)


def gelu(x):
    cubic = x + 0.044715 * (x * x * x)
    return 0.5 * x * (1.0 + jnp.tanh(math.sqrt(2.0 / math.pi) * cubic))


def pack(act):
    half = act.shape[0] // 2
    return jnp.concatenate([act[:half], act[half:]], axis=1)


def unpack(cells):
    half = cells.shape[1] // 2
    return jnp.concatenate([cells[:, :half], cells[:, half:]], axis=0)


def columns(tile, width):
    return pl.ds(tile * width, width)


def project_all(acts, weight, trunk, margin, bias, target):
    rows, channels = target.shape
    width = tile_of(channels)
    cells = jnp.concatenate([unpack(act[...]) for act in acts], axis=1)
    for c in range(channels // width):
        cols = columns(c, width)
        total = dot(cells, weight[:, cols]) + bias[:, cols].astype(jnp.float32)
        total = total + trunk[pl.ds(margin, rows), cols].astype(jnp.float32)
        target[:, cols] = total.astype(BF16)


def convolve(cells, taps, bias, step, act_ref):
    rows = cells.shape[0]
    sums = [dot_last(cells, taps[t]) for t in range(3)]
    inner = sums[1] + pltpu.roll(sums[0], step, 0) + pltpu.roll(sums[2], rows - step, 0)
    keep = 2 * act_ref.shape[0]
    margin = (rows - keep) // 2
    inner = inner[margin : margin + keep] + bias.astype(jnp.float32)
    act_ref[...] = pack(gelu(inner).astype(BF16))


BF16 = jnp.bfloat16
ANY = pl.BlockSpec(memory_space=pl.ANY)
SMEM = pl.BlockSpec(memory_space=pltpu.SMEM)
VMEM = pl.BlockSpec(memory_space=pltpu.VMEM)


def shape(*dims):
    return jax.ShapeDtypeStruct(dims, BF16)


def kernel_call(body, ins, outs, flops, moved, special=0, scalars=0, scratch=(), limit=VMEM_BYTES, specs=None):
    return pl.pallas_call(
        body,
        in_specs=specs or [SMEM] * scalars + [VMEM] * (len(ins) - scalars),
        out_specs=[VMEM] * len(outs),
        out_shape=list(outs),
        scratch_shapes=list(scratch),
        compiler_params=pltpu.CompilerParams(vmem_limit_bytes=limit),
        cost_estimate=pl.CostEstimate(
            flops=flops, bytes_accessed=2 * moved, transcendentals=special
        ),
    )(*ins)


def stage_kernel(plan, *refs):
    sems = refs[-1]
    used = 0
    copies = []
    for source, target, cuts in plan:
        for src, dst in cuts(refs[source], refs[target]):
            copies.append(pltpu.make_async_copy(src, dst, sems.at[used]))
            used += 1
    for copy in copies:
        copy.start()
    for copy in copies:
        copy.wait()


def projection_cuts(part, per_block, share, load, target):
    return [
        (
            load.at[part * per_block + i, pl.ds(j * share, share)],
            target.at[pl.ds((j * per_block + i) * share, share)],
        )
        for j in range(target.shape[0] // (per_block * share))
        for i in range(per_block)
    ]


def tap_cuts(block, conv_in, target):
    return [(conv_in.at[block, t], target.at[t]) for t in range(3)]


def whole_cuts(source, target):
    return [(source, target)]


def stage(sources, targets, cuts):
    count = len(sources)
    plan = [(i, count + i, cut) for i, cut in enumerate(cuts)]
    return kernel_call(
        functools.partial(stage_kernel, plan),
        sources,
        targets,
        0,
        sum(math.prod(t.shape) for t in targets),
        scratch=[pltpu.SemaphoreType.DMA((32,))],
        specs=[ANY] * count,
        limit=STAGE_BYTES,
    )


def first_kernel(step, order_ref, c0, c1, c2, c3, taps, bias_ref, act_ref, trunk, pbias):
    width = c0.shape[1]
    rows = trunk.shape[0]
    for k, cell in enumerate((c0, c1, c2, c3)):
        cols = pl.ds(pl.multiple_of(order_ref[k] * width, 128), width)
        trunk[:, cols] = cell[:rows]
        pbias[:, cols] = cell[rows:]
    convolve(trunk[...], taps, bias_ref[0:1], step, act_ref)


def first_conv(cells, rows, order, taps, conv_bias, step):
    _, hidden, channels = taps.shape
    return kernel_call(
        functools.partial(first_kernel, step),
        (order, *cells, taps, conv_bias),
        [
            shape(rows // 2, 2 * hidden),
            shape(rows, channels),
            shape(cells[0].shape[0] - rows, channels),
        ],
        6 * rows * hidden * channels,
        3 * hidden * channels + 2 * rows * channels,
        rows * hidden,
        scalars=1,
    )


def fused_kernel(
    block, edge_ref, a0, a1, a2, a3, weight, trunk_in, pbias_ref, taps, bias_ref, act_ref, trunk
):
    pbias = pbias_ref[block : block + 1]
    project_all((a0, a1, a2, a3), weight, trunk_in, 0, pbias, trunk)
    rows = trunk.shape[0]
    margin = dilation(FRAMED_BLOCKS)

    @pl.when(edge_ref[0] == 1)
    def _():
        trunk[:margin] = jnp.zeros((margin, trunk.shape[1]), BF16)

    @pl.when(edge_ref[1] == 1)
    def _():
        trunk[rows - margin :] = jnp.zeros((margin, trunk.shape[1]), BF16)

    bias = bias_ref[block + 1 : block + 2]
    convolve(trunk[...], taps, bias, dilation(block + 1), act_ref)


def fused(acts, weight, trunk, pbias, taps, conv_bias, block, edge, rows_out):
    rows, channels = trunk.shape
    hidden = taps.shape[1]
    return kernel_call(
        functools.partial(fused_kernel, block),
        (edge, *acts, weight, trunk, pbias, taps, conv_bias),
        [shape(rows_out // 2, 2 * hidden), shape(rows, channels)],
        14 * rows * hidden * channels,
        7 * hidden * channels + 2 * rows * channels,
        rows * hidden,
        scalars=1,
    )


def projection_kernel(block, a0, a1, a2, a3, weight, trunk_in, pbias_ref, trunk):
    margin = (trunk_in.shape[0] - trunk.shape[0]) // 2
    pbias = pbias_ref[block : block + 1]
    project_all((a0, a1, a2, a3), weight, trunk_in, margin, pbias, trunk)


def projection(acts, weight, trunk, pbias, block):
    channels = trunk.shape[1]
    rows, hidden = 2 * acts[0].shape[0], acts[0].shape[1] // 2
    return kernel_call(
        functools.partial(projection_kernel, block),
        (*acts, weight, trunk, pbias),
        [shape(rows, channels)],
        8 * rows * hidden * channels,
        4 * hidden * channels + 2 * rows * channels,
    )[0]


def conv_kernel(block, above, trunk, below, taps, bias_ref, act_ref):
    cells = jnp.concatenate([above[...], trunk[...], below[...]], axis=0)
    convolve(cells, taps, bias_ref[block : block + 1], dilation(block), act_ref)


def conv(above, trunk, below, taps, conv_bias, block):
    rows, channels = trunk.shape
    hidden = taps.shape[1]
    frame = rows + 2 * dilation(block)
    return kernel_call(
        functools.partial(conv_kernel, block),
        (above, trunk, below, taps, conv_bias),
        [shape(rows // 2, 2 * hidden)],
        6 * frame * hidden * channels,
        3 * hidden * channels + frame * channels,
        rows * hidden,
    )[0]


def head_kernel(
    block, a0, a1, a2, a3, weight, trunk_in, pbias_ref, head_ref, hbias_ref, onehot_ref,
    cover_ref, gene_ref, trunk
):
    pbias = pbias_ref[block : block + 1]
    project_all((a0, a1, a2, a3), weight, trunk_in, 0, pbias, trunk)
    tracks = head_ref.shape[1]
    width = tile_of(tracks)
    for c in range(tracks // width):
        cols = columns(c, width)
        x = dot(trunk[...], head_ref[:, cols]) + hbias_ref[:, cols].astype(jnp.float32)
        tile = (jnp.maximum(x, 0.0) + jnp.log1p(jnp.exp(-jnp.abs(x)))).astype(BF16)
        cover_ref[:, cols] = tile
        gene_ref[:, cols] = dot(onehot_ref[...], tile).astype(BF16)


def head(acts, weight, trunk, pbias, block, head_weight, head_bias, onehot):
    rows, channels = trunk.shape
    hidden = acts[0].shape[1] // 2
    tracks = head_weight.shape[1]
    genes = onehot.shape[0]
    return kernel_call(
        functools.partial(head_kernel, block),
        (*acts, weight, trunk, pbias, head_weight, head_bias, onehot),
        [shape(rows, tracks), shape(genes, tracks)],
        8 * rows * hidden * channels + 2 * rows * channels * tracks,
        4 * hidden * channels + rows * channels + channels * tracks,
        2 * rows * tracks,
        scratch=[pltpu.VMEM((rows, channels), BF16)],
    )


def exon_digits(exon_bins, channels):
    digits = jnp.concatenate([exon_bins >> 7, exon_bins & (DIGIT - 1)], axis=1)
    genes, width = digits.shape
    return jnp.pad(digits.astype(jnp.bfloat16), ((0, -genes % 16), (0, channels - width)))


def exon_lists(rows, genes, entries):
    digits = rows[:, :genes, : 2 * entries].astype(jnp.int32)
    lists = digits[:, :, :entries] * DIGIT + digits[:, :, entries:]
    return lists.reshape(-1, entries)


def exon_onehot(gene_block, first_bin, width_now):
    exon_matches = (
        gene_block[:, :, None] - first_bin == jnp.arange(width_now, dtype=jnp.int32)[None, None, :]
    )
    return jnp.sum(exon_matches.astype(jnp.float32), axis=1).astype(jnp.bfloat16)


def shards(
    trunk_input, conv_in, conv_bias, conv_out, projection_bias, head_weight, head_bias, exon_bins
):
    quarters = lax.axis_size("trk")
    place = lax.axis_index("trk")
    count = lax.axis_size("seq")
    lane = lax.axis_index("seq")
    bin_rows, channels_here = trunk_input.shape
    blocks, hidden, channels = conv_out.shape
    genes_here, entries = exon_bins.shape

    load_rows = BLOCKS_PER_LOAD * hidden
    size = group_size(load_rows, count)
    share = load_rows // size
    per_block = hidden // share
    groups = [[g * size + i for i in range(size)] for g in range(count // size)]
    mine = lax.rem(lane, size)
    packed = size == count and 2 * entries <= channels

    def column(load):
        first = load * BLOCKS_PER_LOAD
        flat = conv_out[first : first + BLOCKS_PER_LOAD].reshape(load_rows, channels)
        return lax.dynamic_slice_in_dim(flat, mine * share, share, 0)

    def gather(parts):
        return lax.all_gather(
            jnp.concatenate(parts, axis=0), "seq", axis=0, tiled=False, axis_index_groups=groups
        )

    margin = dilation(FRAMED_BLOCKS)
    frame = bin_rows + 2 * margin
    order = lax.rem(place - jnp.arange(quarters, dtype=jnp.int32) + quarters, quarters)
    edge = jnp.stack([lane == 0, lane == count - 1]).astype(jnp.int32)

    above, below = halo(trunk_input, margin)
    first_column = from_others(column(0))
    loads = [gather(after_all(first_column, above, below))]
    own = jnp.concatenate(
        [above, trunk_input, below, jnp.pad(projection_bias, ((0, -blocks % 16), (0, 0)))], axis=0
    )
    own = after(own, *first_column)
    cells = from_others(own)
    second = from_others(after(column(1), *cells))

    taps_shape = shape(3, hidden, channels)
    weight_shape = shape(quarters * hidden, channels)
    (taps,) = stage((after(conv_in, own),), (taps_shape,), (functools.partial(tap_cuts, 0),))
    act, trunk, biases = first_conv(cells, frame, order, taps, conv_bias, dilation(0))

    onehot = None
    for block in range(RESIDUAL_BLOCKS):
        others = from_others(act)
        if block == 0:
            third = from_others(after(column(2), *others))
        if block == 1:
            loads.append(gather(after_all(second, act)))
        if block == 2:
            tail = [exon_digits(exon_bins, channels)] if packed else []
            loads.append(gather(after_all(third, act) + tail))
        if block == 4:
            if packed:
                gene_lists = exon_lists(loads[2][:, quarters * share :], genes_here, entries)
            else:
                gene_lists = lax.all_gather(exon_bins, "seq", axis=0, tiled=True)
            onehot = exon_onehot(gene_lists, lane * bin_rows, bin_rows)
        later = block + 1
        part = functools.partial(projection_cuts, block % BLOCKS_PER_LOAD, per_block, share)
        load = after(loads[block // BLOCKS_PER_LOAD], act)
        if later < RESIDUAL_BLOCKS:
            weight, taps = stage(
                (load, conv_in),
                (weight_shape, taps_shape),
                (part, functools.partial(tap_cuts, later)),
            )
        else:
            weight, head_rows = stage(
                (load, head_weight), (weight_shape, shape(*head_weight.shape)), (part, whole_cuts)
            )
        if later < FRAMED_BLOCKS:
            rows_out = frame if later < FRAMED_BLOCKS - 1 else bin_rows
            act, trunk = fused(
                others, weight, trunk, biases, taps, conv_bias, block, edge, rows_out
            )
        elif later < RESIDUAL_BLOCKS:
            trunk = projection(others, weight, trunk, biases, block)
            above, below = halo(trunk, dilation(later))
            act = conv(above, trunk, below, taps, conv_bias, later)
        else:
            coverage, partial = head(
                others, weight, trunk, biases, block, head_rows, head_bias[None, :], onehot
            )

    parts = lax.all_to_all(
        partial.reshape(count, genes_here, partial.shape[1]), "seq", 0, 0, tiled=False
    )
    gene_sum = jnp.sum(parts.astype(jnp.float32), axis=0)
    counts = jnp.sum((exon_bins >= 0).astype(jnp.float32), axis=1)
    gene_cov = gene_sum / counts[:, None]
    return (coverage, gene_cov)


def solution(mesh):
    in_specs = (
        P("seq", "trk"),
        P(None, None, "trk", None),
        P(None, "trk"),
        P(None, "trk", None),
        P(None, "trk"),
        P(None, "trk"),
        P("trk"),
        P("seq", None),
    )
    out_specs = (P("seq", "trk"), P("seq", "trk"))
    return jax.shard_map(shards, mesh=mesh, in_specs=in_specs, out_specs=out_specs, check_vma=False)
```

```python
import functools
import math

import jax
import jax.numpy as jnp
from jax import lax
from jax.experimental import pallas as pl
from jax.experimental.pallas import tpu as pltpu
from jax.sharding import PartitionSpec as P

RESIDUAL_BLOCKS = 6
BASE_DILATION = 2
BLOCKS_PER_LOAD = 2
FRAMED_BLOCKS = 4
DIGIT = 128
VMEM_BYTES = 20 * 2**20
STAGE_BYTES = 40 * 2**20


def dilation(block):
    return BASE_DILATION * 2**block


def after(cells, *earlier):
    return lax.optimization_barrier((cells,) + earlier)[0]


def after_all(cells, *earlier):
    return list(lax.optimization_barrier(tuple(cells) + earlier)[: len(cells)])


def from_others(cells):
    count = lax.axis_size("trk")
    return [cells] + [
        lax.ppermute(cells, "trk", [(i, (i + k) % count) for i in range(count)])
        for k in range(1, count)
    ]


def halo(cells, width):
    count = lax.axis_size("seq")
    head = cells[:width]
    tail = cells[cells.shape[0] - width :]
    above = lax.ppermute(tail, "seq", [(i, i + 1) for i in range(count - 1)])
    below = lax.ppermute(head, "seq", [(i + 1, i) for i in range(count - 1)])
    return above, below


def group_size(rows, count):
    size = 1
    for g in range(1, count + 1):
        if count % g == 0 and rows % (16 * g) == 0:
            size = g
    return size


def tile_of(channels):
    for width in (512, 256, 384, 128):
        if channels % width == 0:
            return width
    return channels


def dot(a, b):
    return jnp.dot(a, b, preferred_element_type=jnp.float32)


def dot_last(a, b):
    return lax.dot_general(a, b, (((1,), (1,)), ((), ())), preferred_element_type=jnp.float32)


def gelu(x):
    cubic = x + 0.044715 * (x * x * x)
    return 0.5 * x * (1.0 + jnp.tanh(math.sqrt(2.0 / math.pi) * cubic))


def pack(act):
    half = act.shape[0] // 2
    return jnp.concatenate([act[:half], act[half:]], axis=1)


def unpack(cells):
    half = cells.shape[1] // 2
    return jnp.concatenate([cells[:, :half], cells[:, half:]], axis=0)


def columns(tile, width):
    return pl.ds(tile * width, width)


def project_all(cells, weight, trunk, margin, bias, target):
    rows, channels = target.shape
    width = tile_of(channels)
    for c in range(channels // width):
        cols = columns(c, width)
        total = dot(cells, weight[:, cols]) + bias[:, cols].astype(jnp.float32)
        total = total + trunk[pl.ds(margin, rows), cols].astype(jnp.float32)
        target[:, cols] = total.astype(BF16)


def dilated(cells, taps, step):
    rows = cells.shape[0]
    sums = [dot_last(cells, taps[t]) for t in range(3)]
    return sums[1] + pltpu.roll(sums[0], step, 0) + pltpu.roll(sums[2], rows - step, 0)


def convolve(cells, taps, bias, step, act_ref):
    keep = 2 * act_ref.shape[0]
    margin = (cells.shape[0] - keep) // 2
    inner = dilated(cells, taps, step)[margin : margin + keep] + bias.astype(jnp.float32)
    act_ref[...] = pack(gelu(inner).astype(BF16))


BF16 = jnp.bfloat16
ANY = pl.BlockSpec(memory_space=pl.ANY)
SMEM = pl.BlockSpec(memory_space=pltpu.SMEM)
VMEM = pl.BlockSpec(memory_space=pltpu.VMEM)


def shape(*dims):
    return jax.ShapeDtypeStruct(dims, BF16)


def kernel_call(body, ins, outs, flops, moved, special=0, scalars=0, scratch=(), limit=VMEM_BYTES, specs=None):
    return pl.pallas_call(
        body,
        in_specs=specs or [SMEM] * scalars + [VMEM] * (len(ins) - scalars),
        out_specs=[VMEM] * len(outs),
        out_shape=list(outs),
        scratch_shapes=list(scratch),
        compiler_params=pltpu.CompilerParams(vmem_limit_bytes=limit),
        cost_estimate=pl.CostEstimate(
            flops=flops, bytes_accessed=2 * moved, transcendentals=special
        ),
    )(*ins)


def stage_kernel(plan, *refs):
    sems = refs[-1]
    used = 0
    copies = []
    for source, target, cuts in plan:
        for src, dst in cuts(refs[source], refs[target]):
            copies.append(pltpu.make_async_copy(src, dst, sems.at[used]))
            used += 1
    for copy in copies:
        copy.start()
    for copy in copies:
        copy.wait()


def projection_cuts(part, per_block, share, load, target):
    return [
        (
            load.at[part * per_block + i, pl.ds(j * share, share)],
            target.at[pl.ds((j * per_block + i) * share, share)],
        )
        for j in range(target.shape[0] // (per_block * share))
        for i in range(per_block)
    ]


def tap_cuts(block, conv_in, target):
    return [(conv_in.at[block, t], target.at[t]) for t in range(3)]


def whole_cuts(source, target):
    return [(source, target)]


def stage(sources, targets, cuts):
    count = len(sources)
    plan = [(i, count + i, cut) for i, cut in enumerate(cuts)]
    return kernel_call(
        functools.partial(stage_kernel, plan),
        sources,
        targets,
        0,
        sum(math.prod(t.shape) for t in targets),
        scratch=[pltpu.SemaphoreType.DMA((32,))],
        specs=[ANY] * count,
        limit=STAGE_BYTES,
    )


def join_kernel(*refs):
    parts, target, sems = refs[:-2], refs[-2], refs[-1]
    copies = []
    row = 0
    for k, part in enumerate(parts):
        rows = part.shape[0]
        copies.append(pltpu.make_async_copy(part, target.at[pl.ds(row, rows)], sems.at[k]))
        row += rows
    for copy in copies:
        copy.start()
    for copy in copies:
        copy.wait()


def join(parts):
    rows = sum(part.shape[0] for part in parts)
    return pl.pallas_call(
        join_kernel,
        in_specs=[ANY] * len(parts),
        out_specs=pl.BlockSpec(memory_space=pltpu.HBM),
        out_shape=shape(rows, parts[0].shape[1]),
        scratch_shapes=[pltpu.SemaphoreType.DMA((len(parts),))],
        compiler_params=pltpu.CompilerParams(vmem_limit_bytes=2**22),
        cost_estimate=pl.CostEstimate(
            flops=0, bytes_accessed=4 * rows * parts[0].shape[1], transcendentals=0
        ),
    )(*parts)


def first_kernel(step, order_ref, c0, c1, c2, c3, taps, bias_ref, act_ref, trunk, pbias):
    width = c0.shape[1]
    rows = trunk.shape[0]
    for k, cell in enumerate((c0, c1, c2, c3)):
        cols = pl.ds(pl.multiple_of(order_ref[k] * width, 128), width)
        trunk[:, cols] = cell[:rows]
        pbias[:, cols] = cell[rows:]
    convolve(trunk[...], taps, bias_ref[0:1], step, act_ref)


def first_conv(cells, rows, order, taps, conv_bias, step):
    _, hidden, channels = taps.shape
    return kernel_call(
        functools.partial(first_kernel, step),
        (order, *cells, taps, conv_bias),
        [
            shape(rows // 2, 2 * hidden),
            shape(rows, channels),
            shape(cells[0].shape[0] - rows, channels),
        ],
        6 * rows * hidden * channels,
        3 * hidden * channels + 2 * rows * channels,
        rows * hidden,
        scalars=1,
    )


def gather_acts(acts, edges=()):
    cells = []
    for j, act in enumerate(acts):
        parts = [unpack(act[...])]
        if edges:
            half = edges[j].shape[1] // 2
            parts = [edges[j][:, :half]] + parts + [edges[j][:, half:]]
        cells.append(jnp.concatenate(parts, axis=0))
    return jnp.concatenate(cells, axis=1)


def close_window(edge_ref, trunk, margin):
    rows, channels = trunk.shape

    @pl.when(edge_ref[0] == 1)
    def _():
        trunk[:margin] = jnp.zeros((margin, channels), BF16)

    @pl.when(edge_ref[1] == 1)
    def _():
        trunk[rows - margin :] = jnp.zeros((margin, channels), BF16)


def fused_kernel(
    block, margin, edge_ref, a0, a1, a2, a3, weight, trunk_in, pbias_ref, taps, bias_ref, act_ref,
    trunk
):
    pbias = pbias_ref[block : block + 1]
    project_all(gather_acts((a0, a1, a2, a3)), weight, trunk_in, 0, pbias, trunk)
    close_window(edge_ref, trunk, margin)
    bias = bias_ref[block + 1 : block + 2]
    convolve(trunk[...], taps, bias, dilation(block + 1), act_ref)


def fused(acts, weight, trunk, pbias, taps, conv_bias, block, edge, rows_out, margin):
    rows, channels = trunk.shape
    hidden = taps.shape[1]
    return kernel_call(
        functools.partial(fused_kernel, block, margin),
        (edge, *acts, weight, trunk, pbias, taps, conv_bias),
        [shape(rows_out // 2, 2 * hidden), shape(rows, channels)],
        14 * rows * hidden * channels,
        7 * hidden * channels + 2 * rows * channels,
        rows * hidden,
        scalars=1,
    )


def edged_kernel(
    block, margin, edge_ref, a0, a1, a2, a3, e0, e1, e2, e3, weight, above, trunk_in, below,
    pbias_ref, taps, bias_ref, act_ref, trunk, frame
):
    rows = trunk_in.shape[0]
    frame[:margin] = above[above.shape[0] - margin :]
    frame[margin : margin + rows] = trunk_in[...]
    frame[margin + rows :] = below[:margin]
    pbias = pbias_ref[block : block + 1]
    cells = gather_acts((a0, a1, a2, a3), (e0, e1, e2, e3))
    project_all(cells, weight, frame, 0, pbias, trunk)
    close_window(edge_ref, trunk, margin)
    bias = bias_ref[block + 1 : block + 2]
    convolve(trunk[...], taps, bias, dilation(block + 1), act_ref)


def edged(acts, edges, weight, above, trunk, below, pbias, taps, conv_bias, block, edge):
    rows, channels = trunk.shape
    hidden = taps.shape[1]
    margin = dilation(block + 1)
    frame = rows + 2 * margin
    return kernel_call(
        functools.partial(edged_kernel, block, margin),
        (edge, *acts, *edges, weight, above, trunk, below, pbias, taps, conv_bias),
        [shape(rows // 2, 2 * hidden), shape(frame, channels)],
        14 * frame * hidden * channels,
        7 * hidden * channels + 2 * frame * channels,
        rows * hidden,
        scalars=1,
        scratch=[pltpu.VMEM((frame, channels), BF16)],
    )


def projection_kernel(block, a0, a1, a2, a3, weight, trunk_in, pbias_ref, trunk):
    margin = (trunk_in.shape[0] - trunk.shape[0]) // 2
    pbias = pbias_ref[block : block + 1]
    project_all(gather_acts((a0, a1, a2, a3)), weight, trunk_in, margin, pbias, trunk)


def projection(acts, weight, trunk, pbias, block):
    channels = trunk.shape[1]
    rows, hidden = 2 * acts[0].shape[0], acts[0].shape[1] // 2
    return kernel_call(
        functools.partial(projection_kernel, block),
        (*acts, weight, trunk, pbias),
        [shape(rows, channels)],
        8 * rows * hidden * channels,
        4 * hidden * channels + 2 * rows * channels,
    )[0]


def center_kernel(block, trunk, taps, bias_ref, act_ref):
    convolve(trunk[...], taps, bias_ref[block : block + 1], dilation(block), act_ref)


def center_conv(trunk, taps, conv_bias, block):
    rows, channels = trunk.shape
    hidden = taps.shape[1]
    return kernel_call(
        functools.partial(center_kernel, block),
        (trunk, taps, conv_bias),
        [shape((rows - 2 * dilation(block)) // 2, 2 * hidden)],
        6 * rows * hidden * channels,
        3 * hidden * channels + rows * channels,
        rows * hidden,
    )[0]


def edge_kernel(block, above, trunk, below, taps, bias_ref, act_ref):
    step = dilation(block)
    rows = trunk.shape[0]
    keep = act_ref.shape[0]
    part = keep + 2 * step
    inner_rows = part - above.shape[0]
    cells = jnp.concatenate(
        [above[...], trunk[:inner_rows], trunk[rows - inner_rows :], below[...]], axis=0
    )
    inner = dilated(cells, taps, step) + bias_ref[block : block + 1].astype(jnp.float32)
    top = inner[step : step + keep]
    bottom = inner[part + step : part + step + keep]
    act_ref[...] = jnp.concatenate([gelu(top).astype(BF16), gelu(bottom).astype(BF16)], axis=1)


def edge_conv(above, trunk, below, taps, conv_bias, block):
    channels = trunk.shape[1]
    hidden = taps.shape[1]
    step = dilation(block)
    keep = above.shape[0]
    rows = 2 * (keep + 2 * step)
    return kernel_call(
        functools.partial(edge_kernel, block),
        (above, trunk, below, taps, conv_bias),
        [shape(keep, 2 * hidden)],
        6 * rows * hidden * channels,
        3 * hidden * channels + rows * channels,
        rows * hidden,
    )[0]


def head_kernel(
    block, a0, a1, a2, a3, weight, trunk_in, pbias_ref, head_ref, hbias_ref, onehot_ref,
    cover_ref, gene_ref, trunk
):
    pbias = pbias_ref[block : block + 1]
    margin = (trunk_in.shape[0] - trunk.shape[0]) // 2
    project_all(gather_acts((a0, a1, a2, a3)), weight, trunk_in, margin, pbias, trunk)
    tracks = head_ref.shape[1]
    width = tile_of(tracks)
    for c in range(tracks // width):
        cols = columns(c, width)
        x = dot(trunk[...], head_ref[:, cols]) + hbias_ref[:, cols].astype(jnp.float32)
        tile = (jnp.maximum(x, 0.0) + jnp.log1p(jnp.exp(-jnp.abs(x)))).astype(BF16)
        cover_ref[:, cols] = tile
        gene_ref[:, cols] = dot(onehot_ref[...], tile).astype(BF16)


def head(acts, weight, trunk, pbias, block, head_weight, head_bias, onehot):
    channels = trunk.shape[1]
    rows, hidden = 2 * acts[0].shape[0], acts[0].shape[1] // 2
    tracks = head_weight.shape[1]
    genes = onehot.shape[0]
    return kernel_call(
        functools.partial(head_kernel, block),
        (*acts, weight, trunk, pbias, head_weight, head_bias, onehot),
        [shape(rows, tracks), shape(genes, tracks)],
        8 * rows * hidden * channels + 2 * rows * channels * tracks,
        4 * hidden * channels + rows * channels + channels * tracks,
        2 * rows * tracks,
        scratch=[pltpu.VMEM((rows, channels), BF16)],
    )


def exon_digits(exon_bins, channels):
    digits = jnp.concatenate([exon_bins >> 7, exon_bins & (DIGIT - 1)], axis=1)
    genes, width = digits.shape
    return jnp.pad(digits.astype(jnp.bfloat16), ((0, -genes % 16), (0, channels - width)))


def exon_lists(rows, genes, entries):
    digits = rows[:, :genes, : 2 * entries].astype(jnp.int32)
    lists = digits[:, :, :entries] * DIGIT + digits[:, :, entries:]
    return lists.reshape(-1, entries)


def exon_onehot(gene_block, first_bin, width_now):
    exon_matches = (
        gene_block[:, :, None] - first_bin == jnp.arange(width_now, dtype=jnp.int32)[None, None, :]
    )
    return jnp.sum(exon_matches.astype(jnp.float32), axis=1).astype(jnp.bfloat16)


def shards(
    trunk_input, conv_in, conv_bias, conv_out, projection_bias, head_weight, head_bias, exon_bins
):
    quarters = lax.axis_size("trk")
    place = lax.axis_index("trk")
    count = lax.axis_size("seq")
    lane = lax.axis_index("seq")
    bin_rows, channels_here = trunk_input.shape
    blocks, hidden, channels = conv_out.shape
    genes_here, entries = exon_bins.shape

    load_rows = BLOCKS_PER_LOAD * hidden
    size = group_size(load_rows, count)
    share = load_rows // size
    per_block = hidden // share
    groups = [[g * size + i for i in range(size)] for g in range(count // size)]
    mine = lax.rem(lane, size)
    packed = size == count and 2 * entries <= channels

    flat = conv_out.reshape(blocks * hidden, channels)

    def column(load):
        return lax.dynamic_slice_in_dim(flat, load * load_rows + mine * share, share, 0)

    def gather(parts):
        return lax.all_gather(
            join(parts), "seq", axis=0, tiled=False, axis_index_groups=groups
        )

    margin = dilation(FRAMED_BLOCKS)
    frame = bin_rows + 2 * margin
    order = lax.rem(place - jnp.arange(quarters, dtype=jnp.int32) + quarters, quarters)
    edge = jnp.stack([lane == 0, lane == count - 1]).astype(jnp.int32)

    above, below = halo(trunk_input, margin)
    first = from_others(column(0))
    loads = [gather(after_all(first, above, below))]
    own = jnp.concatenate(
        [above, trunk_input, below, jnp.pad(projection_bias, ((0, -blocks % 16), (0, 0)))], axis=0
    )
    own = after(own, *first)
    cells = from_others(own)
    second = from_others(after(column(1), *cells))

    taps_shape = shape(3, hidden, channels)
    weight_shape = shape(quarters * hidden, channels)
    (taps,) = stage((after(conv_in, own),), (taps_shape,), (functools.partial(tap_cuts, 0),))
    act, trunk, biases = first_conv(cells, frame, order, taps, conv_bias, dilation(0))

    def staged(block, extra, extra_shape, extra_cut, token):
        part = functools.partial(projection_cuts, block % BLOCKS_PER_LOAD, per_block, share)
        load = after(loads[block // BLOCKS_PER_LOAD], token)
        return stage((load, extra), (weight_shape, extra_shape), (part, extra_cut))

    for block in range(FRAMED_BLOCKS):
        later = block + 1
        others = from_others(act)
        if block == 0:
            third = from_others(after(column(2), *others))
        if block == 1:
            loads.append(gather(after_all(second, act)))
        if block == 2:
            tail = [exon_digits(exon_bins, channels)] if packed else []
            loads.append(gather(after_all(third, act) + tail))
        weight, taps = staged(
            block, conv_in, taps_shape, functools.partial(tap_cuts, later), act
        )
        if later < FRAMED_BLOCKS:
            rows_out = frame if later < FRAMED_BLOCKS - 1 else bin_rows
            act, trunk = fused(
                others, weight, trunk, biases, taps, conv_bias, block, edge, rows_out, margin
            )
        else:
            trunk = projection(others, weight, trunk, biases, block)

    block = FRAMED_BLOCKS
    later = block + 1
    act = center_conv(trunk, taps, conv_bias, block)
    others = from_others(act)
    above, below = halo(trunk, dilation(block) + dilation(later))
    edges = from_others(edge_conv(above, trunk, below, taps, conv_bias, block))
    weight, taps = staged(block, conv_in, taps_shape, functools.partial(tap_cuts, later), act)
    act, trunk = edged(
        others, edges, weight, above, trunk, below, biases, taps, conv_bias, block, edge
    )

    others = from_others(act)
    weight, head_rows = staged(
        later, head_weight, shape(*head_weight.shape), whole_cuts, act
    )
    if packed:
        gene_lists = exon_lists(loads[2][:, quarters * share :], genes_here, entries)
    else:
        gene_lists = lax.all_gather(exon_bins, "seq", axis=0, tiled=True)
    onehot = exon_onehot(gene_lists, lane * bin_rows, bin_rows)
    coverage, partial = head(
        others, weight, trunk, biases, later, head_rows, head_bias[None, :], onehot
    )

    parts = lax.all_to_all(
        partial.reshape(count, genes_here, partial.shape[1]), "seq", 0, 0, tiled=False
    )
    gene_sum = jnp.sum(parts.astype(jnp.float32), axis=0)
    counts = jnp.sum((exon_bins >= 0).astype(jnp.float32), axis=1)
    gene_cov = gene_sum / counts[:, None]
    return (coverage, gene_cov)


def solution(mesh):
    in_specs = (
        P("seq", "trk"),
        P(None, None, "trk", None),
        P(None, "trk"),
        P(None, "trk", None),
        P(None, "trk"),
        P(None, "trk"),
        P("trk"),
        P("seq", None),
    )
    out_specs = (P("seq", "trk"), P("seq", "trk"))
    return jax.shard_map(shards, mesh=mesh, in_specs=in_specs, out_specs=out_specs, check_vma=False)
```

```python
import functools
import math

import jax
import jax.numpy as jnp
from jax import lax
from jax.experimental import pallas as pl
from jax.experimental.pallas import tpu as pltpu
from jax.sharding import PartitionSpec as P

RESIDUAL_BLOCKS = 6
BASE_DILATION = 2
BLOCKS_PER_LOAD = 2
FRAMED_BLOCKS = 4
DIGIT = 128
VMEM_BYTES = 20 * 2**20
STAGE_BYTES = 40 * 2**20


def dilation(block):
    return BASE_DILATION * 2**block


def after(cells, *earlier):
    return lax.optimization_barrier((cells,) + earlier)[0]


def after_all(cells, *earlier):
    return list(lax.optimization_barrier(tuple(cells) + earlier)[: len(cells)])


def from_others(cells):
    count = lax.axis_size("trk")
    return [cells] + [
        lax.ppermute(cells, "trk", [(i, (i + k) % count) for i in range(count)])
        for k in range(1, count)
    ]


def relayed(cells):
    count = lax.axis_size("trk")
    last = count - 1
    across = lax.ppermute(cells, "trk", [(i, (i + 2) % count) for i in range(count)])
    up = lax.ppermute(cells, "trk", [(i, i + 1) for i in range(last)])
    down = lax.ppermute(cells, "trk", [(i + 1, i) for i in range(last)])
    far = lax.ppermute(across, "trk", [(last - 1, last), (1, 0)])
    return [cells, up, across, down, far]


def halo(cells, width):
    count = lax.axis_size("seq")
    head = cells[:width]
    tail = cells[cells.shape[0] - width :]
    above = lax.ppermute(tail, "seq", [(i, i + 1) for i in range(count - 1)])
    below = lax.ppermute(head, "seq", [(i + 1, i) for i in range(count - 1)])
    return above, below


def group_size(rows, count):
    size = 1
    for g in range(1, count + 1):
        if count % g == 0 and rows % (16 * g) == 0:
            size = g
    return size


def tile_of(channels):
    for width in (512, 256, 384, 128):
        if channels % width == 0:
            return width
    return channels


def dot(a, b):
    return jnp.dot(a, b, preferred_element_type=jnp.float32)


def dot_last(a, b):
    return lax.dot_general(a, b, (((1,), (1,)), ((), ())), preferred_element_type=jnp.float32)


def gelu(x):
    cubic = x + 0.044715 * (x * x * x)
    return 0.5 * x * (1.0 + jnp.tanh(math.sqrt(2.0 / math.pi) * cubic))


def pack(act):
    half = act.shape[0] // 2
    return jnp.concatenate([act[:half], act[half:]], axis=1)


def unpack(cells):
    half = cells.shape[1] // 2
    return jnp.concatenate([cells[:, :half], cells[:, half:]], axis=0)


def columns(tile, width):
    return pl.ds(tile * width, width)


def project_all(cells, weight, trunk, margin, bias, target):
    rows, channels = target.shape
    width = tile_of(channels)
    for c in range(channels // width):
        cols = columns(c, width)
        total = dot(cells, weight[:, :, :, cols].reshape(-1, width)) + bias[:, cols].astype(jnp.float32)
        total = total + trunk[pl.ds(margin, rows), cols].astype(jnp.float32)
        target[:, cols] = total.astype(BF16)


def dilated(cells, taps, step):
    rows = cells.shape[0]
    sums = [dot_last(cells, taps[t]) for t in range(3)]
    return sums[1] + pltpu.roll(sums[0], step, 0) + pltpu.roll(sums[2], rows - step, 0)


def convolve(cells, taps, bias, step, act_ref):
    keep = 2 * act_ref.shape[0]
    margin = (cells.shape[0] - keep) // 2
    inner = dilated(cells, taps, step)[margin : margin + keep] + bias.astype(jnp.float32)
    act_ref[...] = pack(gelu(inner).astype(BF16))


BF16 = jnp.bfloat16
ANY = pl.BlockSpec(memory_space=pl.ANY)
SMEM = pl.BlockSpec(memory_space=pltpu.SMEM)
VMEM = pl.BlockSpec(memory_space=pltpu.VMEM)


def shape(*dims):
    return jax.ShapeDtypeStruct(dims, BF16)


def kernel_call(body, ins, outs, flops, moved, special=0, scalars=0, scratch=(), limit=VMEM_BYTES, specs=None):
    return pl.pallas_call(
        body,
        in_specs=specs or [SMEM] * scalars + [VMEM] * (len(ins) - scalars),
        out_specs=[VMEM] * len(outs),
        out_shape=list(outs),
        scratch_shapes=list(scratch),
        compiler_params=pltpu.CompilerParams(vmem_limit_bytes=limit),
        cost_estimate=pl.CostEstimate(
            flops=flops, bytes_accessed=2 * moved, transcendentals=special
        ),
    )(*ins)


def stage_kernel(plan, order_ref, *refs):
    sems = refs[-1]
    used = 0
    copies = []
    for source, target, cuts in plan:
        if cuts.func is direct_cuts:
            cuts = functools.partial(cuts, order_ref)
        for src, dst in cuts(refs[source], refs[target]):
            copies.append(pltpu.make_async_copy(src, dst, sems.at[used]))
            used += 1
    for copy in copies:
        copy.start()
    for copy in copies:
        copy.wait()


def projection_cuts(part, per_block, share, load, target):
    return [
        (load.at[pl.ds(part * per_block, per_block), pl.ds(j * share, share)], target.at[j])
        for j in range(target.shape[0])
    ]


def direct_cuts(part, per_block, order_ref, load, target):
    return [
        (load.at[order_ref[j], pl.ds(part * per_block, per_block)], target.at[j])
        for j in range(target.shape[0])
    ]


def tap_cuts(block, conv_in, target):
    return [(conv_in.at[block, t], target.at[t]) for t in range(3)]


def whole_cuts(_, source, target):
    return [(source, target)]


def stage(order, sources, targets, cuts):
    count = len(sources)
    plan = [(i, count + i, cut) for i, cut in enumerate(cuts)]
    return kernel_call(
        functools.partial(stage_kernel, plan),
        (order, *sources),
        targets,
        0,
        sum(math.prod(t.shape) for t in targets),
        scratch=[pltpu.SemaphoreType.DMA((32,))],
        specs=[SMEM] + [ANY] * count,
        limit=STAGE_BYTES,
    )


def join_kernel(*refs):
    parts, target, sems = refs[:-2], refs[-2], refs[-1]
    copies = []
    row = 0
    for k, part in enumerate(parts):
        rows = part.shape[0]
        copies.append(pltpu.make_async_copy(part, target.at[pl.ds(row, rows)], sems.at[k]))
        row += rows
    for copy in copies:
        copy.start()
    for copy in copies:
        copy.wait()


def join(parts):
    rows = sum(part.shape[0] for part in parts)
    return pl.pallas_call(
        join_kernel,
        in_specs=[ANY] * len(parts),
        out_specs=pl.BlockSpec(memory_space=pltpu.HBM),
        out_shape=shape(rows, parts[0].shape[1]),
        scratch_shapes=[pltpu.SemaphoreType.DMA((len(parts),))],
        compiler_params=pltpu.CompilerParams(vmem_limit_bytes=2**22),
        cost_estimate=pl.CostEstimate(
            flops=0, bytes_accessed=4 * rows * parts[0].shape[1], transcendentals=0
        ),
    )(*parts)


def first_kernel(step, owner_ref, c0, c1, c2, c3, c4, taps, bias_ref, act_ref, trunk, pbias):
    width = c0.shape[1]
    rows = trunk.shape[0]
    for k, cell in enumerate((c0, c1, c2, c3, c4)):

        @pl.when(owner_ref[k] >= 0)
        def _():
            cols = pl.ds(pl.multiple_of(owner_ref[k] * width, 128), width)
            trunk[:, cols] = cell[:rows]
            pbias[:, cols] = cell[rows:]

    convolve(trunk[...], taps, bias_ref[0:1], step, act_ref)


def first_conv(cells, rows, order, taps, conv_bias, step):
    _, hidden, channels = taps.shape
    return kernel_call(
        functools.partial(first_kernel, step),
        (order, *cells, taps, conv_bias),
        [
            shape(rows // 2, 2 * hidden),
            shape(rows, channels),
            shape(cells[0].shape[0] - rows, channels),
        ],
        6 * rows * hidden * channels,
        3 * hidden * channels + 2 * rows * channels,
        rows * hidden,
        scalars=1,
    )


def gather_acts(acts, edges=()):
    cells = []
    for j, act in enumerate(acts):
        parts = [unpack(act[...])]
        if edges:
            half = edges[j].shape[1] // 2
            parts = [edges[j][:, :half]] + parts + [edges[j][:, half:]]
        cells.append(jnp.concatenate(parts, axis=0))
    return jnp.concatenate(cells, axis=1)


def close_window(edge_ref, trunk, margin):
    rows, channels = trunk.shape

    @pl.when(edge_ref[0] == 1)
    def _():
        trunk[:margin] = jnp.zeros((margin, channels), BF16)

    @pl.when(edge_ref[1] == 1)
    def _():
        trunk[rows - margin :] = jnp.zeros((margin, channels), BF16)


def fused_kernel(
    block, margin, edge_ref, a0, a1, a2, a3, weight, trunk_in, pbias_ref, taps, bias_ref, act_ref,
    trunk
):
    pbias = pbias_ref[block : block + 1]
    skip = (trunk_in.shape[0] - trunk.shape[0]) // 2
    project_all(gather_acts((a0, a1, a2, a3)), weight, trunk_in, skip, pbias, trunk)
    close_window(edge_ref, trunk, margin - skip)
    bias = bias_ref[block + 1 : block + 2]
    convolve(trunk[...], taps, bias, dilation(block + 1), act_ref)


def fused(acts, weight, trunk, pbias, taps, conv_bias, block, edge, rows_out):
    channels = trunk.shape[1]
    rows = 2 * acts[0].shape[0]
    margin = dilation(FRAMED_BLOCKS)
    hidden = taps.shape[1]
    return kernel_call(
        functools.partial(fused_kernel, block, margin),
        (edge, *acts, weight, trunk, pbias, taps, conv_bias),
        [shape(rows_out // 2, 2 * hidden), shape(rows, channels)],
        14 * rows * hidden * channels,
        7 * hidden * channels + 2 * rows * channels,
        rows * hidden,
        scalars=1,
    )


def edged_kernel(
    block, margin, edge_ref, a0, a1, a2, a3, e0, e1, e2, e3, weight, above, trunk_in, below,
    pbias_ref, taps, bias_ref, act_ref, trunk, frame
):
    rows = trunk_in.shape[0]
    frame[:margin] = above[above.shape[0] - margin :]
    frame[margin : margin + rows] = trunk_in[...]
    frame[margin + rows :] = below[:margin]
    pbias = pbias_ref[block : block + 1]
    cells = gather_acts((a0, a1, a2, a3), (e0, e1, e2, e3))
    project_all(cells, weight, frame, 0, pbias, trunk)
    close_window(edge_ref, trunk, margin)
    bias = bias_ref[block + 1 : block + 2]
    convolve(trunk[...], taps, bias, dilation(block + 1), act_ref)


def edged(acts, edges, weight, above, trunk, below, pbias, taps, conv_bias, block, edge):
    rows, channels = trunk.shape
    hidden = taps.shape[1]
    margin = dilation(block + 1)
    frame = rows + 2 * margin
    return kernel_call(
        functools.partial(edged_kernel, block, margin),
        (edge, *acts, *edges, weight, above, trunk, below, pbias, taps, conv_bias),
        [shape(rows // 2, 2 * hidden), shape(frame, channels)],
        14 * frame * hidden * channels,
        7 * hidden * channels + 2 * frame * channels,
        rows * hidden,
        scalars=1,
        scratch=[pltpu.VMEM((frame, channels), BF16)],
    )


def projection_kernel(block, a0, a1, a2, a3, weight, trunk_in, pbias_ref, trunk):
    margin = (trunk_in.shape[0] - trunk.shape[0]) // 2
    pbias = pbias_ref[block : block + 1]
    project_all(gather_acts((a0, a1, a2, a3)), weight, trunk_in, margin, pbias, trunk)


def projection(acts, weight, trunk, pbias, block):
    channels = trunk.shape[1]
    rows, hidden = 2 * acts[0].shape[0], acts[0].shape[1] // 2
    return kernel_call(
        functools.partial(projection_kernel, block),
        (*acts, weight, trunk, pbias),
        [shape(rows, channels)],
        8 * rows * hidden * channels,
        4 * hidden * channels + 2 * rows * channels,
    )[0]


def center_kernel(block, trunk, taps, bias_ref, act_ref):
    convolve(trunk[...], taps, bias_ref[block : block + 1], dilation(block), act_ref)


def center_conv(trunk, taps, conv_bias, block):
    rows, channels = trunk.shape
    hidden = taps.shape[1]
    return kernel_call(
        functools.partial(center_kernel, block),
        (trunk, taps, conv_bias),
        [shape((rows - 2 * dilation(block)) // 2, 2 * hidden)],
        6 * rows * hidden * channels,
        3 * hidden * channels + rows * channels,
        rows * hidden,
    )[0]


def edge_kernel(block, above, trunk, below, taps, bias_ref, act_ref):
    step = dilation(block)
    rows = trunk.shape[0]
    keep = act_ref.shape[0]
    part = keep + 2 * step
    inner_rows = part - above.shape[0]
    cells = jnp.concatenate(
        [above[...], trunk[:inner_rows], trunk[rows - inner_rows :], below[...]], axis=0
    )
    inner = dilated(cells, taps, step) + bias_ref[block : block + 1].astype(jnp.float32)
    top = inner[step : step + keep]
    bottom = inner[part + step : part + step + keep]
    act_ref[...] = jnp.concatenate([gelu(top).astype(BF16), gelu(bottom).astype(BF16)], axis=1)


def edge_conv(above, trunk, below, taps, conv_bias, block):
    channels = trunk.shape[1]
    hidden = taps.shape[1]
    step = dilation(block)
    keep = above.shape[0]
    rows = 2 * (keep + 2 * step)
    return kernel_call(
        functools.partial(edge_kernel, block),
        (above, trunk, below, taps, conv_bias),
        [shape(keep, 2 * hidden)],
        6 * rows * hidden * channels,
        3 * hidden * channels + rows * channels,
        rows * hidden,
    )[0]


def head_kernel(
    block, a0, a1, a2, a3, weight, trunk_in, pbias_ref, head_ref, hbias_ref, onehot_ref,
    cover_ref, gene_ref, trunk
):
    pbias = pbias_ref[block : block + 1]
    margin = (trunk_in.shape[0] - trunk.shape[0]) // 2
    project_all(gather_acts((a0, a1, a2, a3)), weight, trunk_in, margin, pbias, trunk)
    tracks = head_ref.shape[1]
    width = tile_of(tracks)
    for c in range(tracks // width):
        cols = columns(c, width)
        x = dot(trunk[...], head_ref[:, cols]) + hbias_ref[:, cols].astype(jnp.float32)
        tile = (jnp.maximum(x, 0.0) + jnp.log1p(jnp.exp(-jnp.abs(x)))).astype(BF16)
        cover_ref[:, cols] = tile
        gene_ref[:, cols] = dot(onehot_ref[...], tile).astype(BF16)


def head(acts, weight, trunk, pbias, block, head_weight, head_bias, onehot):
    channels = trunk.shape[1]
    rows, hidden = 2 * acts[0].shape[0], acts[0].shape[1] // 2
    tracks = head_weight.shape[1]
    genes = onehot.shape[0]
    return kernel_call(
        functools.partial(head_kernel, block),
        (*acts, weight, trunk, pbias, head_weight, head_bias, onehot),
        [shape(rows, tracks), shape(genes, tracks)],
        8 * rows * hidden * channels + 2 * rows * channels * tracks,
        4 * hidden * channels + rows * channels + channels * tracks,
        2 * rows * tracks,
        scratch=[pltpu.VMEM((rows, channels), BF16)],
    )


def exon_digits(exon_bins, channels):
    digits = jnp.concatenate([exon_bins >> 7, exon_bins & (DIGIT - 1)], axis=1)
    genes, width = digits.shape
    return jnp.pad(digits.astype(jnp.bfloat16), ((0, -genes % 16), (0, channels - width)))


def exon_lists(rows, genes, entries):
    digits = rows[:, :genes, : 2 * entries].astype(jnp.int32)
    lists = digits[:, :, :entries] * DIGIT + digits[:, :, entries:]
    return lists.reshape(-1, entries)


def exon_onehot(gene_block, first_bin, width_now):
    exon_matches = (
        gene_block[:, :, None] - first_bin == jnp.arange(width_now, dtype=jnp.int32)[None, None, :]
    )
    return jnp.sum(exon_matches.astype(jnp.float32), axis=1).astype(jnp.bfloat16)


def shards(
    trunk_input, conv_in, conv_bias, conv_out, projection_bias, head_weight, head_bias, exon_bins
):
    quarters = lax.axis_size("trk")
    place = lax.axis_index("trk")
    count = lax.axis_size("seq")
    lane = lax.axis_index("seq")
    bin_rows, channels_here = trunk_input.shape
    blocks, hidden, channels = conv_out.shape
    genes_here, entries = exon_bins.shape

    load_rows = BLOCKS_PER_LOAD * hidden
    size = group_size(load_rows, count)
    share = load_rows // size
    per_block = hidden // share
    groups = [[g * size + i for i in range(size)] for g in range(count // size)]
    mine = lax.rem(lane, size)
    packed = size == count and 2 * entries <= channels

    flat = conv_out.reshape(blocks * hidden, channels)

    def column(load):
        return lax.dynamic_slice_in_dim(flat, load * load_rows + mine * share, share, 0)

    def gather(parts):
        return lax.all_gather(
            join(parts), "seq", axis=0, tiled=False, axis_index_groups=groups
        )

    margin = dilation(FRAMED_BLOCKS)
    frame = bin_rows + 2 * margin
    order = lax.rem(place - jnp.arange(quarters, dtype=jnp.int32) + quarters, quarters)
    last_place = quarters - 1
    owners = jnp.stack(
        [
            place,
            place - 1,
            lax.rem(place + 2, quarters),
            jnp.where(place == last_place, -1, place + 1),
            jnp.where((place == 0) | (place == last_place), last_place - place, -1),
        ]
    ).astype(jnp.int32)
    edge = jnp.stack([lane == 0, lane == count - 1]).astype(jnp.int32)

    above, below = halo(trunk_input, margin)
    first = from_others(column(0))
    loads = [gather(after_all(first, above, below))]
    own = jnp.concatenate(
        [above, trunk_input, below, jnp.pad(projection_bias, ((0, -blocks % 16), (0, 0)))], axis=0
    )
    own = after(own, first[1])
    cells = relayed(own)
    exon_rows = [exon_digits(exon_bins, channels)] if packed else []
    exon_rows = [exon_digits(exon_bins, channels)] if packed else []
    second = from_others(after(column(1), cells[2]))
    taps_shape = shape(3, hidden, channels)
    weight_shape = shape(quarters, per_block, share, channels)
    (taps,) = stage(order, (after(conv_in, own),), (taps_shape,), (functools.partial(tap_cuts, 0),))
    act, trunk, biases = first_conv(cells, frame, owners, taps, conv_bias, dilation(0))

    def staged(block, extra, extra_shape, extra_cut, token):
        place = block // BLOCKS_PER_LOAD
        part = block % BLOCKS_PER_LOAD
        cut = functools.partial(projection_cuts, part, per_block, share)
        load = after(loads[place], token)
        return stage(order, (load, extra), (weight_shape, extra_shape), (cut, extra_cut))

    for block in range(FRAMED_BLOCKS):
        later = block + 1
        others = from_others(act)
        if block == 0:
            loads.append(gather(after_all(second, act) + exon_rows))
        if block == 2:
            loads.append(gather(after_all(third, act)))
        weight, taps = staged(
            block, conv_in, taps_shape, functools.partial(tap_cuts, later), act
        )
        if block == 1:
            third = from_others(after(column(2), weight))
        if later < FRAMED_BLOCKS:
            reach = sum(dilation(b) for b in range(later + 1, FRAMED_BLOCKS))
            rows_out = bin_rows + 2 * (-(-reach // 16) * 16)
            act, trunk = fused(
                others, weight, trunk, biases, taps, conv_bias, block, edge, rows_out
            )
        else:
            trunk = projection(others, weight, trunk, biases, block)

    block = FRAMED_BLOCKS
    later = block + 1
    act = center_conv(trunk, taps, conv_bias, block)
    others = from_others(act)
    above, below = halo(trunk, dilation(block) + dilation(later))
    edges = from_others(edge_conv(above, trunk, below, taps, conv_bias, block))
    weight, taps = staged(block, conv_in, taps_shape, functools.partial(tap_cuts, later), act)
    act, trunk = edged(
        others, edges, weight, above, trunk, below, biases, taps, conv_bias, block, edge
    )

    others = from_others(act)
    weight, head_rows = staged(
        later, head_weight, shape(*head_weight.shape), functools.partial(whole_cuts, 0), act
    )
    if packed:
        gene_lists = exon_lists(loads[1][:, quarters * share :], genes_here, entries)
    else:
        gene_lists = lax.all_gather(exon_bins, "seq", axis=0, tiled=True)
    onehot = exon_onehot(gene_lists, lane * bin_rows, bin_rows)
    coverage, partial = head(
        others, weight, trunk, biases, later, head_rows, head_bias[None, :], onehot
    )

    parts = lax.all_to_all(
        partial.reshape(count, genes_here, partial.shape[1]), "seq", 0, 0, tiled=False
    )
    gene_sum = jnp.sum(parts.astype(jnp.float32), axis=0)
    counts = jnp.sum((exon_bins >= 0).astype(jnp.float32), axis=1)
    gene_cov = gene_sum / counts[:, None]
    return (coverage, gene_cov)


def solution(mesh):
    in_specs = (
        P("seq", "trk"),
        P(None, None, "trk", None),
        P(None, "trk"),
        P(None, "trk", None),
        P(None, "trk"),
        P(None, "trk"),
        P("trk"),
        P("seq", None),
    )
    out_specs = (P("seq", "trk"), P("seq", "trk"))
    return jax.shard_map(shards, mesh=mesh, in_specs=in_specs, out_specs=out_specs, check_vma=False)
```

```python
import functools
import math

import jax
import jax.numpy as jnp
from jax import lax
from jax.experimental import pallas as pl
from jax.experimental.pallas import tpu as pltpu
from jax.sharding import PartitionSpec as P

RESIDUAL_BLOCKS = 6
BASE_DILATION = 2
BLOCKS_PER_LOAD = 2
FRAMED_BLOCKS = 4
DIGIT = 128
VMEM_BYTES = 20 * 2**20
STAGE_BYTES = 40 * 2**20


def dilation(block):
    return BASE_DILATION * 2**block


def after(cells, *earlier):
    return lax.optimization_barrier((cells,) + earlier)[0]


def after_all(cells, *earlier):
    return list(lax.optimization_barrier(tuple(cells) + earlier)[: len(cells)])


def from_others(cells):
    count = lax.axis_size("trk")
    return [cells] + [
        lax.ppermute(cells, "trk", [(i, (i + k) % count) for i in range(count)])
        for k in range(1, count)
    ]


def relayed(cells):
    count = lax.axis_size("trk")
    last = count - 1
    across = lax.ppermute(cells, "trk", [(i, (i + 2) % count) for i in range(count)])
    up = lax.ppermute(cells, "trk", [(i, i + 1) for i in range(last)])
    down = lax.ppermute(cells, "trk", [(i + 1, i) for i in range(last)])
    far = lax.ppermute(across, "trk", [(last - 1, last), (1, 0)])
    return [cells, up, across, down, far]


def halo(cells, width):
    count = lax.axis_size("seq")
    head = cells[:width]
    tail = cells[cells.shape[0] - width :]
    above = lax.ppermute(tail, "seq", [(i, i + 1) for i in range(count - 1)])
    below = lax.ppermute(head, "seq", [(i + 1, i) for i in range(count - 1)])
    return above, below


def group_size(rows, count):
    size = 1
    for g in range(1, count + 1):
        if count % g == 0 and rows % (16 * g) == 0:
            size = g
    return size


def tile_of(channels):
    for width in (512, 256, 384, 128):
        if channels % width == 0:
            return width
    return channels


def dot(a, b):
    return jnp.dot(a, b, preferred_element_type=jnp.float32)


def dot_last(a, b):
    return lax.dot_general(a, b, (((1,), (1,)), ((), ())), preferred_element_type=jnp.float32)


def gelu(x):
    cubic = x + 0.044715 * (x * x * x)
    return 0.5 * x * (1.0 + jnp.tanh(math.sqrt(2.0 / math.pi) * cubic))


def pack(act):
    half = act.shape[0] // 2
    return jnp.concatenate([act[:half], act[half:]], axis=1)


def unpack(cells):
    half = cells.shape[1] // 2
    return jnp.concatenate([cells[:, :half], cells[:, half:]], axis=0)


def columns(tile, width):
    return pl.ds(tile * width, width)


def project_all(cells, weight, trunk, margin, bias, target, edge=None, closed=0):
    rows, channels = target.shape
    width = tile_of(channels)
    if closed:
        keep_top = (1 - edge[0]).astype(jnp.float32)
        keep_bottom = (1 - edge[1]).astype(jnp.float32)
    for c in range(channels // width):
        cols = columns(c, width)
        total = dot(cells, weight[:, :, :, cols].reshape(-1, width))
        total = total + bias[:, cols].astype(jnp.float32)
        total = total + trunk[pl.ds(margin, rows), cols].astype(jnp.float32)
        if closed:
            target[:closed, cols] = (total[:closed] * keep_top).astype(BF16)
            target[closed : rows - closed, cols] = total[closed : rows - closed].astype(BF16)
            target[rows - closed :, cols] = (total[rows - closed :] * keep_bottom).astype(BF16)
        else:
            target[:, cols] = total.astype(BF16)


def dilated(cells, taps, step):
    rows = cells.shape[0]
    hidden = taps.shape[1]
    joint = dot_last(cells, taps[...].reshape(3 * hidden, -1))
    sums = [joint[:, t * hidden : (t + 1) * hidden] for t in range(3)]
    return sums[1] + pltpu.roll(sums[0], step, 0) + pltpu.roll(sums[2], rows - step, 0)


def convolve(cells, taps, bias, step, act_ref):
    keep = 2 * act_ref.shape[0]
    margin = (cells.shape[0] - keep) // 2
    inner = dilated(cells, taps, step)[margin : margin + keep] + bias.astype(jnp.float32)
    act_ref[...] = pack(gelu(inner).astype(BF16))


BF16 = jnp.bfloat16
ANY = pl.BlockSpec(memory_space=pl.ANY)
SMEM = pl.BlockSpec(memory_space=pltpu.SMEM)
VMEM = pl.BlockSpec(memory_space=pltpu.VMEM)


def shape(*dims):
    return jax.ShapeDtypeStruct(dims, BF16)


def kernel_call(body, ins, outs, flops, moved, special=0, scalars=0, scratch=(), limit=VMEM_BYTES, specs=None):
    return pl.pallas_call(
        body,
        in_specs=specs or [SMEM] * scalars + [VMEM] * (len(ins) - scalars),
        out_specs=[VMEM] * len(outs),
        out_shape=list(outs),
        scratch_shapes=list(scratch),
        compiler_params=pltpu.CompilerParams(vmem_limit_bytes=limit),
        cost_estimate=pl.CostEstimate(
            flops=flops, bytes_accessed=2 * moved, transcendentals=special
        ),
    )(*ins)


def stage_kernel(plan, order_ref, *refs):
    sems = refs[-1]
    used = 0
    copies = []
    for source, target, cuts in plan:
        if cuts.func is direct_cuts:
            cuts = functools.partial(cuts, order_ref)
        for src, dst in cuts(refs[source], refs[target]):
            copies.append(pltpu.make_async_copy(src, dst, sems.at[used]))
            used += 1
    for copy in copies:
        copy.start()
    for copy in copies:
        copy.wait()


def projection_cuts(part, per_block, share, load, target):
    return [
        (load.at[pl.ds(part * per_block, per_block), pl.ds(j * share, share)], target.at[j])
        for j in range(target.shape[0])
    ]


def direct_cuts(part, per_block, order_ref, load, target):
    return [
        (load.at[order_ref[j], pl.ds(part * per_block, per_block)], target.at[j])
        for j in range(target.shape[0])
    ]


def tap_cuts(block, conv_in, target):
    return [(conv_in.at[block, t], target.at[t]) for t in range(3)]


def whole_cuts(_, source, target):
    return [(source, target)]


def stage(order, sources, targets, cuts):
    count = len(sources)
    plan = [(i, count + i, cut) for i, cut in enumerate(cuts)]
    return kernel_call(
        functools.partial(stage_kernel, plan),
        (order, *sources),
        targets,
        0,
        sum(math.prod(t.shape) for t in targets),
        scratch=[pltpu.SemaphoreType.DMA((32,))],
        specs=[SMEM] + [ANY] * count,
        limit=STAGE_BYTES,
    )


def join_kernel(*refs):
    parts, target, sems = refs[:-2], refs[-2], refs[-1]
    copies = []
    row = 0
    for k, part in enumerate(parts):
        rows = part.shape[0]
        copies.append(pltpu.make_async_copy(part, target.at[pl.ds(row, rows)], sems.at[k]))
        row += rows
    for copy in copies:
        copy.start()
    for copy in copies:
        copy.wait()


def join(parts):
    rows = sum(part.shape[0] for part in parts)
    return pl.pallas_call(
        join_kernel,
        in_specs=[ANY] * len(parts),
        out_specs=pl.BlockSpec(memory_space=pltpu.HBM),
        out_shape=shape(rows, parts[0].shape[1]),
        scratch_shapes=[pltpu.SemaphoreType.DMA((len(parts),))],
        compiler_params=pltpu.CompilerParams(vmem_limit_bytes=2**22),
        cost_estimate=pl.CostEstimate(
            flops=0, bytes_accessed=4 * rows * parts[0].shape[1], transcendentals=0
        ),
    )(*parts)


def first_kernel(step, owner_ref, c0, c1, c2, c3, c4, taps, bias_ref, act_ref, trunk, pbias):
    width = c0.shape[1]
    rows = trunk.shape[0]
    for k, cell in enumerate((c0, c1, c2, c3, c4)):

        @pl.when(owner_ref[k] >= 0)
        def _():
            cols = pl.ds(pl.multiple_of(owner_ref[k] * width, 128), width)
            trunk[:, cols] = cell[:rows]
            pbias[:, cols] = cell[rows:]

    convolve(trunk[...], taps, bias_ref[0:1], step, act_ref)


def first_conv(cells, rows, order, taps, conv_bias, step):
    _, hidden, channels = taps.shape
    return kernel_call(
        functools.partial(first_kernel, step),
        (order, *cells, taps, conv_bias),
        [
            shape(rows // 2, 2 * hidden),
            shape(rows, channels),
            shape(cells[0].shape[0] - rows, channels),
        ],
        6 * rows * hidden * channels,
        3 * hidden * channels + 2 * rows * channels,
        rows * hidden,
        scalars=1,
    )


def gather_acts(acts, edges=()):
    cells = []
    for j, act in enumerate(acts):
        parts = [unpack(act[...])]
        if edges:
            half = edges[j].shape[1] // 2
            parts = [edges[j][:, :half]] + parts + [edges[j][:, half:]]
        cells.append(jnp.concatenate(parts, axis=0))
    return jnp.concatenate(cells, axis=1)


def fused_kernel(
    block, margin, edge_ref, a0, a1, a2, a3, weight, trunk_in, pbias_ref, taps, bias_ref, act_ref,
    trunk
):
    pbias = pbias_ref[block : block + 1]
    skip = (trunk_in.shape[0] - trunk.shape[0]) // 2
    cells = gather_acts((a0, a1, a2, a3))
    project_all(cells, weight, trunk_in, skip, pbias, trunk, edge_ref, margin - skip)
    bias = bias_ref[block + 1 : block + 2]
    convolve(trunk[...], taps, bias, dilation(block + 1), act_ref)


def fused(acts, weight, trunk, pbias, taps, conv_bias, block, edge, rows_out):
    channels = trunk.shape[1]
    rows = 2 * acts[0].shape[0]
    margin = dilation(FRAMED_BLOCKS)
    hidden = taps.shape[1]
    return kernel_call(
        functools.partial(fused_kernel, block, margin),
        (edge, *acts, weight, trunk, pbias, taps, conv_bias),
        [shape(rows_out // 2, 2 * hidden), shape(rows, channels)],
        14 * rows * hidden * channels,
        7 * hidden * channels + 2 * rows * channels,
        rows * hidden,
        scalars=1,
    )


def edged_kernel(
    block, margin, edge_ref, a0, a1, a2, a3, e0, e1, e2, e3, weight, above, trunk_in, below,
    pbias_ref, taps, bias_ref, act_ref, trunk, frame
):
    rows = trunk_in.shape[0]
    frame[:margin] = above[above.shape[0] - margin :]
    frame[margin : margin + rows] = trunk_in[...]
    frame[margin + rows :] = below[:margin]
    pbias = pbias_ref[block : block + 1]
    cells = gather_acts((a0, a1, a2, a3), (e0, e1, e2, e3))
    project_all(cells, weight, frame, 0, pbias, trunk, edge_ref, margin)
    bias = bias_ref[block + 1 : block + 2]
    convolve(trunk[...], taps, bias, dilation(block + 1), act_ref)


def edged(acts, edges, weight, above, trunk, below, pbias, taps, conv_bias, block, edge):
    rows, channels = trunk.shape
    hidden = taps.shape[1]
    margin = dilation(block + 1)
    frame = rows + 2 * margin
    return kernel_call(
        functools.partial(edged_kernel, block, margin),
        (edge, *acts, *edges, weight, above, trunk, below, pbias, taps, conv_bias),
        [shape(rows // 2, 2 * hidden), shape(frame, channels)],
        14 * frame * hidden * channels,
        7 * hidden * channels + 2 * frame * channels,
        rows * hidden,
        scalars=1,
        scratch=[pltpu.VMEM((frame, channels), BF16)],
    )


def projection_kernel(block, a0, a1, a2, a3, weight, trunk_in, pbias_ref, trunk):
    margin = (trunk_in.shape[0] - trunk.shape[0]) // 2
    pbias = pbias_ref[block : block + 1]
    project_all(gather_acts((a0, a1, a2, a3)), weight, trunk_in, margin, pbias, trunk)


def projection(acts, weight, trunk, pbias, block):
    channels = trunk.shape[1]
    rows, hidden = 2 * acts[0].shape[0], acts[0].shape[1] // 2
    return kernel_call(
        functools.partial(projection_kernel, block),
        (*acts, weight, trunk, pbias),
        [shape(rows, channels)],
        8 * rows * hidden * channels,
        4 * hidden * channels + 2 * rows * channels,
    )[0]


def center_kernel(block, trunk, taps, bias_ref, act_ref):
    convolve(trunk[...], taps, bias_ref[block : block + 1], dilation(block), act_ref)


def center_conv(trunk, taps, conv_bias, block):
    rows, channels = trunk.shape
    hidden = taps.shape[1]
    return kernel_call(
        functools.partial(center_kernel, block),
        (trunk, taps, conv_bias),
        [shape((rows - 2 * dilation(block)) // 2, 2 * hidden)],
        6 * rows * hidden * channels,
        3 * hidden * channels + rows * channels,
        rows * hidden,
    )[0]


def edge_kernel(block, above, trunk, below, taps, bias_ref, act_ref):
    step = dilation(block)
    rows = trunk.shape[0]
    keep = act_ref.shape[0]
    part = keep + 2 * step
    inner_rows = part - above.shape[0]
    cells = jnp.concatenate(
        [above[...], trunk[:inner_rows], trunk[rows - inner_rows :], below[...]], axis=0
    )
    inner = dilated(cells, taps, step) + bias_ref[block : block + 1].astype(jnp.float32)
    top = inner[step : step + keep]
    bottom = inner[part + step : part + step + keep]
    act_ref[...] = jnp.concatenate([gelu(top).astype(BF16), gelu(bottom).astype(BF16)], axis=1)


def edge_conv(above, trunk, below, taps, conv_bias, block):
    channels = trunk.shape[1]
    hidden = taps.shape[1]
    step = dilation(block)
    keep = above.shape[0]
    rows = 2 * (keep + 2 * step)
    return kernel_call(
        functools.partial(edge_kernel, block),
        (above, trunk, below, taps, conv_bias),
        [shape(keep, 2 * hidden)],
        6 * rows * hidden * channels,
        3 * hidden * channels + rows * channels,
        rows * hidden,
    )[0]


def head_kernel(
    block, a0, a1, a2, a3, weight, trunk_in, pbias_ref, head_ref, hbias_ref, onehot_ref,
    cover_ref, gene_ref, trunk
):
    pbias = pbias_ref[block : block + 1]
    margin = (trunk_in.shape[0] - trunk.shape[0]) // 2
    project_all(gather_acts((a0, a1, a2, a3)), weight, trunk_in, margin, pbias, trunk)
    tracks = head_ref.shape[1]
    width = tile_of(tracks)
    for c in range(tracks // width):
        cols = columns(c, width)
        x = dot(trunk[...], head_ref[:, cols]) + hbias_ref[:, cols].astype(jnp.float32)
        tile = (jnp.maximum(x, 0.0) + jnp.log1p(jnp.exp(-jnp.abs(x)))).astype(BF16)
        cover_ref[:, cols] = tile
        gene_ref[:, cols] = dot(onehot_ref[...], tile).astype(BF16)


def head(acts, weight, trunk, pbias, block, head_weight, head_bias, onehot):
    channels = trunk.shape[1]
    rows, hidden = 2 * acts[0].shape[0], acts[0].shape[1] // 2
    tracks = head_weight.shape[1]
    genes = onehot.shape[0]
    return kernel_call(
        functools.partial(head_kernel, block),
        (*acts, weight, trunk, pbias, head_weight, head_bias, onehot),
        [shape(rows, tracks), shape(genes, tracks)],
        8 * rows * hidden * channels + 2 * rows * channels * tracks,
        4 * hidden * channels + rows * channels + channels * tracks,
        2 * rows * tracks,
        scratch=[pltpu.VMEM((rows, channels), BF16)],
    )


def exon_digits(exon_bins, channels):
    digits = jnp.concatenate([exon_bins >> 7, exon_bins & (DIGIT - 1)], axis=1)
    genes, width = digits.shape
    return jnp.pad(digits.astype(jnp.bfloat16), ((0, -genes % 16), (0, channels - width)))


def exon_lists(rows, genes, entries):
    digits = rows[:, :genes, : 2 * entries].astype(jnp.int32)
    lists = digits[:, :, :entries] * DIGIT + digits[:, :, entries:]
    return lists.reshape(-1, entries)


def exon_onehot(gene_block, first_bin, width_now):
    exon_matches = (
        gene_block[:, :, None] - first_bin == jnp.arange(width_now, dtype=jnp.int32)[None, None, :]
    )
    return jnp.sum(exon_matches.astype(jnp.float32), axis=1).astype(jnp.bfloat16)


def shards(
    trunk_input, conv_in, conv_bias, conv_out, projection_bias, head_weight, head_bias, exon_bins
):
    quarters = lax.axis_size("trk")
    place = lax.axis_index("trk")
    count = lax.axis_size("seq")
    lane = lax.axis_index("seq")
    bin_rows, channels_here = trunk_input.shape
    blocks, hidden, channels = conv_out.shape
    genes_here, entries = exon_bins.shape

    load_rows = BLOCKS_PER_LOAD * hidden
    size = group_size(load_rows, count)
    share = load_rows // size
    per_block = hidden // share
    groups = [[g * size + i for i in range(size)] for g in range(count // size)]
    mine = lax.rem(lane, size)
    packed = size == count and 2 * entries <= channels

    flat = conv_out.reshape(blocks * hidden, channels)

    def column(load):
        return lax.dynamic_slice_in_dim(flat, load * load_rows + mine * share, share, 0)

    def gather(parts):
        return lax.all_gather(
            join(parts), "seq", axis=0, tiled=False, axis_index_groups=groups
        )

    margin = dilation(FRAMED_BLOCKS)
    frame = bin_rows + 2 * margin
    order = lax.rem(place - jnp.arange(quarters, dtype=jnp.int32) + quarters, quarters)
    last_place = quarters - 1
    owners = jnp.stack(
        [
            place,
            place - 1,
            lax.rem(place + 2, quarters),
            jnp.where(place == last_place, -1, place + 1),
            jnp.where((place == 0) | (place == last_place), last_place - place, -1),
        ]
    ).astype(jnp.int32)
    edge = jnp.stack([lane == 0, lane == count - 1]).astype(jnp.int32)

    above, below = halo(trunk_input, margin)
    first = from_others(column(0))
    loads = [gather(after_all(first, above, below))]
    own = jnp.concatenate(
        [above, trunk_input, below, jnp.pad(projection_bias, ((0, -blocks % 16), (0, 0)))], axis=0
    )
    own = after(own, first[1])
    cells = relayed(own)
    exon_rows = [exon_digits(exon_bins, channels)] if packed else []
    exon_rows = [exon_digits(exon_bins, channels)] if packed else []
    second = from_others(after(column(1), cells[2]))
    taps_shape = shape(3, hidden, channels)
    weight_shape = shape(quarters, per_block, share, channels)
    head_row = head_bias[None, :]
    (taps,) = stage(order, (after(conv_in, own, head_row),), (taps_shape,), (functools.partial(tap_cuts, 0),))
    act, trunk, biases = first_conv(cells, frame, owners, taps, conv_bias, dilation(0))

    def staged(block, extra, extra_shape, extra_cut, token):
        place = block // BLOCKS_PER_LOAD
        part = block % BLOCKS_PER_LOAD
        cut = functools.partial(projection_cuts, part, per_block, share)
        load = after(loads[place], token)
        return stage(order, (load, extra), (weight_shape, extra_shape), (cut, extra_cut))

    for block in range(FRAMED_BLOCKS):
        later = block + 1
        others = from_others(act)
        if block == 0:
            third = from_others(after(column(2), others[2]))
            loads.append(gather(after_all(second, act) + exon_rows))
        if block == 2:
            loads.append(gather(after_all(third, act)))
        if block == 3:
            if packed:
                gene_lists = exon_lists(loads[1][:, quarters * share :], genes_here, entries)
            else:
                gene_lists = lax.all_gather(exon_bins, "seq", axis=0, tiled=True)
            onehot = exon_onehot(gene_lists, lane * bin_rows, bin_rows)
            loads[1] = after(loads[1], onehot)
        weight, taps = staged(
            block, conv_in, taps_shape, functools.partial(tap_cuts, later), act
        )
        if later < FRAMED_BLOCKS:
            reach = sum(dilation(b) for b in range(later + 1, FRAMED_BLOCKS))
            rows_out = bin_rows + 2 * (-(-reach // 16) * 16)
            act, trunk = fused(
                others, weight, trunk, biases, taps, conv_bias, block, edge, rows_out
            )
        else:
            trunk = projection(others, weight, trunk, biases, block)

    block = FRAMED_BLOCKS
    later = block + 1
    act = center_conv(trunk, taps, conv_bias, block)
    others = from_others(act)
    above, below = halo(after(trunk, act), dilation(block) + dilation(later))
    edges = from_others(edge_conv(above, trunk, below, taps, conv_bias, block))
    weight, taps = staged(block, conv_in, taps_shape, functools.partial(tap_cuts, later), act)
    act, trunk = edged(
        others, edges, weight, above, trunk, below, biases, taps, conv_bias, block, edge
    )

    others = from_others(act)
    weight, head_rows = staged(
        later, head_weight, shape(*head_weight.shape), functools.partial(whole_cuts, 0), act
    )
    coverage, partial = head(
        others, weight, trunk, biases, later, head_rows, head_row, onehot
    )

    parts = lax.all_to_all(
        partial.reshape(count, genes_here, partial.shape[1]), "seq", 0, 0, tiled=False
    )
    gene_sum = jnp.sum(parts.astype(jnp.float32), axis=0)
    counts = jnp.sum((exon_bins >= 0).astype(jnp.float32), axis=1)
    gene_cov = gene_sum / counts[:, None]
    return (coverage, gene_cov)


def solution(mesh):
    in_specs = (
        P("seq", "trk"),
        P(None, None, "trk", None),
        P(None, "trk"),
        P(None, "trk", None),
        P(None, "trk"),
        P(None, "trk"),
        P("trk"),
        P("seq", None),
    )
    out_specs = (P("seq", "trk"), P("seq", "trk"))
    return jax.shard_map(shards, mesh=mesh, in_specs=in_specs, out_specs=out_specs, check_vma=False)
```

```python
import functools
import math

import jax
import jax.numpy as jnp
from jax import lax
from jax.experimental import pallas as pl
from jax.experimental.pallas import tpu as pltpu
from jax.sharding import PartitionSpec as P

RESIDUAL_BLOCKS = 6
BASE_DILATION = 2
BLOCKS_PER_LOAD = 2
FRAMED_BLOCKS = 4
DIGIT = 128
VMEM_BYTES = 20 * 2**20
STAGE_BYTES = 40 * 2**20


def dilation(block):
    return BASE_DILATION * 2**block


def after(cells, *earlier):
    return lax.optimization_barrier((cells,) + earlier)[0]


def after_all(cells, *earlier):
    return list(lax.optimization_barrier(tuple(cells) + earlier)[: len(cells)])


def from_others(cells):
    count = lax.axis_size("trk")
    return [cells] + [
        lax.ppermute(cells, "trk", [(i, (i + k) % count) for i in range(count)])
        for k in range(1, count)
    ]


def relayed(cells):
    count = lax.axis_size("trk")
    last = count - 1
    across = lax.ppermute(cells, "trk", [(i, (i + 2) % count) for i in range(count)])
    up = lax.ppermute(cells, "trk", [(i, i + 1) for i in range(last)])
    down = lax.ppermute(cells, "trk", [(i + 1, i) for i in range(last)])
    far = lax.ppermute(across, "trk", [(last - 1, last), (1, 0)])
    return [cells, up, across, down, far]


def halo(cells, width):
    count = lax.axis_size("seq")
    head = cells[:width]
    tail = cells[cells.shape[0] - width :]
    above = lax.ppermute(tail, "seq", [(i, i + 1) for i in range(count - 1)])
    below = lax.ppermute(head, "seq", [(i + 1, i) for i in range(count - 1)])
    return above, below


def group_size(rows, count):
    size = 1
    for g in range(1, count + 1):
        if count % g == 0 and rows % (16 * g) == 0:
            size = g
    return size


def tile_of(channels):
    for width in (512, 256, 384, 128):
        if channels % width == 0:
            return width
    return channels


def dot(a, b):
    return jnp.dot(a, b, preferred_element_type=jnp.float32)


def dot_last(a, b):
    return lax.dot_general(a, b, (((1,), (1,)), ((), ())), preferred_element_type=jnp.float32)


def gelu(x):
    cubic = x + 0.044715 * (x * x * x)
    return 0.5 * x * (1.0 + jnp.tanh(math.sqrt(2.0 / math.pi) * cubic))


def pack(act):
    half = act.shape[0] // 2
    return jnp.concatenate([act[:half], act[half:]], axis=1)


def unpack(cells):
    half = cells.shape[1] // 2
    return jnp.concatenate([cells[:, :half], cells[:, half:]], axis=0)


def columns(tile, width):
    return pl.ds(tile * width, width)


def project_all(cells, weight, trunk, margin, bias, target, edge=None, closed=0):
    rows, channels = target.shape
    width = tile_of(channels)
    if closed:
        keep_top = (1 - edge[0]).astype(jnp.float32)
        keep_bottom = (1 - edge[1]).astype(jnp.float32)
    for c in range(channels // width):
        cols = columns(c, width)
        total = dot(cells, weight[:, :, :, cols].reshape(-1, width))
        total = total + bias[:, cols].astype(jnp.float32)
        total = total + trunk[pl.ds(margin, rows), cols].astype(jnp.float32)
        if closed:
            target[:closed, cols] = (total[:closed] * keep_top).astype(BF16)
            target[closed : rows - closed, cols] = total[closed : rows - closed].astype(BF16)
            target[rows - closed :, cols] = (total[rows - closed :] * keep_bottom).astype(BF16)
        else:
            target[:, cols] = total.astype(BF16)


def dilated(cells, taps, step):
    rows = cells.shape[0]
    hidden = taps.shape[1]
    joint = dot_last(cells, taps[...].reshape(3 * hidden, -1))
    sums = [joint[:, t * hidden : (t + 1) * hidden] for t in range(3)]
    return sums[1] + pltpu.roll(sums[0], step, 0) + pltpu.roll(sums[2], rows - step, 0)


def convolve(cells, taps, bias, step, act_ref):
    keep = 2 * act_ref.shape[0]
    margin = (cells.shape[0] - keep) // 2
    inner = dilated(cells, taps, step)[margin : margin + keep] + bias.astype(jnp.float32)
    act_ref[...] = pack(gelu(inner).astype(BF16))


BF16 = jnp.bfloat16
ANY = pl.BlockSpec(memory_space=pl.ANY)
SMEM = pl.BlockSpec(memory_space=pltpu.SMEM)
VMEM = pl.BlockSpec(memory_space=pltpu.VMEM)


def shape(*dims):
    return jax.ShapeDtypeStruct(dims, BF16)


def kernel_call(body, ins, outs, flops, moved, special=0, scalars=0, scratch=(), limit=VMEM_BYTES, specs=None):
    return pl.pallas_call(
        body,
        in_specs=specs or [SMEM] * scalars + [VMEM] * (len(ins) - scalars),
        out_specs=[VMEM] * len(outs),
        out_shape=list(outs),
        scratch_shapes=list(scratch),
        compiler_params=pltpu.CompilerParams(vmem_limit_bytes=limit),
        cost_estimate=pl.CostEstimate(
            flops=flops, bytes_accessed=2 * moved, transcendentals=special
        ),
    )(*ins)


def stage_kernel(plan, order_ref, *refs):
    sems = refs[-1]
    used = 0
    copies = []
    for source, target, cuts in plan:
        if cuts.func is direct_cuts:
            cuts = functools.partial(cuts, order_ref)
        for src, dst in cuts(refs[source], refs[target]):
            copies.append(pltpu.make_async_copy(src, dst, sems.at[used]))
            used += 1
    for copy in copies:
        copy.start()
    for copy in copies:
        copy.wait()


def projection_cuts(part, per_block, share, load, target):
    return [
        (load.at[pl.ds(part * per_block, per_block), pl.ds(j * share, share)], target.at[j])
        for j in range(target.shape[0])
    ]


def direct_cuts(part, per_block, order_ref, load, target):
    return [
        (load.at[order_ref[j], pl.ds(part * per_block, per_block)], target.at[j])
        for j in range(target.shape[0])
    ]


def tap_cuts(block, conv_in, target):
    return [(conv_in.at[block, t], target.at[t]) for t in range(3)]


def whole_cuts(_, source, target):
    return [(source, target)]


def stage(order, sources, targets, cuts):
    count = len(sources)
    plan = [(i, count + i, cut) for i, cut in enumerate(cuts)]
    return kernel_call(
        functools.partial(stage_kernel, plan),
        (order, *sources),
        targets,
        0,
        sum(math.prod(t.shape) for t in targets),
        scratch=[pltpu.SemaphoreType.DMA((32,))],
        specs=[SMEM] + [ANY] * count,
        limit=STAGE_BYTES,
    )


def join_kernel(*refs):
    parts, target, sems = refs[:-2], refs[-2], refs[-1]
    copies = []
    row = 0
    for k, part in enumerate(parts):
        rows = part.shape[0]
        copies.append(pltpu.make_async_copy(part, target.at[pl.ds(row, rows)], sems.at[k]))
        row += rows
    for copy in copies:
        copy.start()
    for copy in copies:
        copy.wait()


def join(parts):
    rows = sum(part.shape[0] for part in parts)
    return pl.pallas_call(
        join_kernel,
        in_specs=[ANY] * len(parts),
        out_specs=pl.BlockSpec(memory_space=pltpu.HBM),
        out_shape=shape(rows, parts[0].shape[1]),
        scratch_shapes=[pltpu.SemaphoreType.DMA((len(parts),))],
        compiler_params=pltpu.CompilerParams(vmem_limit_bytes=2**22),
        cost_estimate=pl.CostEstimate(
            flops=0, bytes_accessed=4 * rows * parts[0].shape[1], transcendentals=0
        ),
    )(*parts)


def first_kernel(step, owner_ref, c0, c1, c2, c3, c4, taps, bias_ref, act_ref, trunk, pbias):
    width = c0.shape[1]
    rows = trunk.shape[0]
    for k, cell in enumerate((c0, c1, c2, c3, c4)):

        @pl.when(owner_ref[k] >= 0)
        def _():
            cols = pl.ds(pl.multiple_of(owner_ref[k] * width, 128), width)
            trunk[:, cols] = cell[:rows]
            pbias[:, cols] = cell[rows:]

    convolve(trunk[...], taps, bias_ref[0:1], step, act_ref)


def first_conv(cells, rows, order, taps, conv_bias, step):
    _, hidden, channels = taps.shape
    return kernel_call(
        functools.partial(first_kernel, step),
        (order, *cells, taps, conv_bias),
        [
            shape(rows // 2, 2 * hidden),
            shape(rows, channels),
            shape(cells[0].shape[0] - rows, channels),
        ],
        6 * rows * hidden * channels,
        3 * hidden * channels + 2 * rows * channels,
        rows * hidden,
        scalars=1,
    )


def gather_acts(acts, edges=()):
    cells = []
    for j, act in enumerate(acts):
        parts = [unpack(act[...])]
        if edges:
            half = edges[j].shape[1] // 2
            parts = [edges[j][:, :half]] + parts + [edges[j][:, half:]]
        cells.append(jnp.concatenate(parts, axis=0))
    return jnp.concatenate(cells, axis=1)


def fused_kernel(
    block, margin, edge_ref, a0, a1, a2, a3, weight, trunk_in, pbias_ref, taps, bias_ref, act_ref,
    trunk
):
    pbias = pbias_ref[block : block + 1]
    skip = (trunk_in.shape[0] - trunk.shape[0]) // 2
    cells = gather_acts((a0, a1, a2, a3))
    project_all(cells, weight, trunk_in, skip, pbias, trunk, edge_ref, margin - skip)
    bias = bias_ref[block + 1 : block + 2]
    convolve(trunk[...], taps, bias, dilation(block + 1), act_ref)


def fused(acts, weight, trunk, pbias, taps, conv_bias, block, edge, rows_out):
    channels = trunk.shape[1]
    rows = 2 * acts[0].shape[0]
    margin = dilation(FRAMED_BLOCKS)
    hidden = taps.shape[1]
    return kernel_call(
        functools.partial(fused_kernel, block, margin),
        (edge, *acts, weight, trunk, pbias, taps, conv_bias),
        [shape(rows_out // 2, 2 * hidden), shape(rows, channels)],
        14 * rows * hidden * channels,
        7 * hidden * channels + 2 * rows * channels,
        rows * hidden,
        scalars=1,
    )


def edged_kernel(
    block, margin, edge_ref, a0, a1, a2, a3, e0, e1, e2, e3, weight, above, trunk_in, below,
    pbias_ref, taps, bias_ref, act_ref, trunk, frame
):
    rows = trunk_in.shape[0]
    frame[:margin] = above[above.shape[0] - margin :]
    frame[margin : margin + rows] = trunk_in[...]
    frame[margin + rows :] = below[:margin]
    pbias = pbias_ref[block : block + 1]
    cells = gather_acts((a0, a1, a2, a3), (e0, e1, e2, e3))
    project_all(cells, weight, frame, 0, pbias, trunk, edge_ref, margin)
    bias = bias_ref[block + 1 : block + 2]
    convolve(trunk[...], taps, bias, dilation(block + 1), act_ref)


def edged(acts, edges, weight, above, trunk, below, pbias, taps, conv_bias, block, edge):
    rows, channels = trunk.shape
    hidden = taps.shape[1]
    margin = dilation(block + 1)
    frame = rows + 2 * margin
    return kernel_call(
        functools.partial(edged_kernel, block, margin),
        (edge, *acts, *edges, weight, above, trunk, below, pbias, taps, conv_bias),
        [shape(rows // 2, 2 * hidden), shape(frame, channels)],
        14 * frame * hidden * channels,
        7 * hidden * channels + 2 * frame * channels,
        rows * hidden,
        scalars=1,
        scratch=[pltpu.VMEM((frame, channels), BF16)],
    )


def projection_kernel(block, a0, a1, a2, a3, weight, trunk_in, pbias_ref, trunk):
    margin = (trunk_in.shape[0] - trunk.shape[0]) // 2
    pbias = pbias_ref[block : block + 1]
    project_all(gather_acts((a0, a1, a2, a3)), weight, trunk_in, margin, pbias, trunk)


def projection(acts, weight, trunk, pbias, block):
    channels = trunk.shape[1]
    rows, hidden = 2 * acts[0].shape[0], acts[0].shape[1] // 2
    return kernel_call(
        functools.partial(projection_kernel, block),
        (*acts, weight, trunk, pbias),
        [shape(rows, channels)],
        8 * rows * hidden * channels,
        4 * hidden * channels + 2 * rows * channels,
    )[0]


def center_kernel(block, trunk, taps, bias_ref, act_ref):
    convolve(trunk[...], taps, bias_ref[block : block + 1], dilation(block), act_ref)


def center_conv(trunk, taps, conv_bias, block):
    rows, channels = trunk.shape
    hidden = taps.shape[1]
    return kernel_call(
        functools.partial(center_kernel, block),
        (trunk, taps, conv_bias),
        [shape((rows - 2 * dilation(block)) // 2, 2 * hidden)],
        6 * rows * hidden * channels,
        3 * hidden * channels + rows * channels,
        rows * hidden,
    )[0]


def edge_kernel(block, above, trunk, below, taps, bias_ref, act_ref):
    step = dilation(block)
    rows = trunk.shape[0]
    keep = act_ref.shape[0]
    part = keep + 2 * step
    inner_rows = part - above.shape[0]
    cells = jnp.concatenate(
        [above[...], trunk[:inner_rows], trunk[rows - inner_rows :], below[...]], axis=0
    )
    inner = dilated(cells, taps, step) + bias_ref[block : block + 1].astype(jnp.float32)
    top = inner[step : step + keep]
    bottom = inner[part + step : part + step + keep]
    act_ref[...] = jnp.concatenate([gelu(top).astype(BF16), gelu(bottom).astype(BF16)], axis=1)


def edge_conv(above, trunk, below, taps, conv_bias, block):
    channels = trunk.shape[1]
    hidden = taps.shape[1]
    step = dilation(block)
    keep = above.shape[0]
    rows = 2 * (keep + 2 * step)
    return kernel_call(
        functools.partial(edge_kernel, block),
        (above, trunk, below, taps, conv_bias),
        [shape(keep, 2 * hidden)],
        6 * rows * hidden * channels,
        3 * hidden * channels + rows * channels,
        rows * hidden,
    )[0]


def head_kernel(
    block, a0, a1, a2, a3, weight, trunk_in, pbias_ref, head_ref, hbias_ref, onehot_ref,
    cover_ref, gene_ref, trunk
):
    pbias = pbias_ref[block : block + 1]
    margin = (trunk_in.shape[0] - trunk.shape[0]) // 2
    project_all(gather_acts((a0, a1, a2, a3)), weight, trunk_in, margin, pbias, trunk)
    tracks = head_ref.shape[1]
    width = tile_of(tracks)
    for c in range(tracks // width):
        cols = columns(c, width)
        x = dot(trunk[...], head_ref[:, cols]) + hbias_ref[:, cols].astype(jnp.float32)
        tile = (jnp.maximum(x, 0.0) + jnp.log1p(jnp.exp(-jnp.abs(x)))).astype(BF16)
        cover_ref[:, cols] = tile
        gene_ref[:, cols] = dot(onehot_ref[...], tile).astype(BF16)


def head(acts, weight, trunk, pbias, block, head_weight, head_bias, onehot):
    channels = trunk.shape[1]
    rows, hidden = 2 * acts[0].shape[0], acts[0].shape[1] // 2
    tracks = head_weight.shape[1]
    genes = onehot.shape[0]
    return kernel_call(
        functools.partial(head_kernel, block),
        (*acts, weight, trunk, pbias, head_weight, head_bias, onehot),
        [shape(rows, tracks), shape(genes, tracks)],
        8 * rows * hidden * channels + 2 * rows * channels * tracks,
        4 * hidden * channels + rows * channels + channels * tracks,
        2 * rows * tracks,
        scratch=[pltpu.VMEM((rows, channels), BF16)],
    )


def exon_digits(exon_bins, channels):
    digits = jnp.concatenate([exon_bins >> 7, exon_bins & (DIGIT - 1)], axis=1)
    genes, width = digits.shape
    return jnp.pad(digits.astype(jnp.bfloat16), ((0, -genes % 16), (0, channels - width)))


def exon_lists(rows, genes, entries):
    digits = rows[:, :genes, : 2 * entries].astype(jnp.int32)
    lists = digits[:, :, :entries] * DIGIT + digits[:, :, entries:]
    return lists.reshape(-1, entries)


def exon_onehot(gene_block, first_bin, width_now):
    exon_matches = (
        gene_block[:, :, None] - first_bin == jnp.arange(width_now, dtype=jnp.int32)[None, None, :]
    )
    return jnp.sum(exon_matches.astype(jnp.float32), axis=1).astype(jnp.bfloat16)


def shards(
    trunk_input, conv_in, conv_bias, conv_out, projection_bias, head_weight, head_bias, exon_bins
):
    quarters = lax.axis_size("trk")
    place = lax.axis_index("trk")
    count = lax.axis_size("seq")
    lane = lax.axis_index("seq")
    bin_rows, channels_here = trunk_input.shape
    blocks, hidden, channels = conv_out.shape
    genes_here, entries = exon_bins.shape

    load_rows = BLOCKS_PER_LOAD * hidden
    size = group_size(load_rows, count)
    share = load_rows // size
    per_block = hidden // share
    groups = [[g * size + i for i in range(size)] for g in range(count // size)]
    mine = lax.rem(lane, size)
    packed = size == count and 2 * entries <= channels

    flat = conv_out.reshape(blocks * hidden, channels)

    def column(load):
        return lax.dynamic_slice_in_dim(flat, load * load_rows + mine * share, share, 0)

    def gather(parts):
        return lax.all_gather(
            join(parts), "seq", axis=0, tiled=False, axis_index_groups=groups
        )

    margin = dilation(FRAMED_BLOCKS)
    frame = bin_rows + 2 * margin
    order = lax.rem(place - jnp.arange(quarters, dtype=jnp.int32) + quarters, quarters)
    last_place = quarters - 1
    owners = jnp.stack(
        [
            place,
            place - 1,
            lax.rem(place + 2, quarters),
            jnp.where(place == last_place, -1, place + 1),
            jnp.where((place == 0) | (place == last_place), last_place - place, -1),
        ]
    ).astype(jnp.int32)
    edge = jnp.stack([lane == 0, lane == count - 1]).astype(jnp.int32)

    above, below = halo(trunk_input, margin)
    first = from_others(column(0))
    loads = [gather(after_all(first, above, below))]
    own = jnp.concatenate(
        [above, trunk_input, below, jnp.pad(projection_bias, ((0, -blocks % 16), (0, 0)))], axis=0
    )
    own = after(own, first[1])
    cells = relayed(own)
    exon_rows = [exon_digits(exon_bins, channels)] if packed else []
    exon_rows = [exon_digits(exon_bins, channels)] if packed else []
    second = from_others(after(column(1), cells[3]))
    taps_shape = shape(3, hidden, channels)
    weight_shape = shape(quarters, per_block, share, channels)
    head_row = head_bias[None, :]
    (taps,) = stage(order, (after(conv_in, own, head_row),), (taps_shape,), (functools.partial(tap_cuts, 0),))
    act, trunk, biases = first_conv(cells, frame, owners, taps, conv_bias, dilation(0))

    def staged(block, extra, extra_shape, extra_cut, token):
        place = block // BLOCKS_PER_LOAD
        part = block % BLOCKS_PER_LOAD
        cut = functools.partial(projection_cuts, part, per_block, share)
        load = after(loads[place], token)
        return stage(order, (load, extra), (weight_shape, extra_shape), (cut, extra_cut))

    for block in range(FRAMED_BLOCKS):
        later = block + 1
        others = from_others(act)
        if block == 0:
            loads.append(gather(after_all(second, act) + exon_rows))
        if block == 2:
            loads.append(gather(after_all(third, act)))
        if block == 3:
            if packed:
                gene_lists = exon_lists(loads[1][:, quarters * share :], genes_here, entries)
            else:
                gene_lists = lax.all_gather(exon_bins, "seq", axis=0, tiled=True)
            onehot = exon_onehot(gene_lists, lane * bin_rows, bin_rows)
            loads[1] = after(loads[1], onehot)
        weight, taps = staged(
            block, conv_in, taps_shape, functools.partial(tap_cuts, later), act
        )
        if block == 1:
            third = from_others(after(column(2), weight))
        if later < FRAMED_BLOCKS:
            reach = sum(dilation(b) for b in range(later + 1, FRAMED_BLOCKS))
            rows_out = bin_rows + 2 * (-(-reach // 16) * 16)
            act, trunk = fused(
                others, weight, trunk, biases, taps, conv_bias, block, edge, rows_out
            )
        else:
            trunk = projection(others, weight, trunk, biases, block)

    block = FRAMED_BLOCKS
    later = block + 1
    act = center_conv(trunk, taps, conv_bias, block)
    others = from_others(act)
    above, below = halo(after(trunk, act), dilation(block) + dilation(later))
    edges = from_others(edge_conv(above, trunk, below, taps, conv_bias, block))
    weight, taps = staged(block, conv_in, taps_shape, functools.partial(tap_cuts, later), act)
    act, trunk = edged(
        others, edges, weight, above, trunk, below, biases, taps, conv_bias, block, edge
    )

    others = from_others(act)
    weight, head_rows = staged(
        later, head_weight, shape(*head_weight.shape), functools.partial(whole_cuts, 0), act
    )
    coverage, partial = head(
        others, weight, trunk, biases, later, head_rows, head_row, onehot
    )

    parts = lax.all_to_all(
        partial.reshape(count, genes_here, partial.shape[1]), "seq", 0, 0, tiled=False
    )
    gene_sum = jnp.sum(parts.astype(jnp.float32), axis=0)
    counts = jnp.sum((exon_bins >= 0).astype(jnp.float32), axis=1)
    gene_cov = gene_sum / counts[:, None]
    return (coverage, gene_cov)


def solution(mesh):
    in_specs = (
        P("seq", "trk"),
        P(None, None, "trk", None),
        P(None, "trk"),
        P(None, "trk", None),
        P(None, "trk"),
        P(None, "trk"),
        P("trk"),
        P("seq", None),
    )
    out_specs = (P("seq", "trk"), P("seq", "trk"))
    return jax.shard_map(shards, mesh=mesh, in_specs=in_specs, out_specs=out_specs, check_vma=False)
```

```python
import functools
import math

import jax
import jax.numpy as jnp
from jax import lax
from jax.experimental import pallas as pl
from jax.experimental.pallas import tpu as pltpu
from jax.sharding import PartitionSpec as P

RESIDUAL_BLOCKS = 6
BASE_DILATION = 2
BLOCKS_PER_LOAD = 2
FRAMED_BLOCKS = 4
DIGIT = 128
VMEM_BYTES = 20 * 2**20
STAGE_BYTES = 40 * 2**20


def dilation(block):
    return BASE_DILATION * 2**block


def after(cells, *earlier):
    return lax.optimization_barrier((cells,) + earlier)[0]


def after_all(cells, *earlier):
    return list(lax.optimization_barrier(tuple(cells) + earlier)[: len(cells)])


def from_others(cells):
    count = lax.axis_size("trk")
    return [cells] + [
        lax.ppermute(cells, "trk", [(i, (i + k) % count) for i in range(count)])
        for k in range(1, count)
    ]


def relayed(cells):
    count = lax.axis_size("trk")
    last = count - 1
    across = lax.ppermute(cells, "trk", [(i, (i + 2) % count) for i in range(count)])
    up = lax.ppermute(cells, "trk", [(i, i + 1) for i in range(last)])
    down = lax.ppermute(cells, "trk", [(i + 1, i) for i in range(last)])
    far = lax.ppermute(across, "trk", [(last - 1, last), (1, 0)])
    return [cells, up, across, down, far]


def halo(cells, width):
    count = lax.axis_size("seq")
    head = cells[:width]
    tail = cells[cells.shape[0] - width :]
    above = lax.ppermute(tail, "seq", [(i, i + 1) for i in range(count - 1)])
    below = lax.ppermute(head, "seq", [(i + 1, i) for i in range(count - 1)])
    return above, below


def group_size(rows, count):
    size = 1
    for g in range(1, count + 1):
        if count % g == 0 and rows % (16 * g) == 0:
            size = g
    return size


def tile_of(channels):
    for width in (512, 256, 384, 128):
        if channels % width == 0:
            return width
    return channels


def dot(a, b):
    return jnp.dot(a, b, preferred_element_type=jnp.float32)


def dot_last(a, b):
    return lax.dot_general(a, b, (((1,), (1,)), ((), ())), preferred_element_type=jnp.float32)


def gelu(x):
    cubic = x + 0.044715 * (x * x * x)
    return 0.5 * x * (1.0 + jnp.tanh(math.sqrt(2.0 / math.pi) * cubic))


def pack(act):
    half = act.shape[0] // 2
    return jnp.concatenate([act[:half], act[half:]], axis=1)


def unpack(cells):
    half = cells.shape[1] // 2
    return jnp.concatenate([cells[:, :half], cells[:, half:]], axis=0)


def columns(tile, width):
    return pl.ds(tile * width, width)


def project_all(cells, weight, trunk, margin, bias, target, edge=None, closed=0):
    rows, channels = target.shape
    width = tile_of(channels)
    if closed:
        keep_top = (1 - edge[0]).astype(jnp.float32)
        keep_bottom = (1 - edge[1]).astype(jnp.float32)
    for c in range(channels // width):
        cols = columns(c, width)
        total = dot(cells, weight[:, :, :, cols].reshape(-1, width))
        total = total + bias[:, cols].astype(jnp.float32)
        total = total + trunk[pl.ds(margin, rows), cols].astype(jnp.float32)
        if closed:
            target[:closed, cols] = (total[:closed] * keep_top).astype(BF16)
            target[closed : rows - closed, cols] = total[closed : rows - closed].astype(BF16)
            target[rows - closed :, cols] = (total[rows - closed :] * keep_bottom).astype(BF16)
        else:
            target[:, cols] = total.astype(BF16)


def dilated(cells, taps, step):
    rows = cells.shape[0]
    hidden = taps.shape[1]
    joint = dot_last(cells, taps[...].reshape(3 * hidden, -1))
    sums = [joint[:, t * hidden : (t + 1) * hidden] for t in range(3)]
    return sums[1] + pltpu.roll(sums[0], step, 0) + pltpu.roll(sums[2], rows - step, 0)


def convolve(cells, taps, bias, step, act_ref):
    keep = 2 * act_ref.shape[0]
    margin = (cells.shape[0] - keep) // 2
    inner = dilated(cells, taps, step)[margin : margin + keep] + bias.astype(jnp.float32)
    act_ref[...] = pack(gelu(inner).astype(BF16))


BF16 = jnp.bfloat16
ANY = pl.BlockSpec(memory_space=pl.ANY)
SMEM = pl.BlockSpec(memory_space=pltpu.SMEM)
VMEM = pl.BlockSpec(memory_space=pltpu.VMEM)


def shape(*dims):
    return jax.ShapeDtypeStruct(dims, BF16)


def kernel_call(body, ins, outs, flops, moved, special=0, scalars=0, scratch=(), limit=VMEM_BYTES, specs=None):
    return pl.pallas_call(
        body,
        in_specs=specs or [SMEM] * scalars + [VMEM] * (len(ins) - scalars),
        out_specs=[VMEM] * len(outs),
        out_shape=list(outs),
        scratch_shapes=list(scratch),
        compiler_params=pltpu.CompilerParams(vmem_limit_bytes=limit),
        cost_estimate=pl.CostEstimate(
            flops=flops, bytes_accessed=2 * moved, transcendentals=special
        ),
    )(*ins)


def stage_kernel(plan, order_ref, *refs):
    sems = refs[-1]
    used = 0
    copies = []
    for source, target, cuts in plan:
        if cuts.func is direct_cuts:
            cuts = functools.partial(cuts, order_ref)
        for src, dst in cuts(refs[source], refs[target]):
            copies.append(pltpu.make_async_copy(src, dst, sems.at[used]))
            used += 1
    for copy in copies:
        copy.start()
    for copy in copies:
        copy.wait()


def projection_cuts(part, per_block, share, load, target):
    return [
        (load.at[pl.ds(part * per_block, per_block), pl.ds(j * share, share)], target.at[j])
        for j in range(target.shape[0])
    ]


def direct_cuts(part, per_block, order_ref, load, target):
    return [
        (load.at[order_ref[j], pl.ds(part * per_block, per_block)], target.at[j])
        for j in range(target.shape[0])
    ]


def tap_cuts(block, conv_in, target):
    return [(conv_in.at[block, t], target.at[t]) for t in range(3)]


def whole_cuts(_, source, target):
    return [(source, target)]


def stage(order, sources, targets, cuts):
    count = len(sources)
    plan = [(i, count + i, cut) for i, cut in enumerate(cuts)]
    return kernel_call(
        functools.partial(stage_kernel, plan),
        (order, *sources),
        targets,
        0,
        sum(math.prod(t.shape) for t in targets),
        scratch=[pltpu.SemaphoreType.DMA((32,))],
        specs=[SMEM] + [ANY] * count,
        limit=STAGE_BYTES,
    )


def join_kernel(*refs):
    parts, target, sems = refs[:-2], refs[-2], refs[-1]
    copies = []
    row = 0
    for k, part in enumerate(parts):
        rows = part.shape[0]
        copies.append(pltpu.make_async_copy(part, target.at[pl.ds(row, rows)], sems.at[k]))
        row += rows
    for copy in copies:
        copy.start()
    for copy in copies:
        copy.wait()


def join(parts):
    rows = sum(part.shape[0] for part in parts)
    return pl.pallas_call(
        join_kernel,
        in_specs=[ANY] * len(parts),
        out_specs=pl.BlockSpec(memory_space=pltpu.HBM),
        out_shape=shape(rows, parts[0].shape[1]),
        scratch_shapes=[pltpu.SemaphoreType.DMA((len(parts),))],
        compiler_params=pltpu.CompilerParams(vmem_limit_bytes=2**22),
        cost_estimate=pl.CostEstimate(
            flops=0, bytes_accessed=4 * rows * parts[0].shape[1], transcendentals=0
        ),
    )(*parts)


def first_kernel(step, owner_ref, c0, c1, c2, c3, c4, taps, bias_ref, act_ref, trunk, pbias):
    width = c0.shape[1]
    rows = trunk.shape[0]
    for k, cell in enumerate((c0, c1, c2, c3, c4)):

        @pl.when(owner_ref[k] >= 0)
        def _():
            cols = pl.ds(pl.multiple_of(owner_ref[k] * width, 128), width)
            trunk[:, cols] = cell[:rows]
            pbias[:, cols] = cell[rows:]

    convolve(trunk[...], taps, bias_ref[0:1], step, act_ref)


def first_conv(cells, rows, order, taps, conv_bias, step):
    _, hidden, channels = taps.shape
    return kernel_call(
        functools.partial(first_kernel, step),
        (order, *cells, taps, conv_bias),
        [
            shape(rows // 2, 2 * hidden),
            shape(rows, channels),
            shape(cells[0].shape[0] - rows, channels),
        ],
        6 * rows * hidden * channels,
        3 * hidden * channels + 2 * rows * channels,
        rows * hidden,
        scalars=1,
    )


def gather_acts(acts, edges=()):
    cells = []
    for j, act in enumerate(acts):
        parts = [unpack(act[...])]
        if edges:
            half = edges[j].shape[1] // 2
            parts = [edges[j][:, :half]] + parts + [edges[j][:, half:]]
        cells.append(jnp.concatenate(parts, axis=0))
    return jnp.concatenate(cells, axis=1)


def fused_kernel(
    block, margin, edge_ref, a0, a1, a2, a3, weight, trunk_in, pbias_ref, taps, bias_ref, act_ref,
    trunk
):
    pbias = pbias_ref[block : block + 1]
    skip = (trunk_in.shape[0] - trunk.shape[0]) // 2
    cells = gather_acts((a0, a1, a2, a3))
    project_all(cells, weight, trunk_in, skip, pbias, trunk, edge_ref, margin - skip)
    bias = bias_ref[block + 1 : block + 2]
    convolve(trunk[...], taps, bias, dilation(block + 1), act_ref)


def fused(acts, weight, trunk, pbias, taps, conv_bias, block, edge, rows_out):
    channels = trunk.shape[1]
    rows = 2 * acts[0].shape[0]
    margin = dilation(FRAMED_BLOCKS)
    hidden = taps.shape[1]
    return kernel_call(
        functools.partial(fused_kernel, block, margin),
        (edge, *acts, weight, trunk, pbias, taps, conv_bias),
        [shape(rows_out // 2, 2 * hidden), shape(rows, channels)],
        14 * rows * hidden * channels,
        7 * hidden * channels + 2 * rows * channels,
        rows * hidden,
        scalars=1,
    )


def edged_kernel(
    block, margin, edge_ref, a0, a1, a2, a3, e0, e1, e2, e3, weight, above, trunk_in, below,
    pbias_ref, taps, bias_ref, act_ref, trunk, frame
):
    rows = trunk_in.shape[0]
    frame[:margin] = above[above.shape[0] - margin :]
    frame[margin : margin + rows] = trunk_in[...]
    frame[margin + rows :] = below[:margin]
    pbias = pbias_ref[block : block + 1]
    cells = gather_acts((a0, a1, a2, a3), (e0, e1, e2, e3))
    project_all(cells, weight, frame, 0, pbias, trunk, edge_ref, margin)
    bias = bias_ref[block + 1 : block + 2]
    convolve(trunk[...], taps, bias, dilation(block + 1), act_ref)


def edged(acts, edges, weight, above, trunk, below, pbias, taps, conv_bias, block, edge):
    rows, channels = trunk.shape
    hidden = taps.shape[1]
    margin = dilation(block + 1)
    frame = rows + 2 * margin
    return kernel_call(
        functools.partial(edged_kernel, block, margin),
        (edge, *acts, *edges, weight, above, trunk, below, pbias, taps, conv_bias),
        [shape(rows // 2, 2 * hidden), shape(frame, channels)],
        14 * frame * hidden * channels,
        7 * hidden * channels + 2 * frame * channels,
        rows * hidden,
        scalars=1,
        scratch=[pltpu.VMEM((frame, channels), BF16)],
    )


def projection_kernel(block, a0, a1, a2, a3, weight, trunk_in, pbias_ref, trunk):
    margin = (trunk_in.shape[0] - trunk.shape[0]) // 2
    pbias = pbias_ref[block : block + 1]
    project_all(gather_acts((a0, a1, a2, a3)), weight, trunk_in, margin, pbias, trunk)


def projection(acts, weight, trunk, pbias, block):
    channels = trunk.shape[1]
    rows, hidden = 2 * acts[0].shape[0], acts[0].shape[1] // 2
    return kernel_call(
        functools.partial(projection_kernel, block),
        (*acts, weight, trunk, pbias),
        [shape(rows, channels)],
        8 * rows * hidden * channels,
        4 * hidden * channels + 2 * rows * channels,
    )[0]


def center_kernel(block, trunk, taps, bias_ref, act_ref):
    convolve(trunk[...], taps, bias_ref[block : block + 1], dilation(block), act_ref)


def center_conv(trunk, taps, conv_bias, block):
    rows, channels = trunk.shape
    hidden = taps.shape[1]
    return kernel_call(
        functools.partial(center_kernel, block),
        (trunk, taps, conv_bias),
        [shape((rows - 2 * dilation(block)) // 2, 2 * hidden)],
        6 * rows * hidden * channels,
        3 * hidden * channels + rows * channels,
        rows * hidden,
    )[0]


def edge_kernel(block, above, trunk, below, taps, bias_ref, act_ref):
    step = dilation(block)
    rows = trunk.shape[0]
    keep = act_ref.shape[0]
    part = keep + 2 * step
    inner_rows = part - above.shape[0]
    cells = jnp.concatenate(
        [above[...], trunk[:inner_rows], trunk[rows - inner_rows :], below[...]], axis=0
    )
    inner = dilated(cells, taps, step) + bias_ref[block : block + 1].astype(jnp.float32)
    top = inner[step : step + keep]
    bottom = inner[part + step : part + step + keep]
    act_ref[...] = jnp.concatenate([gelu(top).astype(BF16), gelu(bottom).astype(BF16)], axis=1)


def edge_conv(above, trunk, below, taps, conv_bias, block):
    channels = trunk.shape[1]
    hidden = taps.shape[1]
    step = dilation(block)
    keep = above.shape[0]
    rows = 2 * (keep + 2 * step)
    return kernel_call(
        functools.partial(edge_kernel, block),
        (above, trunk, below, taps, conv_bias),
        [shape(keep, 2 * hidden)],
        6 * rows * hidden * channels,
        3 * hidden * channels + rows * channels,
        rows * hidden,
    )[0]


def head_kernel(
    block, a0, a1, a2, a3, weight, trunk_in, pbias_ref, head_ref, hbias_ref, onehot_ref,
    cover_ref, gene_ref, trunk
):
    pbias = pbias_ref[block : block + 1]
    margin = (trunk_in.shape[0] - trunk.shape[0]) // 2
    project_all(gather_acts((a0, a1, a2, a3)), weight, trunk_in, margin, pbias, trunk)
    tracks = head_ref.shape[1]
    width = tracks
    for c in range(tracks // width):
        cols = columns(c, width)
        x = dot(trunk[...], head_ref[:, cols]) + hbias_ref[:, cols].astype(jnp.float32)
        tile = (jnp.maximum(x, 0.0) + jnp.log1p(jnp.exp(-jnp.abs(x)))).astype(BF16)
        cover_ref[:, cols] = tile
        gene_ref[:, cols] = dot(onehot_ref[...], tile).astype(BF16)


def head(acts, weight, trunk, pbias, block, head_weight, head_bias, onehot):
    channels = trunk.shape[1]
    rows, hidden = 2 * acts[0].shape[0], acts[0].shape[1] // 2
    tracks = head_weight.shape[1]
    genes = onehot.shape[0]
    return kernel_call(
        functools.partial(head_kernel, block),
        (*acts, weight, trunk, pbias, head_weight, head_bias, onehot),
        [shape(rows, tracks), shape(genes, tracks)],
        8 * rows * hidden * channels + 2 * rows * channels * tracks,
        4 * hidden * channels + rows * channels + channels * tracks,
        2 * rows * tracks,
        scratch=[pltpu.VMEM((rows, channels), BF16)],
    )


def exon_digits(exon_bins, channels):
    digits = jnp.concatenate([exon_bins >> 7, exon_bins & (DIGIT - 1)], axis=1)
    genes, width = digits.shape
    return jnp.pad(digits.astype(jnp.bfloat16), ((0, -genes % 16), (0, channels - width)))


def exon_lists(rows, genes, entries):
    digits = rows[:, :genes, : 2 * entries].astype(jnp.int32)
    lists = digits[:, :, :entries] * DIGIT + digits[:, :, entries:]
    return lists.reshape(-1, entries)


def exon_onehot(gene_block, first_bin, width_now):
    exon_matches = (
        gene_block[:, :, None] - first_bin == jnp.arange(width_now, dtype=jnp.int32)[None, None, :]
    )
    return jnp.sum(exon_matches.astype(jnp.float32), axis=1).astype(jnp.bfloat16)


def shards(
    trunk_input, conv_in, conv_bias, conv_out, projection_bias, head_weight, head_bias, exon_bins
):
    quarters = lax.axis_size("trk")
    place = lax.axis_index("trk")
    count = lax.axis_size("seq")
    lane = lax.axis_index("seq")
    bin_rows, channels_here = trunk_input.shape
    blocks, hidden, channels = conv_out.shape
    genes_here, entries = exon_bins.shape

    load_rows = BLOCKS_PER_LOAD * hidden
    size = group_size(load_rows, count)
    share = load_rows // size
    per_block = hidden // share
    groups = [[g * size + i for i in range(size)] for g in range(count // size)]
    mine = lax.rem(lane, size)
    packed = size == count and 2 * entries <= channels

    flat = conv_out.reshape(blocks * hidden, channels)

    def column(load):
        return lax.dynamic_slice_in_dim(flat, load * load_rows + mine * share, share, 0)

    def gather(parts):
        return lax.all_gather(
            join(parts), "seq", axis=0, tiled=False, axis_index_groups=groups
        )

    margin = dilation(FRAMED_BLOCKS)
    frame = bin_rows + 2 * margin
    order = lax.rem(place - jnp.arange(quarters, dtype=jnp.int32) + quarters, quarters)
    last_place = quarters - 1
    owners = jnp.stack(
        [
            place,
            place - 1,
            lax.rem(place + 2, quarters),
            jnp.where(place == last_place, -1, place + 1),
            jnp.where((place == 0) | (place == last_place), last_place - place, -1),
        ]
    ).astype(jnp.int32)
    edge = jnp.stack([lane == 0, lane == count - 1]).astype(jnp.int32)

    above, below = halo(trunk_input, margin)
    first = from_others(column(0))
    loads = [gather(after_all(first, above, below))]
    own = jnp.concatenate(
        [above, trunk_input, below, jnp.pad(projection_bias, ((0, -blocks % 16), (0, 0)))], axis=0
    )
    cells = relayed(own)
    exon_rows = [exon_digits(exon_bins, channels)] if packed else []
    exon_rows = [exon_digits(exon_bins, channels)] if packed else []
    second = from_others(after(column(1), cells[3]))
    taps_shape = shape(3, hidden, channels)
    weight_shape = shape(quarters, per_block, share, channels)
    head_row = head_bias[None, :]
    (taps,) = stage(order, (after(conv_in, own, head_row),), (taps_shape,), (functools.partial(tap_cuts, 0),))
    act, trunk, biases = first_conv(cells, frame, owners, taps, conv_bias, dilation(0))

    def staged(block, extra, extra_shape, extra_cut, token):
        place = block // BLOCKS_PER_LOAD
        part = block % BLOCKS_PER_LOAD
        cut = functools.partial(projection_cuts, part, per_block, share)
        load = after(loads[place], token)
        return stage(order, (load, extra), (weight_shape, extra_shape), (cut, extra_cut))

    for block in range(FRAMED_BLOCKS):
        later = block + 1
        others = from_others(act)
        if block == 0:
            loads.append(gather(after_all(second, act) + exon_rows))
        if block == 2:
            loads.append(gather(after_all(third, act)))
        if block == 3:
            if packed:
                gene_lists = exon_lists(loads[1][:, quarters * share :], genes_here, entries)
            else:
                gene_lists = lax.all_gather(exon_bins, "seq", axis=0, tiled=True)
            onehot = exon_onehot(gene_lists, lane * bin_rows, bin_rows)
            loads[1] = after(loads[1], onehot)
        weight, taps = staged(
            block, conv_in, taps_shape, functools.partial(tap_cuts, later), act
        )
        if block == 1:
            third = from_others(after(column(2), weight))
        if later < FRAMED_BLOCKS:
            reach = sum(dilation(b) for b in range(later + 1, FRAMED_BLOCKS))
            rows_out = bin_rows + 2 * (-(-reach // 16) * 16)
            act, trunk = fused(
                others, weight, trunk, biases, taps, conv_bias, block, edge, rows_out
            )
        else:
            trunk = projection(others, weight, trunk, biases, block)

    block = FRAMED_BLOCKS
    later = block + 1
    act = center_conv(trunk, taps, conv_bias, block)
    others = from_others(act)
    above, below = halo(after(trunk, act), dilation(block) + dilation(later))
    edges = from_others(edge_conv(above, trunk, below, taps, conv_bias, block))
    weight, taps = staged(block, conv_in, taps_shape, functools.partial(tap_cuts, later), act)
    act, trunk = edged(
        others, edges, weight, above, trunk, below, biases, taps, conv_bias, block, edge
    )

    others = from_others(act)
    weight, head_rows = staged(
        later, head_weight, shape(*head_weight.shape), functools.partial(whole_cuts, 0), act
    )
    coverage, partial = head(
        others, weight, trunk, biases, later, head_rows, head_row, onehot
    )

    parts = lax.all_to_all(
        partial.reshape(count, genes_here, partial.shape[1]), "seq", 0, 0, tiled=False
    )
    gene_sum = jnp.sum(parts.astype(jnp.float32), axis=0)
    counts = jnp.sum((exon_bins >= 0).astype(jnp.float32), axis=1)
    gene_cov = gene_sum / counts[:, None]
    return (coverage, gene_cov)


def solution(mesh):
    in_specs = (
        P("seq", "trk"),
        P(None, None, "trk", None),
        P(None, "trk"),
        P(None, "trk", None),
        P(None, "trk"),
        P(None, "trk"),
        P("trk"),
        P("seq", None),
    )
    out_specs = (P("seq", "trk"), P("seq", "trk"))
    return jax.shard_map(shards, mesh=mesh, in_specs=in_specs, out_specs=out_specs, check_vma=False)
```
